32 devices in a mesh: dp: 8 (over y, x, core), fsdp: 4 (over z).
Axes of the slice: x: 2, y: 2, z: 4, core: 2. Of those that a mesh axis runs over, the one named last changes fastest.
Arguments:
- master: float32 [3, 1777664], P(None, ('dp', 'fsdp')), as said below
- first_moment: float32 [3, 1777664], P(None, ('dp', 'fsdp')), as said below
- second_moment: float32 [3, 1777664], P(None, ('dp', 'fsdp')), as said below
- patches_small: bfloat16 [128, 196, 768], P(('dp', 'fsdp')), may hold values from -6 to 6
- patches_large: bfloat16 [64, 576, 768], P(('dp', 'fsdp')), may hold values from -6 to 6
- labels_small: int32 [128], P(('dp', 'fsdp')), may hold values from 0 to 999
- labels_large: int32 [64], P(('dp', 'fsdp')), may hold values from 0 to 999
- counts: int32 [32, 2], P(('dp', 'fsdp')), may hold values from 0 to 4, as said below
- step: int32 [1], replicated, may hold values from 1 to 20
Outputs:
- loss: float32 [], replicated
- gradients: float32 [3, 1777664], P(None, ('dp', 'fsdp'))
- new_first: float32 [3, 1777664], P(None, ('dp', 'fsdp'))
- new_second: float32 [3, 1777664], P(None, ('dp', 'fsdp'))
- new_master: float32 [3, 1777664], P(None, ('dp', 'fsdp'))
- weight_norms: float32 [3, 16], replicated
- update_norms: float32 [3, 16], replicated
- trust_ratios: float32 [3, 16], replicated
The draws below stay inside these ranges and needn't reach their ends.
Inputs may be any that keep to these rules, and one draw needn't show every extreme that they name: `master`: each row holds its segments in the order of the steps, zeros after the last one. `first_moment`: zeros after the last segment of each row. `second_moment`: positive on every segment entry, zeros after the last segment of each row. `counts`: column 0 lies in 1 to 4, column 1 in 0 to 2; the first device has all its slots live.
All inputs are finite; a program needn't handle non-finite values.
Results may differ from the reference program's by a relative error of at most 0.0095.
The reference program's roundings to bfloat16 on the way (of `weights`) count: a program that leaves them out, or rounds other values in their place, can miss the bound.
Values may be sent and summed in bfloat16 or wider, within the bound.
No kernel may reach another device: no remote copies, remote signals or barrier semaphores. Data moves between devices by JAX's collectives and lax.ppermute only.
A program may use at most 256 MiB of HBM per device.

```python
import math
import jax
import jax.numpy as jnp
import numpy as np
from jax import lax

D = 384
HEADS = 8
FF = 1536
CLASSES = 1000
PATCH_IN = 768
GRID_SMALL = 14
GRID_LARGE = 24
SEGMENTS = 16
SMALL_DEV = 4
LARGE_DEV = 2
LS = 196
LL = 576
IMG_SMALL = 128
IMG_LARGE = 64
FLAT = 1777664
N_DP = 8
N_FSDP = 4


def segment_laws():
    dim = D

    def matrix(rows, cols, factor):
        return ((rows, cols), factor / math.sqrt(rows), 0.0, 0.0, 0.0)

    def bias(size, scale):
        return ((size,), scale, 0.0, 0.0, 0.0)
    gain = ((dim,), 0.1, 0.0, 1.0, 0.0)
    layer = ((dim,), 0.0, 0.5, 0.5, 0.0)
    tail = [gain, bias(dim, 0.2), matrix(dim, FF, 1.0), bias(FF, 0.2), matrix(FF, dim, 1.0), bias(dim, 0.2), layer]
    stem = [matrix(PATCH_IN, dim, 1.0), bias(dim, 0.2), bias(GRID_SMALL * GRID_SMALL * dim, 0.5), bias(dim, 1.0), gain, bias(dim, 0.2), matrix(dim, CLASSES, 2.0), bias(CLASSES, 0.3)]
    mix_first = ((HEADS, HEADS), 0.5 / math.sqrt(HEADS), 0.0, 0.0, 1.5)
    mix_second = ((HEADS, HEADS), 0.3, 0.0, 0.0, 1.0)
    selfb = [gain, bias(dim, 0.2), matrix(dim, 3 * dim, 1.0), bias(2 * dim, 0.2), mix_first, mix_second, matrix(dim, dim, 4.0), bias(dim, 0.2), layer] + tail
    classb = [gain, bias(dim, 0.2), matrix(dim, dim, 1.5), bias(dim, 0.2), matrix(dim, 2 * dim, 1.0), bias(dim, 0.2), matrix(dim, dim, 4.0), bias(dim, 0.2), layer] + tail
    return [stem, selfb, classb]


def entry_tables():
    normal_table = np.zeros((3, FLAT), np.float32)
    uniform_table = np.zeros((3, FLAT), np.float32)
    const_table = np.zeros((3, FLAT), np.float32)
    grad_table = np.zeros((3, FLAT), np.float32)
    images = (SMALL_DEV + LARGE_DEV) * N_DP * N_FSDP
    for group, laws in enumerate(segment_laws()):
        offset = 0
        for shape, normal, uniform, const, diagonal in laws:
            count = int(np.prod(shape))
            normal_table[group, offset:offset + count] = normal
            uniform_table[group, offset:offset + count] = uniform
            const_table[group, offset:offset + count] = const
            if diagonal > 0:
                const_table[group, offset + np.arange(shape[0]) * (shape[1] + 1)] = diagonal
            if len(shape) == 2 and diagonal == 0:
                grad_table[group, offset:offset + count] = 1.0 / math.sqrt(images * shape[0])
            else:
                grad_table[group, offset:offset + count] = 0.3 / math.sqrt(images)
            offset += count
    return (normal_table, uniform_table, const_table, grad_table)


def draw_master(key, part):
    normal_table, uniform_table, const_table, grad_table = entry_tables()
    noise = jax.random.normal(jax.random.fold_in(key, 11), (3, FLAT), jnp.float32)
    spread = jax.random.uniform(jax.random.fold_in(key, 12), (3, FLAT), jnp.float32)
    return noise * normal_table + spread * uniform_table + const_table


def draw_first_moment(key, part):
    normal_table, uniform_table, const_table, grad_table = entry_tables()
    noise = jax.random.normal(jax.random.fold_in(key, 21), (3, FLAT), jnp.float32)
    return 0.1 / 0.9 * grad_table * noise


def draw_second_moment(key, part):
    normal_table, uniform_table, const_table, grad_table = entry_tables()
    spread = jax.random.uniform(jax.random.fold_in(key, 31), (3, FLAT), jnp.float32)
    return 0.001 / 0.999 * grad_table * grad_table * jnp.exp(spread * math.log(4.0))


def draw_counts(key, part):
    devices = N_DP * N_FSDP
    small = jax.random.randint(jax.random.fold_in(key, 41), (devices,), 1, SMALL_DEV + 1)
    large = jax.random.randint(jax.random.fold_in(key, 42), (devices,), 0, LARGE_DEV + 1)
    leading = jnp.arange(devices) == 0
    return jnp.stack([jnp.where(leading, SMALL_DEV, small), jnp.where(leading, LARGE_DEV, large)], 1).astype(jnp.int32)


def set_ends(values, key, low, high):
    spot = [jax.random.randint(jax.random.fold_in(key, axis), (), 0, length) for axis, length in enumerate(values.shape)]
    widest = values.shape.index(max(values.shape))
    beside = spot[:widest] + [(spot[widest] + 1) % values.shape[widest]] + spot[widest + 1:]
    return values.at[tuple(spot)].set(low).at[tuple(beside)].set(high)


def level_of(stream_key, extent, split, least, largest):
    factor_of = 1.0
    for dim, shards_of in split:
        steps = jax.random.uniform(jax.random.fold_in(jax.random.fold_in(stream_key, 6), dim), (shards_of,), jnp.float32, least / len(split), largest / len(split))
        factor_of = factor_of * jnp.repeat(jnp.exp(steps), extent[dim] // shards_of).reshape((-1,) + (1,) * (len(extent) - 1 - dim))
    return factor_of


def normal_values(key, dims, scale, bound, shards=(), kind=jnp.bfloat16):
    entries = jax.random.normal(key, dims, jnp.float32) * scale
    if len(shards) > 0:
        entries = level_of(key, dims, shards, -0.22, 0.18) * entries
    return jnp.clip(entries, min=-bound, max=bound).astype(kind)


def setup_inputs(seed: int = 0) -> dict:
    key_list = jax.random.split(jax.random.key(seed), 10)
    return {
        "master": draw_master(jax.random.fold_in(key_list[9], 71), 0),
        "first_moment": draw_first_moment(jax.random.fold_in(key_list[9], 71), 0),
        "second_moment": draw_second_moment(jax.random.fold_in(key_list[9], 71), 0),
        "patches_small": normal_values(key_list[3], (IMG_SMALL, LS, PATCH_IN), 1.0, 6.0, ((0, 32),)),
        "patches_large": normal_values(key_list[4], (IMG_LARGE, LL, PATCH_IN), 1.0, 6.0, ((0, 32),)),
        "labels_small": set_ends(jax.random.randint(key_list[5], (IMG_SMALL,), 0, CLASSES), jax.random.fold_in(key_list[5], 1), 0, CLASSES - 1).astype(jnp.int32),
        "labels_large": set_ends(jax.random.randint(key_list[6], (IMG_LARGE,), 0, CLASSES), jax.random.fold_in(key_list[6], 1), 0, CLASSES - 1).astype(jnp.int32),
        "counts": draw_counts(jax.random.fold_in(key_list[9], 71), 0),
        "step": jax.random.randint(key_list[8], (1,), 1, 21).astype(jnp.int32),
    }


@jax.custom_vjp
def low(v):
    return lax.optimization_barrier(v.astype(jnp.bfloat16)).astype(jnp.float32)

@jax.custom_vjp
def low_back(v):
    return v

def low_keep(v):
    return (low(v), None)

def low_pass(kept, grad):
    return (grad,)

def back_keep(v):
    return (v, None)

def back_low(kept, grad):
    return (low(grad),)
low.defvjp(low_keep, low_pass)
low_back.defvjp(back_keep, back_low)
highest = lax.Precision.HIGHEST
smooth = 0.1
beta_one = 0.9
beta_two = 0.999
adam_eps = 1e-06
decay_rate = 0.01
learn_rate = 0.3
norm_eps = 1e-06

def shapes_of():
    dim = D
    tail = [(dim,), (dim,), (dim, FF), (FF,), (FF, dim), (dim,), (dim,)]
    stem = [(PATCH_IN, dim), (dim,), (GRID_SMALL * GRID_SMALL, dim), (dim,), (dim,), (dim,), (dim, CLASSES), (CLASSES,)]
    selfb = [(dim,), (dim,), (dim, 3 * dim), (2 * dim,), (HEADS, HEADS), (HEADS, HEADS), (dim, dim), (dim,), (dim,)] + tail
    classb = [(dim,), (dim,), (dim, dim), (dim,), (dim, 2 * dim), (dim,), (dim, dim), (dim,), (dim,)] + tail
    return [stem, selfb, classb]

def unpack(packed, shapes):
    pieces = []
    start = 0
    for shape in shapes:
        count = int(np.prod(shape))
        pieces.append(packed[start:start + count].reshape(shape))
        start += count
    return pieces

def resize_matrix(small, large):
    rows = jnp.arange(large).astype(jnp.float32) * ((small - 1) / (large - 1))
    cols = jnp.arange(small).astype(jnp.float32)
    line = jnp.maximum(0.0, 1.0 - jnp.abs(rows[:, None] - cols[None, :]))
    return (line[:, None, :, None] * line[None, :, None, :]).reshape(large * large, small * small)

def normed(value, gain, shift):
    centred = value - lax.optimization_barrier(jnp.mean(value, -1, keepdims=True))
    spread = lax.optimization_barrier(jnp.mean(centred * centred, -1, keepdims=True))
    return centred * lax.rsqrt(spread + 1e-06) * gain + shift

def dense(left, right):
    return jnp.einsum('...i,ij->...j', left, right, precision=highest)

def feed_forward(mid, weights):
    norm_gain, norm_shift, w_upper, b_upper, w_lower, b_lower, scale_two = weights
    normed_mid = low(normed(mid, norm_gain, norm_shift))
    upper = low_back(dense(normed_mid, w_upper) + b_upper)
    active = low(jax.nn.gelu(upper, approximate=False))
    lower = low_back(dense(active, w_lower) + b_lower)
    return mid + scale_two * lower

def self_block(tokens, weights):
    gain, shift, w_qkv, b_qv, mix_pre, mix_post, w_out, b_out, scale_one = weights[:9]
    length, dim = tokens.shape
    width = dim // HEADS
    normed_in = low(normed(tokens, gain, shift))
    bias = jnp.concatenate([b_qv[:dim], jnp.zeros((dim,), tokens.dtype), b_qv[dim:]])
    projected = low(low_back(dense(normed_in, w_qkv) + bias)).reshape(length, 3, HEADS, width)
    query, keys, values = (projected[:, 0], projected[:, 1], projected[:, 2])
    scores = low_back(jnp.einsum('qhc,khc->hqk', query, keys, precision=highest) * width ** (-0.5))
    mixed = jnp.einsum('gh,hqk->gqk', mix_pre, scores, precision=highest)
    probs = jax.nn.softmax(mixed, -1)
    weighted = low(jnp.einsum('gh,hqk->gqk', mix_post, probs, precision=highest))
    attended = jnp.einsum('hqk,khc->qhc', weighted, values, precision=highest).reshape(length, dim)
    attended = low(low_back(attended))
    branch = low_back(dense(attended, w_out) + b_out)
    return feed_forward(tokens + scale_one * branch, weights[9:])

def class_block(cls_tok, tokens, weights):
    gain, shift, w_query, b_query, w_kv, b_value, w_out, b_out, scale_one = weights[:9]
    length, dim = tokens.shape
    width = dim // HEADS
    joined = jnp.concatenate([cls_tok[None], tokens], 0)
    normed_all = low(normed(joined, gain, shift))
    query = low(low_back(dense(normed_all[0], w_query) + b_query)).reshape(HEADS, width)
    bias = jnp.concatenate([jnp.zeros((dim,), tokens.dtype), b_value])
    keyval = low(low_back(dense(normed_all, w_kv) + bias)).reshape(length + 1, 2, HEADS, width)
    scores = low_back(jnp.einsum('hc,khc->hk', query, keyval[:, 0], precision=highest) * width ** (-0.5))
    probs = low(jax.nn.softmax(scores, -1))
    attended = low(low_back(jnp.einsum('hk,khc->hc', probs, keyval[:, 1], precision=highest).reshape(dim)))
    branch = low_back(dense(attended, w_out) + b_out)
    return feed_forward(cls_tok + scale_one * branch, weights[9:])

def image_loss(patches, label, pos, stem, selfw, classw):
    tokens = low_back(dense(patches, stem[0])) + stem[1] + pos
    tokens = self_block(tokens, selfw)
    cls_out = class_block(stem[3], tokens, classw)
    final = low(normed(cls_out, stem[4], stem[5]))
    logits = low_back(dense(final, stem[6]) + stem[7])
    logp = jax.nn.log_softmax(logits)
    picked = jnp.sum(jnp.where(jnp.arange(logits.shape[0]) == label, logp, 0.0))
    return -((1.0 - smooth) * picked + smooth * jnp.mean(logp))

def model_loss(params, groups, patches_small, patches_large, labels_small, labels_large, live_small, live_large, total):
    stem, selfw, classw = [unpack(params[index], groups[index]) for index in range(3)]
    pos_small = stem[2]
    pos_large = jnp.dot(resize_matrix(GRID_SMALL, GRID_LARGE).astype(params.dtype), pos_small, precision=highest)

    def summed(patches, labels, live, pos):

        def run(item):
            return item[2] * image_loss(item[0], item[1], pos, stem, selfw, classw)
        return jnp.sum(lax.map(jax.checkpoint(run), (patches, labels, live)))
    small = summed(patches_small, labels_small, live_small, pos_small)
    large = summed(patches_large, labels_large, live_large, pos_large)
    return (small + large) / total

def reference(master, first_moment, second_moment, patches_small, patches_large, labels_small, labels_large, counts, step):
    groups = shapes_of()
    weights = lax.optimization_barrier(master.astype(jnp.bfloat16)).astype(jnp.float32)
    live_small = (jnp.arange(IMG_SMALL) % SMALL_DEV < jnp.repeat(counts[:, 0], SMALL_DEV)).astype(master.dtype)
    live_large = (jnp.arange(IMG_LARGE) % LARGE_DEV < jnp.repeat(counts[:, 1], LARGE_DEV)).astype(master.dtype)
    total = jnp.sum(counts).astype(master.dtype)
    small_in = patches_small.astype(jnp.float32)
    large_in = patches_large.astype(jnp.float32)
    loss, pullback = jax.vjp(lambda params: model_loss(params, groups, small_in, large_in, labels_small, labels_large, live_small, live_large, total), weights)
    gradients = pullback(jnp.ones_like(loss))[0]
    new_first = beta_one * first_moment + (1.0 - beta_one) * gradients
    new_second = beta_two * second_moment + (1.0 - beta_two) * gradients * gradients
    count_f = step[0].astype(jnp.float32)
    update = new_first / (1.0 - beta_one ** count_f) / (jnp.sqrt(new_second / (1.0 - beta_two ** count_f)) + adam_eps) + decay_rate * master
    weight_rows, update_rows, trust_rows, new_rows = ([], [], [], [])
    for group in range(3):
        offset = 0
        weight_list, update_list, trust_list, moved = ([], [], [], [])
        for shape in groups[group]:
            count = int(np.prod(shape))
            weight_seg = master[group, offset:offset + count]
            update_seg = update[group, offset:offset + count]
            weight_norm = jnp.sqrt(jnp.sum(weight_seg * weight_seg))
            update_norm = jnp.sqrt(jnp.sum(update_seg * update_seg))
            ratio = weight_norm / (update_norm + norm_eps)
            weight_list.append(weight_norm)
            update_list.append(update_norm)
            trust_list.append(ratio)
            moved.append(weight_seg - learn_rate * ratio * update_seg)
            offset += count
        moved.append(master[group, offset:])
        while len(weight_list) < SEGMENTS:
            weight_list.append(jnp.zeros((), master.dtype))
            update_list.append(jnp.zeros((), master.dtype))
            trust_list.append(jnp.ones((), master.dtype))
        weight_rows.append(jnp.stack(weight_list))
        update_rows.append(jnp.stack(update_list))
        trust_rows.append(jnp.stack(trust_list))
        new_rows.append(jnp.concatenate(moved))
    return (loss, gradients, new_first, new_second, jnp.stack(new_rows), jnp.stack(weight_rows), jnp.stack(update_rows), jnp.stack(trust_rows))
```

```python
import functools

import jax
import jax.numpy as jnp
import numpy as np
from jax import lax
from jax.experimental import pallas as pl
from jax.experimental.pallas import tpu as pltpu
from jax.sharding import PartitionSpec as P

D = 384
HEADS = 8
WIDTH = D // HEADS
FF = 1536
CLASSES = 1000
CLASS_PAD = 1024
PATCH_IN = 768
GRID_SMALL = 14
GRID_LARGE = 24
LANES = 128
SEGMENTS = 16

LOG2E = 1.4426950408889634
SCALE = WIDTH**-0.5
NEG = -1e30
smooth = 0.1
beta_one = 0.9
beta_two = 0.999
adam_eps = 1e-06
decay_rate = 0.01
learn_rate = 0.3
norm_eps = 1e-06

f32 = jnp.float32
bf16 = jnp.bfloat16
AXES = ("dp", "fsdp")
VMEM_BYTES = 60 << 20


def shapes_of():
    dim = D
    tail = [(dim,), (dim,), (dim, FF), (FF,), (FF, dim), (dim,), (dim,)]
    stem = [
        (PATCH_IN, dim),
        (dim,),
        (GRID_SMALL * GRID_SMALL, dim),
        (dim,),
        (dim,),
        (dim,),
        (dim, CLASSES),
        (CLASSES,),
    ]
    selfb = [
        (dim,),
        (dim,),
        (dim, 3 * dim),
        (2 * dim,),
        (HEADS, HEADS),
        (HEADS, HEADS),
        (dim, dim),
        (dim,),
        (dim,),
    ] + tail
    classb = [
        (dim,),
        (dim,),
        (dim, dim),
        (dim,),
        (dim, 2 * dim),
        (dim,),
        (dim, dim),
        (dim,),
        (dim,),
    ] + tail
    return [stem, selfb, classb]


def segment_bounds():
    starts = np.zeros((3, SEGMENTS), np.int32)
    ends = np.zeros((3, SEGMENTS), np.int32)
    real = np.zeros((3, SEGMENTS), np.float32)
    for group, shapes in enumerate(shapes_of()):
        offset = 0
        for number, shape in enumerate(shapes):
            count = int(np.prod(shape))
            starts[group, number] = offset
            ends[group, number] = offset + count
            real[group, number] = 1.0
            offset += count
    return starts, ends, real


STARTS, ENDS, REAL = segment_bounds()


def row_of(group, number):
    return int(STARTS[group, number]) // LANES


def rows_used(group):
    return -(-int(ENDS[group].max()) // LANES)


def resize_table():
    rows = np.arange(GRID_LARGE).astype(np.float32) * np.float32((GRID_SMALL - 1) / (GRID_LARGE - 1))
    cols = np.arange(GRID_SMALL).astype(np.float32)
    line = np.maximum(np.float32(0.0), np.float32(1.0) - np.abs(rows[:, None] - cols[None, :]))
    return (line[:, None, :, None] * line[None, :, None, :]).reshape(GRID_LARGE**2, GRID_SMALL**2)


def nn(a, b):
    return lax.dot_general(a, b, (((1,), (0,)), ((), ())), preferred_element_type=f32)


def nt(a, b):
    return lax.dot_general(a, b, (((1,), (1,)), ((), ())), preferred_element_type=f32)


def tn(a, b):
    return lax.dot_general(a, b, (((0,), (0,)), ((), ())), preferred_element_type=f32)


def colsum(value):
    return jnp.sum(value, 0, keepdims=True)


def split(value):
    high = value.astype(bf16)
    return high, (value - high.astype(f32)).astype(bf16)


def stats(value):
    centred = value - jnp.mean(value, -1, keepdims=True)
    inverse = lax.rsqrt(jnp.mean(centred * centred, -1, keepdims=True) + 1e-06)
    return centred * inverse, inverse


def norm_back(d_out, unit, inverse, gain):
    inner = d_out * gain
    first = jnp.mean(inner, -1, keepdims=True)
    second = jnp.mean(inner * unit, -1, keepdims=True)
    return inverse * (inner - first - unit * second)


def gelu_pair(upper):
    cdf = 0.5 * (1.0 + lax.erf(upper * (0.5**0.5)))
    density = jnp.exp(-0.5 * upper * upper) * 0.3989422804014327
    return upper * cdf, cdf + upper * density


def head_mask(rows):
    lane = lax.broadcasted_iota(jnp.int32, (rows, D), 1)
    row = lax.broadcasted_iota(jnp.int32, (rows, D), 0)
    return (lane // WIDTH) == lax.rem(row, HEADS)


VM = pl.BlockSpec(memory_space=pltpu.VMEM)
SM = pl.BlockSpec(memory_space=pltpu.SMEM)


def params(**kw):
    return pltpu.CompilerParams(vmem_limit_bytes=VMEM_BYTES, **kw)


def sds(shape, dtype):
    return jax.ShapeDtypeStruct(shape, dtype)


def log2(n):
    return n.bit_length() - 1


def exchange(value, bit, z_bits):
    if bit < z_bits:
        n = lax.axis_size("fsdp")
        return lax.ppermute(value, "fsdp", [(i, i ^ (1 << bit)) for i in range(n)])
    n = lax.axis_size("dp")
    return lax.ppermute(value, "dp", [(i, i ^ (1 << (bit - z_bits))) for i in range(n)])


def gather_pieces(state, order, z_bits):
    merged = False
    for bit in order:
        if bit >= z_bits and not merged:
            state = merge(state)
            merged = True
        state = state + [(exchange(a, bit, z_bits), [r | (1 << bit) for r in rel]) for a, rel in state]
        if bit < z_bits:
            state = merge(state)
            merged = True
    return state


def merge(state):
    if len(state) == 1:
        return state
    return [(jnp.concatenate([a for a, _ in state], 0), [r for _, rel in state for r in rel])]


def put_matrix(flat, row, out_ref, rows, cols):
    step = cols // LANES
    for j in range(step):
        out_ref[:, LANES * j : LANES * (j + 1)] = flat[pl.ds(row + j, rows, stride=step), :].astype(bf16)


def put_row(flat, row, out_ref, at, cols):
    for j in range(cols // LANES):
        out_ref[at : at + 1, LANES * j : LANES * (j + 1)] = flat[row + j : row + j + 1, :]


def fill_flat(me, piece_refs, rels, rows, flat):
    for ref, rel in zip(piece_refs, rels):
        for k, r in enumerate(rel):
            flat[pl.ds(rows * jnp.bitwise_xor(me, r), rows), :] = ref[k, 0:rows, :].astype(f32)


def unpack_stem_kernel(rels, rows, me_ref, resize_ref, *refs):
    n = len(rels)
    pieces, (patch_w, vec, pos_small, pos_large, head_w, head_b), (flat, tiles) = refs[:n], refs[n : n + 6], refs[n + 6 :]
    fill_flat(me_ref[0], pieces, rels, rows, flat)
    put_matrix(flat, row_of(0, 0), patch_w, PATCH_IN, D)
    vec[...] = jnp.zeros_like(vec)
    for at, number in enumerate((1, 3, 4, 5)):
        put_row(flat, row_of(0, number), vec, at, D)
    bias = vec[0:1, :]
    small = GRID_SMALL**2
    pos_small[...] = jnp.zeros_like(pos_small)
    for j in range(D // LANES):
        pos_small[0:small, LANES * j : LANES * (j + 1)] = flat[pl.ds(row_of(0, 2) + j, small, stride=D // LANES), :]
    pos_large[...] = (
        lax.dot_general(
            resize_ref[...], pos_small[...], (((1,), (0,)), ((), ())),
            preferred_element_type=f32, precision=lax.Precision.HIGHEST,
        )
        + bias
    )
    pos_small[...] += bias
    lane = lax.broadcasted_iota(jnp.int32, (24, LANES), 1)
    base = row_of(0, 6)
    for rho in range(16):
        first, shift = (CLASSES * rho) // LANES, (CLASSES * rho) % LANES
        parts = [flat[pl.ds(base + first + t, 24, stride=125), :] for t in range(9)]
        if shift:
            parts = [pltpu.roll(p, LANES - shift, 1) for p in parts]
        for t in range(8):
            value = jnp.where(lane < LANES - shift, parts[t], parts[t + 1]) if shift else parts[t]
            if t == 7:
                value = jnp.where(lane < CLASSES - 7 * LANES, value, 0.0)
            tiles[t, pl.ds(rho, 24, stride=16), :] = value
    for t in range(8):
        head_w[:, LANES * t : LANES * (t + 1)] = tiles[t].astype(bf16)
    put_row(flat, row_of(0, 7), head_b, 0, CLASS_PAD)


def unpack_stem(me, pieces, rels, rows, count, padded):
    resize = np.zeros((GRID_LARGE**2, padded), np.float32)
    resize[:, : GRID_SMALL**2] = resize_table()
    return pl.pallas_call(
        functools.partial(unpack_stem_kernel, rels, rows),
        out_shape=[
            sds((PATCH_IN, D), bf16),
            sds((8, D), f32),
            sds((padded, D), f32),
            sds((GRID_LARGE**2, D), f32),
            sds((D, CLASS_PAD), bf16),
            sds((1, CLASS_PAD), f32),
        ],
        in_specs=[SM] + [VM] * (1 + len(pieces)),
        out_specs=[VM] * 6,
        scratch_shapes=[pltpu.VMEM((count * rows, LANES), f32), pltpu.VMEM((8, D, LANES), f32)],
        compiler_params=params(),
        name="unpack_stem",
    )(me, jnp.asarray(resize), *pieces)


SG1, SB1, SBQ, SBV, SBO, SLS1, SG2, SB2, SC2, SLS2 = range(10)
CG1, CB1, CBQ, CBV, CBO, CLS1, CG2, CB2, CC2, CLS2 = range(10)


def unpack_self_kernel(rels, rows, me_ref, *refs):
    n = len(rels)
    pieces = refs[:n]
    wqkv, wo, w1, w2, vec, c1, pre_col, post_col, pre_row, post_row, flat = refs[n:]
    fill_flat(me_ref[0], pieces, rels, rows, flat)
    put_matrix(flat, row_of(1, 2), wqkv, D, 3 * D)
    put_matrix(flat, row_of(1, 6), wo, D, D)
    put_matrix(flat, row_of(1, 11), w1, D, FF)
    put_matrix(flat, row_of(1, 13), w2, FF, D)
    vec[...] = jnp.zeros_like(vec)
    bq = row_of(1, 3)
    for at, row in (
        (SG1, row_of(1, 0)), (SB1, row_of(1, 1)), (SBQ, bq), (SBV, bq + D // LANES), (SBO, row_of(1, 7)),
        (SLS1, row_of(1, 8)), (SG2, row_of(1, 9)), (SB2, row_of(1, 10)), (SC2, row_of(1, 14)), (SLS2, row_of(1, 15)),
    ):
        put_row(flat, row, vec, at, D)
    put_row(flat, row_of(1, 12), c1, 0, FF)
    mix = jnp.broadcast_to(flat[row_of(1, 4) : row_of(1, 4) + 1, :], (HEADS, LANES))
    lane = lax.broadcasted_iota(jnp.int32, (HEADS, LANES), 1)
    row = lax.broadcasted_iota(jnp.int32, (HEADS, LANES), 0)
    pick_pre = jnp.where((lane < 64) & (lane // HEADS == row), mix, 0.0)
    pick_post = jnp.where((lane >= 64) & (lane % HEADS == row), mix, 0.0)
    table_lane = lax.broadcasted_iota(jnp.int32, (LANES, D), 0)
    table_col = lax.broadcasted_iota(jnp.int32, (LANES, D), 1) // WIDTH
    spread_pre = jnp.where(table_lane % HEADS == table_col, 1.0, 0.0).astype(bf16)
    spread_post = jnp.where((table_lane - 64) // HEADS == table_col, 1.0, 0.0).astype(bf16)
    factor = SCALE * LOG2E
    pre_row[...] = nn(pick_pre.astype(bf16), spread_pre) * factor
    post_row[...] = nn(pick_post.astype(bf16), spread_post)
    pre_all = lax.dot_general(
        spread_pre, pick_pre.astype(bf16), (((0,), (1,)), ((), ())), preferred_element_type=f32
    )
    post_all = lax.dot_general(
        spread_post, pick_post.astype(bf16), (((0,), (1,)), ((), ())), preferred_element_type=f32
    )
    pre_col[...] = pre_all * factor
    post_col[...] = post_all


def unpack_self(me, pieces, rels, rows, count):
    return pl.pallas_call(
        functools.partial(unpack_self_kernel, rels, rows),
        out_shape=[
            sds((D, 3 * D), bf16),
            sds((D, D), bf16),
            sds((D, FF), bf16),
            sds((FF, D), bf16),
            sds((16, D), f32),
            sds((1, FF), f32),
            sds((D, HEADS), f32),
            sds((D, HEADS), f32),
            sds((HEADS, D), f32),
            sds((HEADS, D), f32),
        ],
        in_specs=[SM] + [VM] * len(pieces),
        out_specs=[VM] * 10,
        scratch_shapes=[pltpu.VMEM((count * rows, LANES), f32)],
        compiler_params=params(),
        name="unpack_self",
    )(me, *pieces)


def unpack_class_kernel(rels, rows, me_ref, *refs):
    n = len(rels)
    pieces = refs[:n]
    wq, wkv, wo, w1, w2, vec, c1, total, flat = refs[n:]
    fill_flat(me_ref[0], pieces, rels, rows, flat)
    put_matrix(flat, row_of(2, 2), wq, D, D)
    put_matrix(flat, row_of(2, 4), wkv, D, 2 * D)
    put_matrix(flat, row_of(2, 6), wo, D, D)
    put_matrix(flat, row_of(2, 11), w1, D, FF)
    put_matrix(flat, row_of(2, 13), w2, FF, D)
    vec[...] = jnp.zeros_like(vec)
    for at, number in (
        (CG1, 0), (CB1, 1), (CBQ, 3), (CBV, 5), (CBO, 7), (CLS1, 8), (CG2, 9), (CB2, 10), (CC2, 14), (CLS2, 15),
    ):
        put_row(flat, row_of(2, number), vec, at, D)
    put_row(flat, row_of(2, 12), c1, 0, FF)
    count = jnp.zeros((1, LANES), f32)
    for ref, rel in zip(pieces, rels):
        for k in range(len(rel)):
            count = count + ref[k].astype(f32)[rows : rows + 1, :]
    total[...] = count


def unpack_class(me, pieces, rels, rows, count):
    return pl.pallas_call(
        functools.partial(unpack_class_kernel, rels, rows),
        out_shape=[
            sds((D, D), bf16),
            sds((D, 2 * D), bf16),
            sds((D, D), bf16),
            sds((D, FF), bf16),
            sds((FF, D), bf16),
            sds((16, D), f32),
            sds((1, FF), f32),
            sds((1, LANES), f32),
        ],
        in_specs=[SM] + [VM] * len(pieces),
        out_specs=[VM] * 8,
        scratch_shapes=[pltpu.VMEM((count * rows, LANES), f32)],
        compiler_params=params(),
        name="unpack_class",
    )(me, *pieces)


CHUNK = 384


def attend(qkv, lse_at, att_put, valid, pre_col, post_col, scr):
    length = qkv.shape[0]
    q_t, kk, v_t, acc = scr
    q_t[...] = qkv[:, 0:D].astype(f32).T
    kk[:, 0:D] = qkv[:, D : 2 * D]
    kk[:, D:] = qkv[:, D : 2 * D]
    v_t[...] = qkv[:, 2 * D :].astype(f32).T.astype(bf16)
    acc[...] = jnp.zeros_like(acc)
    for g in range(HEADS):
        high, low = split(q_t[...] * pre_col[:, g : g + 1])
        mixed = nn(kk[...], jnp.concatenate([high, low], 0))
        if valid < length:
            mixed = jnp.where(lax.broadcasted_iota(jnp.int32, mixed.shape, 0) < valid, mixed, NEG)
        top = jnp.max(mixed, 0, keepdims=True)
        raw = jnp.exp2(mixed - top)
        weight = colsum(raw)
        lse_at[g : g + 1, :] = top + jnp.log2(weight)
        acc[...] += nn(v_t[...], raw.astype(bf16)) * post_col[:, g : g + 1] * (1.0 / weight)
    att_put(acc[...].T.astype(bf16))


def self_forward_body(tok, lengths, valid, wr, outs, scr):
    wqkv, wo, w1, w2, vec, c1, pre_col, post_col = wr
    qkv_o, lse_o, att_o, branch_o, mid_o, act_o, slope_o, lower_o, out_o = outs
    n, length = qkv_o.shape[0], qkv_o.shape[1]
    rows = n * length
    row = lambda at: vec[at : at + 1, :]
    unit, _ = stats(tok)
    a1 = (unit * row(SG1) + row(SB1)).astype(bf16)
    for part, at in ((0, SBQ), (1, None), (2, SBV)):
        value = nn(a1, wqkv[:, D * part : D * (part + 1)])
        if at is not None:
            value = value + row(at)
        qkv_o[:, :, D * part : D * (part + 1)] = value.astype(bf16).reshape(n, length, D)
    for i in range(n):

        def put(value, i=i):
            att_o[i] = value

        attend(qkv_o.at[i], lse_o.at[i], put, valid, pre_col, post_col, scr)
    att = att_o[...].reshape(rows, D)
    branch = nn(att, wo[...]) + row(SBO)
    branch_o[...] = branch.astype(bf16).reshape(n, length, D)
    mid = tok + row(SLS1) * branch
    mid_o[...] = mid.reshape(n, length, D)
    unit, _ = stats(mid)
    n2 = (unit * row(SG2) + row(SB2)).astype(bf16)
    lower = jnp.broadcast_to(row(SC2), (rows, D))
    for c in range(0, FF, CHUNK):
        upper = nn(n2, w1[:, c : c + CHUNK]) + c1[:, c : c + CHUNK]
        act, slope = gelu_pair(upper)
        act = act.astype(bf16)
        act_o[:, :, c : c + CHUNK] = act.reshape(n, length, CHUNK)
        slope_o[:, :, c : c + CHUNK] = slope.astype(bf16).reshape(n, length, CHUNK)
        lower = lower + nn(act, w2[c : c + CHUNK, :])
    lower_o[...] = lower.astype(bf16).reshape(n, length, D)
    out_o[...] = (mid + row(SLS2) * lower).reshape(n, length, D)


def self_forward_kernel(steps_small, valid, *refs):
    (ps, plg, patch_w, pos_small, pos_large), refs = refs[:5], refs[5:]
    wr, refs = refs[:8], refs[8:]
    out_small, out_large, scr = refs[:10], refs[10:20], refs[20:]
    tok_small, scr_small, scr_large = scr[0], scr[1:5], scr[5:9]
    step = pl.program_id(0)

    @pl.when(step < steps_small)
    def _():
        n, length = out_small[0].shape[0], out_small[0].shape[1]
        for i in range(n):
            tok_small[length * i : length * (i + 1), :] = pos_small[...]
            tok_small[length * i : length * i + valid, :] += nn(ps[i], patch_w[...])
        tok = tok_small[...]
        out_small[0][...] = tok.reshape(n, length, D)
        self_forward_body(tok, None, valid, wr, out_small[1:], scr_small)

    @pl.when(step >= steps_small)
    def _():
        n, length = out_large[0].shape[0], out_large[0].shape[1]
        tok = nn(plg[0], patch_w[...]) + pos_large[...]
        out_large[0][...] = tok.reshape(n, length, D)
        self_forward_body(tok, None, length, wr, out_large[1:], scr_large)


def const_spec(a):
    return pl.BlockSpec(a.shape, lambda i, nd=a.ndim: (0,) * nd, pipeline_mode=pl.Buffered(1))


def pair_of(n):
    return 2 if n % 2 == 0 else 1


def image_specs(pair, steps_small, buffers):
    small = lambda *tail: pl.BlockSpec(
        (pair,) + tail, lambda i: (jnp.minimum(i, steps_small - 1), 0, 0), pipeline_mode=pl.Buffered(buffers)
    )
    large = lambda *tail: pl.BlockSpec((1,) + tail, lambda i: (jnp.maximum(i - steps_small, 0), 0, 0))
    return small, large


SAVED = [(D, f32), (3 * D, bf16), None, (D, bf16), (D, bf16), (D, f32), (FF, bf16), (FF, bf16), (D, bf16), (D, f32)]


def self_forward(ps, plg, stem, selfw, padded):
    ns, valid, _ = ps.shape
    nl, large_len, _ = plg.shape
    pair = pair_of(ns)
    steps_small = ns // pair
    patch_w, _, pos_small, pos_large = stem[:4]
    small, large = image_specs(pair, steps_small, 2)
    shapes, specs = [], []
    for n, length, spec in ((ns, padded, small), (nl, large_len, large)):
        for entry in SAVED:
            tail = (HEADS, length) if entry is None else (length, entry[0])
            shapes.append(sds((n,) + tail, f32 if entry is None else entry[1]))
            specs.append(spec(*tail))
    weights = selfw[:8]
    scratch = [pltpu.VMEM((pair * padded, D), f32)]
    for length in (padded, large_len):
        scratch += [
            pltpu.VMEM((D, length), f32),
            pltpu.VMEM((length, 2 * D), bf16),
            pltpu.VMEM((D, length), bf16),
            pltpu.VMEM((D, length), f32),
        ]
    out = pl.pallas_call(
        functools.partial(self_forward_kernel, steps_small, valid),
        grid=(steps_small + nl,),
        out_shape=shapes,
        in_specs=[small(valid, PATCH_IN), large(large_len, PATCH_IN)]
        + [const_spec(a) for a in (patch_w, pos_small, pos_large, *weights)],
        out_specs=specs,
        scratch_shapes=scratch,
        compiler_params=params(),
        cost_estimate=pl.CostEstimate(flops=60_000_000_000, bytes_accessed=60_000_000, transcendentals=0),
        name="self_forward",
    )(ps, plg, patch_w, pos_small, pos_large, *weights)
    return out[:10], out[10:]


BATCH = 8


def class_kernel(
    ns, nl, valid, out_s, out_l, wq, wkv, wo, w1, w2, vec, c1, svec, head_w, head_b, labels, live,
    d_s, d_l, g_wq, g_wkv, g_wo, g_w1, g_w2, g_vec, g_c1, g_svec, g_head_w, g_head_b, loss_o,
    a_s, a_l, p_s, p_l, z_ref, y_ref, b_ref, ps_ref, pc_ref, da_ref,
):
    row = lambda at: vec[at : at + 1, :]
    mask8 = head_mask(HEADS)
    mask64 = head_mask(HEADS * BATCH)
    cls = svec[1:2, :]
    unit_cls, inv_cls = stats(cls)
    a_cls = (unit_cls * row(CG1) + row(CB1)).astype(bf16)
    a_cls_f = a_cls.astype(f32)
    query = (nn(a_cls, wq[...]) + row(CBQ)).astype(bf16).astype(f32)
    q_diag = jnp.where(mask8, query, 0.0).astype(bf16)
    u_nat = nt(q_diag, wkv[:, 0:D]) * SCALE
    u_hi, u_lo = split(u_nat * LOG2E)
    u16 = jnp.concatenate([u_hi, u_lo], 0)
    s_cls = jnp.sum(u_nat * LOG2E * a_cls_f, -1, keepdims=True)
    z_ref[...] = jnp.zeros_like(z_ref)
    ps_ref[...] = jnp.zeros_like(ps_ref)

    def forward(i, src, a_ref, p_ref, slot):
        unit, _ = stats(src[i])
        a = (unit * row(CG1) + row(CB1)).astype(bf16)
        a_ref[i] = a
        s16 = nt(u16, a)
        s = s16[0:HEADS] + s16[HEADS:]
        keep = valid if a.shape[0] != GRID_LARGE**2 else a.shape[0]
        if keep < a.shape[0]:
            s = jnp.where(lax.broadcasted_iota(jnp.int32, s.shape, 1) < keep, s, NEG)
        top = jnp.maximum(jnp.max(s, -1, keepdims=True), s_cls)
        e = jnp.exp2(s - top)
        e_cls = jnp.exp2(s_cls - top)
        inverse = 1.0 / (jnp.sum(e, -1, keepdims=True) + e_cls)
        p, p_cls = e * inverse, e_cls * inverse
        p_ref[i] = p
        low, low_cls = p.astype(bf16), p_cls.astype(bf16).astype(f32)
        z_ref[pl.ds(slot * HEADS, HEADS), :] = nn(low, a) + low_cls * a_cls_f
        ps_ref[pl.ds(slot * HEADS, HEADS), :] = jnp.sum(low.astype(f32), -1, keepdims=True) + low_cls
        pc_ref[pl.ds(slot * HEADS, HEADS), :] = p_cls

    for i in range(ns):
        forward(i, out_s, a_s, p_s, i)
    for i in range(nl):
        forward(i, out_l, a_l, p_l, ns + i)

    z_hi, z_lo = split(z_ref[...])
    o_all = nn(jnp.concatenate([z_hi, z_lo], 0), wkv[:, D:])
    o_all = o_all[0 : HEADS * BATCH] + o_all[HEADS * BATCH :] + ps_ref[...] * row(CBV)
    att = jnp.sum(jnp.where(mask64, o_all, 0.0).reshape(BATCH, HEADS, D), 1).astype(bf16)
    branch = nn(att, wo[...]) + row(CBO)
    mid = cls + row(CLS1) * branch
    unit_mid, inv_mid = stats(mid)
    n2 = (unit_mid * row(CG2) + row(CB2)).astype(bf16)
    upper = nn(n2, w1[...]) + c1[...]
    act, slope = gelu_pair(upper)
    act = act.astype(bf16)
    lower = nn(act, w2[...]) + row(CC2)
    c_tok = mid + row(CLS2) * lower
    unit_c, inv_c = stats(c_tok)
    final = (unit_c * svec[2:3, :] + svec[3:4, :]).astype(bf16)
    logits = nn(final, head_w[...]) + head_b[...]
    lane = lax.broadcasted_iota(jnp.int32, logits.shape, 1)
    inside = lane < CLASSES
    logits = jnp.where(inside, logits, NEG)
    shifted = logits - jnp.max(logits, -1, keepdims=True)
    raw = jnp.exp(shifted)
    weight = jnp.sum(raw, -1, keepdims=True)
    logp = shifted - jnp.log(weight)
    hit = lane == labels[...]
    picked = jnp.sum(jnp.where(hit, logp, 0.0), -1, keepdims=True)
    mean = jnp.sum(jnp.where(inside, logp, 0.0), -1, keepdims=True) * (1.0 / CLASSES)
    each = -((1.0 - smooth) * picked + smooth * mean)
    scaled = live[...]
    loss_o[...] = jnp.broadcast_to(colsum(scaled * each), loss_o.shape)
    target = jnp.where(hit, 1.0 - smooth, 0.0) + smooth / CLASSES
    d_logits = jnp.where(inside, scaled * (raw / weight - target), 0.0).astype(bf16)

    d_final = nt(d_logits, head_w[...])
    g_head_w[...] = tn(final, d_logits)
    g_head_b[...] = colsum(d_logits.astype(f32))
    g_svec[...] = jnp.zeros_like(g_svec)
    g_svec[2:3, :] = colsum(d_final * unit_c)
    g_svec[3:4, :] = colsum(d_final)
    d_c = norm_back(d_final, unit_c, inv_c, svec[2:3, :])
    g_vec[...] = jnp.zeros_like(g_vec)
    g_vec[CLS2 : CLS2 + 1, :] = colsum(d_c * lower)
    d_lower = (d_c * row(CLS2)).astype(bf16)
    g_vec[CC2 : CC2 + 1, :] = colsum(d_lower.astype(f32))
    g_w2[...] = tn(act, d_lower)
    d_upper = (slope * nt(d_lower, w2[...])).astype(bf16)
    g_c1[...] = colsum(d_upper.astype(f32))
    g_w1[...] = tn(n2, d_upper)
    d_n2 = nt(d_upper, w1[...])
    g_vec[CG2 : CG2 + 1, :] = colsum(d_n2 * unit_mid)
    g_vec[CB2 : CB2 + 1, :] = colsum(d_n2)
    d_mid = d_c + norm_back(d_n2, unit_mid, inv_mid, row(CG2))
    g_vec[CLS1 : CLS1 + 1, :] = colsum(d_mid * branch)
    d_branch = (d_mid * row(CLS1)).astype(bf16)
    g_vec[CBO : CBO + 1, :] = colsum(d_branch.astype(f32))
    g_wo[...] = tn(att, d_branch)
    d_att = nt(d_branch, wo[...]).astype(bf16).astype(f32)
    d_diag = jnp.where(mask64, jnp.broadcast_to(d_att[:, None, :], (BATCH, HEADS, D)).reshape(BATCH * HEADS, D), 0.0)
    g_vec[CBV : CBV + 1, :] = colsum(d_diag * ps_ref[...])
    shift = jnp.sum(d_diag * row(CBV), -1, keepdims=True)
    d_diag_low = d_diag.astype(bf16)
    y_ref[...] = nt(d_diag_low, wkv[:, D:])
    g_wkv[:, D:] = tn(jnp.concatenate([z_hi, z_lo], 0), jnp.concatenate([d_diag_low, d_diag_low], 0))
    z_ref[:, 0:1] = shift
    b_ref[...] = jnp.zeros_like(b_ref)
    da_ref[...] = jnp.zeros_like(da_ref)
    un_hi, un_lo = split(u_nat)

    def backward(i, src, a_ref, p_ref, d_ref, slot):
        unit, inverse = stats(src[i])
        a = a_ref[i]
        here = pl.ds(slot * HEADS, HEADS)
        y = y_ref[here, :]
        y_hi, y_lo = split(y)
        d16 = nt(jnp.concatenate([y_hi, y_lo], 0), a)
        offset = z_ref[here, 0:1]
        d_p = d16[0:HEADS] + d16[HEADS:] + offset
        d_p_cls = jnp.sum(y * a_cls_f, -1, keepdims=True) + offset
        p, p_cls = p_ref[i], pc_ref[here, :]
        delta = jnp.sum(p * d_p, -1, keepdims=True) + p_cls * d_p_cls
        d_score = (p * (d_p - delta)).astype(bf16)
        d_score_cls = (p_cls * (d_p_cls - delta)).astype(bf16).astype(f32)
        low = p.astype(bf16)
        b_ref[...] += nn(d_score, a) + d_score_cls * a_cls_f
        da_ref[...] += d_score_cls * u_nat + p_cls.astype(bf16).astype(f32) * y
        left = jnp.concatenate([d_score.astype(f32), d_score.astype(f32), low.astype(f32), low.astype(f32)], 0)
        d_a = tn(left.astype(bf16), jnp.concatenate([un_hi, un_lo, y_hi, y_lo], 0))
        g_vec[CG1 : CG1 + 1, :] += colsum(d_a * unit)
        g_vec[CB1 : CB1 + 1, :] += colsum(d_a)
        d_ref[i] = norm_back(d_a, unit, inverse, row(CG1))

    for i in range(ns):
        backward(i, out_s, a_s, p_s, d_s, i)
    for i in range(nl):
        backward(i, out_l, a_l, p_l, d_l, ns + i)

    b_hi, b_lo = split(b_ref[...])
    bw = nn(jnp.concatenate([b_hi, b_lo], 0), wkv[:, 0:D])
    bw = bw[0:HEADS] + bw[HEADS:]
    d_query = (colsum(jnp.where(mask8, bw, 0.0)) * SCALE).astype(bf16)
    g_vec[CBQ : CBQ + 1, :] = d_query.astype(f32)
    q_scaled = q_diag.astype(f32) * SCALE
    qs_hi, qs_lo = split(q_scaled)
    g_wkv[:, 0:D] = tn(
        jnp.concatenate([b_hi, b_hi, b_lo, b_lo], 0), jnp.concatenate([qs_hi, qs_lo, qs_hi, qs_lo], 0)
    )
    first = lax.broadcasted_iota(jnp.int32, (16, D), 0) == 0
    spread_a = jnp.where(first, jnp.broadcast_to(a_cls_f, (16, D)), 0.0).astype(bf16)
    spread_q = jnp.where(first, jnp.broadcast_to(d_query.astype(f32), (16, D)), 0.0).astype(bf16)
    g_wq[...] = tn(spread_a, spread_q)
    d_a_cls = colsum(da_ref[...]) + nt(d_query, wq[...])
    g_vec[CG1 : CG1 + 1, :] += d_a_cls * unit_cls
    g_vec[CB1 : CB1 + 1, :] += d_a_cls
    g_svec[1:2, :] = colsum(d_mid) + norm_back(d_a_cls, unit_cls, inv_cls, row(CG1))


def class_block(out_s, out_l, classw, stem, labels, live, valid):
    ns, padded, _ = out_s.shape
    nl, large_len, _ = out_l.shape
    wq, wkv, wo, w1, w2, vec, c1 = classw
    _, svec, _, _, head_w, head_b = stem
    args = (out_s, out_l, wq, wkv, wo, w1, w2, vec, c1, svec, head_w, head_b, labels, live)
    return pl.pallas_call(
        functools.partial(class_kernel, ns, nl, valid),
        out_shape=[
            sds((ns, padded, D), f32),
            sds((nl, large_len, D), f32),
            sds((D, D), f32),
            sds((D, 2 * D), f32),
            sds((D, D), f32),
            sds((D, FF), f32),
            sds((FF, D), f32),
            sds((16, D), f32),
            sds((1, FF), f32),
            sds((8, D), f32),
            sds((D, CLASS_PAD), f32),
            sds((1, CLASS_PAD), f32),
            sds((1, LANES), f32),
        ],
        in_specs=[VM] * len(args),
        out_specs=[VM] * 13,
        scratch_shapes=[
            pltpu.VMEM((ns, padded, D), bf16),
            pltpu.VMEM((nl, large_len, D), bf16),
            pltpu.VMEM((ns, HEADS, padded), f32),
            pltpu.VMEM((nl, HEADS, large_len), f32),
            pltpu.VMEM((BATCH * HEADS, D), f32),
            pltpu.VMEM((BATCH * HEADS, D), f32),
            pltpu.VMEM((HEADS, D), f32),
            pltpu.VMEM((BATCH * HEADS, 1), f32),
            pltpu.VMEM((BATCH * HEADS, 1), f32),
            pltpu.VMEM((HEADS, D), f32),
        ],
        compiler_params=params(),
        cost_estimate=pl.CostEstimate(flops=10_000_000_000, bytes_accessed=60_000_000, transcendentals=0),
        name="class_block",
    )(*args)


def attend_back(qkv, d_att, lse, d_qkv, valid, pre_col, post_col, pre_row, post_row, g_pre, g_post, scr):
    length = qkv.shape[0]
    q_t, kk, k_t, do_t, dq_t, d_k, d_v = scr
    q, k, v = qkv[:, 0:D], qkv[:, D : 2 * D], qkv[:, 2 * D :]
    q_t[...] = q.astype(f32).T
    kk[:, 0:D] = k
    kk[:, D:] = k
    k_t[...] = k.astype(f32).T.astype(bf16)
    do_t[...] = d_att.astype(f32).T
    dq_t[...] = jnp.zeros_like(dq_t)
    d_k[...] = jnp.zeros_like(d_k)
    d_v[...] = jnp.zeros_like(d_v)
    for g in range(HEADS):
        high, low = split(q_t[...] * pre_col[:, g : g + 1])
        mixed = nn(kk[...], jnp.concatenate([high, low], 0))
        d_p = nn(v, (do_t[...] * post_col[:, g : g + 1]).astype(bf16))
        p = jnp.exp2(mixed - lse[g : g + 1, :])
        if valid < length:
            p = jnp.where(lax.broadcasted_iota(jnp.int32, p.shape, 0) < valid, p, 0.0)
        delta = colsum(p * d_p)
        d_mixed = (p * (d_p - delta)).astype(bf16)
        r = nn(p.astype(bf16), d_att)
        t = nn(d_mixed, q)
        u = nn(k_t[...], d_mixed)
        d_v[...] += r * post_row[g : g + 1, :]
        d_k[...] += t * pre_row[g : g + 1, :]
        dq_t[...] += u * pre_col[:, g : g + 1]
        g_post[g : g + 1, :] += colsum(r * v.astype(f32))
        g_pre[g : g + 1, :] += colsum(t * k.astype(f32))
    inverse = 1.0 / LOG2E
    d_qkv[:, 0:D] = (dq_t[...].T * inverse).astype(bf16)
    d_qkv[:, D : 2 * D] = (d_k[...] * inverse).astype(bf16)
    d_qkv[:, 2 * D :] = d_v[...].astype(bf16)


def self_backward_body(d_out, saved, valid, wr, grads, d_qkv, scr):
    wqkv, wo, w1, w2, vec, c1, pre_col, post_col, pre_row, post_row = wr
    g_wqkv, g_wo, g_w1, g_w2, g_vec, g_c1, g_pre, g_post = grads
    tok_r, qkv_r, lse_r, att_r, branch_r, mid_r, act_r, slope_r, lower_r = saved
    n, length = qkv_r.shape[0], qkv_r.shape[1]
    rows = n * length
    row = lambda at: vec[at : at + 1, :]

    def add(at, value):
        g_vec[at : at + 1, :] += value

    flat = lambda ref: ref[...].reshape(rows, D)
    add(SLS2, colsum(d_out * flat(lower_r).astype(f32)))
    d_lower = (d_out * row(SLS2)).astype(bf16)
    add(SC2, colsum(d_lower.astype(f32)))
    unit, inverse = stats(flat(mid_r))
    n2 = (unit * row(SG2) + row(SB2)).astype(bf16)
    d_n2 = None
    for c in range(0, FF, CHUNK):
        d_act = nt(d_lower, w2[c : c + CHUNK, :])
        slope = slope_r[:, :, c : c + CHUNK].reshape(rows, CHUNK).astype(f32)
        d_upper = (d_act * slope).astype(bf16)
        g_w2[c : c + CHUNK, :] += tn(act_r[:, :, c : c + CHUNK].reshape(rows, CHUNK), d_lower)
        g_w1[:, c : c + CHUNK] += tn(n2, d_upper)
        g_c1[:, c : c + CHUNK] += colsum(d_upper.astype(f32))
        part = nt(d_upper, w1[:, c : c + CHUNK])
        d_n2 = part if d_n2 is None else d_n2 + part
    add(SG2, colsum(d_n2 * unit))
    add(SB2, colsum(d_n2))
    d_mid = d_out + norm_back(d_n2, unit, inverse, row(SG2))
    add(SLS1, colsum(d_mid * flat(branch_r).astype(f32)))
    d_branch = (d_mid * row(SLS1)).astype(bf16)
    add(SBO, colsum(d_branch.astype(f32)))
    g_wo[...] += tn(flat(att_r), d_branch)
    d_att = nt(d_branch, wo[...]).astype(bf16)
    for i in range(n):
        attend_back(
            qkv_r.at[i], d_att[length * i : length * (i + 1), :], lse_r.at[i], d_qkv.at[pl.ds(length * i, length)],
            valid, pre_col, post_col, pre_row, post_row, g_pre, g_post, scr,
        )
    add(SBQ, colsum(d_qkv[:, 0:D].astype(f32)))
    add(SBV, colsum(d_qkv[:, 2 * D :].astype(f32)))
    unit, inverse = stats(flat(tok_r))
    a1 = (unit * row(SG1) + row(SB1)).astype(bf16)
    d_a1 = None
    for part in range(3):
        here = slice(D * part, D * (part + 1))
        g_wqkv[:, here] += tn(a1, d_qkv[:, here])
        term = nt(d_qkv[:, here], wqkv[:, here])
        d_a1 = term if d_a1 is None else d_a1 + term
    add(SG1, colsum(d_a1 * unit))
    add(SB1, colsum(d_a1))
    return d_mid + norm_back(d_a1, unit, inverse, row(SG1))


def self_backward_kernel(steps_small, steps, valid, *refs):
    (ps, plg, resize), refs = refs[:3], refs[3:]
    small, large, refs = refs[:10], refs[10:20], refs[20:]
    wr, refs = refs[:10], refs[10:]
    grads, (g_patch_w, g_patch_b, g_pos), refs = refs[:8], refs[8:11], refs[11:]
    pos_large, dq_small, dq_large, scr = refs[0], refs[1], refs[2], refs[3:]
    scr_small, scr_large = scr[:7], scr[7:14]
    step = pl.program_id(0)

    @pl.when(step == 0)
    def _():
        for ref in (*grads, g_patch_w, g_patch_b, g_pos, pos_large):
            ref[...] = jnp.zeros_like(ref)

    @pl.when(step < steps_small)
    def _():
        n, length = small[0].shape[0], small[0].shape[1]
        d_out = small[9][...].reshape(n * length, D)
        d_tok = self_backward_body(d_out, small[:9], valid, wr, grads, dq_small, scr_small)
        g_patch_b[0:1, :] += colsum(d_tok)
        for i in range(n):
            mine = d_tok[length * i : length * (i + 1), :]
            g_pos[...] += mine[0:valid, :]
            g_patch_w[...] += tn(ps[i], mine[0:valid, :].astype(bf16))

    @pl.when(step >= steps_small)
    def _():
        length = large[0].shape[1]
        d_tok = self_backward_body(large[9][0], large[:9], length, wr, grads, dq_large, scr_large)
        g_patch_b[0:1, :] += colsum(d_tok)
        pos_large[...] += d_tok
        g_patch_w[...] += tn(plg[0], d_tok.astype(bf16))

    @pl.when(step == steps - 1)
    def _():
        g_pos[...] += lax.dot_general(
            resize[...], pos_large[...], (((1,), (0,)), ((), ())),
            preferred_element_type=f32, precision=lax.Precision.HIGHEST,
        )


def self_backward(ps, plg, saved_s, saved_l, d_s, d_l, selfw):
    ns, valid, _ = ps.shape
    nl, large_len, _ = plg.shape
    padded = d_s.shape[1]
    pair = pair_of(ns)
    steps_small = ns // pair
    small, large = image_specs(pair, steps_small, 1)
    resize = jnp.asarray(resize_table().T.copy())
    in_specs = [small(valid, PATCH_IN), large(large_len, PATCH_IN), const_spec(resize)]
    for length, spec in ((padded, small), (large_len, large)):
        for entry in SAVED[:9]:
            in_specs.append(spec(*((HEADS, length) if entry is None else (length, entry[0]))))
        in_specs.append(spec(length, D))
    in_specs += [const_spec(a) for a in selfw]
    shapes = [
        sds((D, 3 * D), f32),
        sds((D, D), f32),
        sds((D, FF), f32),
        sds((FF, D), f32),
        sds((16, D), f32),
        sds((1, FF), f32),
        sds((HEADS, D), f32),
        sds((HEADS, D), f32),
        sds((PATCH_IN, D), f32),
        sds((8, D), f32),
        sds((valid, D), f32),
    ]
    scratch = [
        pltpu.VMEM((large_len, D), f32),
        pltpu.VMEM((pair * padded, 3 * D), bf16),
        pltpu.VMEM((large_len, 3 * D), bf16),
    ]
    for length in (padded, large_len):
        scratch += [
            pltpu.VMEM((D, length), f32),
            pltpu.VMEM((length, 2 * D), bf16),
            pltpu.VMEM((D, length), bf16),
            pltpu.VMEM((D, length), f32),
            pltpu.VMEM((D, length), f32),
            pltpu.VMEM((length, D), f32),
            pltpu.VMEM((length, D), f32),
        ]
    return pl.pallas_call(
        functools.partial(self_backward_kernel, steps_small, steps_small + nl, valid),
        grid=(steps_small + nl,),
        out_shape=shapes,
        in_specs=in_specs,
        out_specs=[pl.BlockSpec(s.shape, lambda i: (0, 0), pipeline_mode=pl.Buffered(1)) for s in shapes],
        scratch_shapes=scratch,
        compiler_params=params(),
        cost_estimate=pl.CostEstimate(flops=120_000_000_000, bytes_accessed=60_000_000, transcendentals=0),
        name="self_backward",
    )(ps, plg, resize, *saved_s[:9], d_s, *saved_l[:9], d_l, *selfw)


def take_matrix(flat, row, src, rows, cols):
    step = cols // LANES
    for j in range(step):
        flat[pl.ds(row + j, rows, stride=step), :] = src[:, LANES * j : LANES * (j + 1)]


def take_row(flat, row, src, at, cols):
    for j in range(cols // LANES):
        flat[row + j : row + j + 1, :] = src[at : at + 1, LANES * j : LANES * (j + 1)]


def slots_of(order):
    rels = [0]
    for bit in reversed(order):
        rels = rels + [r | (1 << bit) for r in rels]
    return rels


def emit_slots(me, flat, rows, rels, keep_ref, send_ref):
    half = len(rels) // 2
    for k, r in enumerate(rels):
        value = flat[pl.ds(rows * jnp.bitwise_xor(me, r), rows), :]
        if k < half:
            keep_ref[k] = value
        else:
            send_ref[k - half] = value.astype(bf16)


def pack_class_kernel(rels, rows, me_ref, wq, wkv, wo, w1, w2, vec, c1, keep, send, flat):
    used = rows_used(2)
    flat[used:, :] = jnp.zeros((flat.shape[0] - used, LANES), f32)
    take_matrix(flat, row_of(2, 2), wq, D, D)
    take_matrix(flat, row_of(2, 4), wkv, D, 2 * D)
    take_matrix(flat, row_of(2, 6), wo, D, D)
    take_matrix(flat, row_of(2, 11), w1, D, FF)
    take_matrix(flat, row_of(2, 13), w2, FF, D)
    for at, number in (
        (CG1, 0), (CB1, 1), (CBQ, 3), (CBV, 5), (CBO, 7), (CLS1, 8), (CG2, 9), (CB2, 10), (CC2, 14), (CLS2, 15),
    ):
        take_row(flat, row_of(2, number), vec, at, D)
    take_row(flat, row_of(2, 12), c1, 0, FF)
    emit_slots(me_ref[0], flat, rows, rels, keep, send)


def pack_self_kernel(rels, rows, me_ref, wqkv, wo, w1, w2, vec, c1, pre, post, keep, send, flat):
    used = rows_used(1)
    flat[used:, :] = jnp.zeros((flat.shape[0] - used, LANES), f32)
    take_matrix(flat, row_of(1, 2), wqkv, D, 3 * D)
    take_matrix(flat, row_of(1, 6), wo, D, D)
    take_matrix(flat, row_of(1, 11), w1, D, FF)
    take_matrix(flat, row_of(1, 13), w2, FF, D)
    bq = row_of(1, 3)
    for at, row in (
        (SG1, row_of(1, 0)), (SB1, row_of(1, 1)), (SBQ, bq), (SBV, bq + D // LANES), (SBO, row_of(1, 7)),
        (SLS1, row_of(1, 8)), (SG2, row_of(1, 9)), (SB2, row_of(1, 10)), (SC2, row_of(1, 14)), (SLS2, row_of(1, 15)),
    ):
        take_row(flat, row, vec, at, D)
    take_row(flat, row_of(1, 12), c1, 0, FF)
    table_col = lax.broadcasted_iota(jnp.int32, (D, LANES), 0) // WIDTH
    table_lane = lax.broadcasted_iota(jnp.int32, (D, LANES), 1)
    lane = lax.broadcasted_iota(jnp.int32, (HEADS, LANES), 1)
    row = lax.broadcasted_iota(jnp.int32, (HEADS, LANES), 0)
    exact = lambda a, b: lax.dot_general(
        a, b, (((1,), (0,)), ((), ())), preferred_element_type=f32, precision=lax.Precision.HIGHEST
    )
    sum_pre = exact(pre[...], jnp.where(table_lane % HEADS == table_col, 1.0, 0.0))
    sum_post = exact(post[...], jnp.where((table_lane - 64) // HEADS == table_col, 1.0, 0.0))
    line = colsum(jnp.where((lane < 64) & (lane // HEADS == row), sum_pre * SCALE, 0.0))
    line = line + colsum(jnp.where((lane >= 64) & (lane % HEADS == row), sum_post, 0.0))
    flat[row_of(1, 4) : row_of(1, 4) + 1, :] = line
    emit_slots(me_ref[0], flat, rows, rels, keep, send)


def pack_stem_kernel(
    rels, rows, me_ref, patch_w, patch_b, pos, svec, head_w, head_b, keep, send, flat, tiles
):
    used = row_of(0, 6)
    flat[used:, :] = jnp.zeros((flat.shape[0] - used, LANES), f32)
    take_matrix(flat, row_of(0, 0), patch_w, PATCH_IN, D)
    take_row(flat, row_of(0, 1), patch_b, 0, D)
    take_matrix(flat, row_of(0, 2), pos, GRID_SMALL**2, D)
    for at, number in ((1, 3), (2, 4), (3, 5)):
        take_row(flat, row_of(0, number), svec, at, D)
    for t in range(8):
        tiles[t] = head_w[:, LANES * t : LANES * (t + 1)]
    lane = lax.broadcasted_iota(jnp.int32, (24, LANES), 1)
    base = row_of(0, 6)
    for rho in range(16):
        first, shift = (CLASSES * rho) // LANES, (CLASSES * rho) % LANES
        parts = [tiles[t, pl.ds(rho, 24, stride=16), :] for t in range(8)]
        if shift:
            parts = [pltpu.roll(p, shift, 1) for p in parts]
        for t in range(9 if shift + CLASSES > CLASS_PAD else 8):
            if shift:
                value = jnp.where(lane >= shift, parts[t] if t < 8 else 0.0, parts[t - 1] if t > 0 else 0.0)
            else:
                value = parts[t]
            here = pl.ds(base + first + t, 24, stride=125)
            flat[here, :] = flat[here, :] + value
    take_row(flat, row_of(0, 7), head_b, 0, CLASS_PAD)
    emit_slots(me_ref[0], flat, rows, rels, keep, send)


def pack(kernel, name, me, arrays, rels, rows, extra=()):
    half = len(rels) // 2
    return pl.pallas_call(
        functools.partial(kernel, rels, rows),
        out_shape=[sds((half, rows, LANES), f32), sds((half, rows, LANES), bf16)],
        in_specs=[SM] + [VM] * len(arrays),
        out_specs=[VM] * 2,
        scratch_shapes=[pltpu.VMEM((len(rels) * rows, LANES), f32), *extra],
        compiler_params=params(),
        name=name,
    )(me, *arrays)


def reduce_slots(keep, send, order, z_bits):
    for number, bit in enumerate(order):
        got = exchange(send, bit, z_bits)
        total = keep + got.astype(f32)
        if number == len(order) - 1:
            return total[0]
        half = total.shape[0] // 2
        keep, send = total[:half], total[half:].astype(bf16)


def bounds_of(group, number):
    return int(STARTS[group, number]), int(ENDS[group, number])


def segment_sums(square, position):
    lane = lax.broadcasted_iota(jnp.int32, (3, LANES), 1)
    group = lax.broadcasted_iota(jnp.int32, (3, 1), 0)
    out = jnp.zeros((3, LANES), f32)
    for s in range(SEGMENTS):
        low = pick(group, [int(STARTS[g, s]) for g in range(3)])
        high = pick(group, [int(ENDS[g, s]) for g in range(3)])
        value = jnp.sum(jnp.where((position >= low) & (position < high), square, 0.0), -1, keepdims=True)
        out = jnp.where(lane == s, value, out)
    return out


def pick(group, values):
    return jnp.where(group == 0, values[0], jnp.where(group == 1, values[1], values[2]))


def adam_kernel(rows, me_ref, rate_ref, master, first, second, g0, g1, g2, grad_o, first_o, second_o, update_o, sums_o):
    shard = rows * LANES
    for g, ref in enumerate((g0, g1, g2)):
        grad_o[g : g + 1, :] = ref[...].reshape(1, shard)
    grad = grad_o[...]
    weight = master[...]
    new_first = beta_one * first[...] + (1.0 - beta_one) * grad
    new_second = beta_two * second[...] + (1.0 - beta_two) * grad * grad
    first_o[...] = new_first
    second_o[...] = new_second
    correct_one, correct_two = rate_ref[0], rate_ref[1]
    update = new_first / correct_one / (jnp.sqrt(new_second / correct_two) + adam_eps) + decay_rate * weight
    update_o[...] = update
    position = me_ref[0] * shard + lax.broadcasted_iota(jnp.int32, (3, shard), 1)
    sums_o[0:3, :] = segment_sums(weight * weight, position)
    sums_o[3:6, :] = segment_sums(update * update, position)
    sums_o[6:8, :] = jnp.zeros((2, LANES), f32)


def adam(me, rates, master, first, second, grads, rows):
    shape = master.shape
    return pl.pallas_call(
        functools.partial(adam_kernel, rows),
        out_shape=[sds(shape, f32)] * 4 + [sds((8, LANES), f32)],
        in_specs=[SM, SM] + [VM] * 6,
        out_specs=[VM] * 5,
        compiler_params=params(),
        name="adam",
    )(me, rates, master, first, second, *grads)


def apply_kernel(me_ref, sums, master, update, new_o, norms_o):
    shard = master.shape[1]
    roots = jnp.sqrt(sums[...])
    weight_norms, update_norms = roots[0:3, :], roots[3:6, :]
    lane = lax.broadcasted_iota(jnp.int32, (3, LANES), 1)
    group3 = lax.broadcasted_iota(jnp.int32, (3, LANES), 0)
    used = pick(group3, [int(REAL[g].sum()) for g in range(3)])
    trust = jnp.where(lane < used, weight_norms / (update_norms + norm_eps), 1.0)
    norms_o[0] = weight_norms
    norms_o[1] = update_norms
    norms_o[2] = trust
    position = me_ref[0] * shard + lax.broadcasted_iota(jnp.int32, (3, shard), 1)
    group = lax.broadcasted_iota(jnp.int32, (3, 1), 0)
    ratio = jnp.broadcast_to(trust[:, 0:1], (3, shard))
    for s in range(1, SEGMENTS):
        low = pick(group, [int(STARTS[g, s]) if REAL[g, s] > 0 else 2**30 for g in range(3)])
        ratio = jnp.where(position >= low, trust[:, s : s + 1], ratio)
    new_o[...] = master[...] - learn_rate * ratio * update[...]


def apply_update(me, sums, master, update):
    return pl.pallas_call(
        apply_kernel,
        out_shape=[sds(master.shape, f32), sds((3, 3, LANES), f32)],
        in_specs=[SM] + [VM] * 3,
        out_specs=[VM] * 2,
        compiler_params=params(),
        name="apply_update",
    )(me, sums, master, update)


def round_kernel(rows, count_ref, master, stem, selfb, classb):
    for g, ref in enumerate((stem, selfb, classb)):
        ref[0, 0:rows, :] = master[g : g + 1, :].reshape(rows, LANES).astype(bf16)
    tail = classb.shape[1] - rows
    classb[0, rows:, :] = jnp.full((tail, LANES), count_ref[0], f32).astype(bf16)


def round_shards(count, master, rows, class_rows):
    return pl.pallas_call(
        functools.partial(round_kernel, rows),
        out_shape=[sds((1, rows, LANES), bf16), sds((1, rows, LANES), bf16), sds((1, class_rows, LANES), bf16)],
        in_specs=[SM, VM],
        out_specs=[VM] * 3,
        compiler_params=params(),
        name="round_shards",
    )(count, master)


def on_device(
    master,
    first_moment,
    second_moment,
    patches_small,
    patches_large,
    labels_small,
    labels_large,
    counts,
    step,
):
    rows = master.shape[1] // LANES
    n_dp, n_z = lax.axis_size("dp"), lax.axis_size("fsdp")
    z_bits, bits = log2(n_z), log2(n_dp) + log2(n_z)
    devices = n_dp * n_z
    top = bits - 1
    ns, valid, _ = patches_small.shape
    nl = patches_large.shape[0]
    padded = -(-valid // 16) * 16
    index = lax.axis_index(AXES).astype(jnp.int32)
    me = index.reshape(1)

    z_order = list(range(z_bits - 1, -1, -1))
    core = z_bits
    middle = list(range(core + 1, bits))
    stem_short = int(ENDS[0].max()) <= (devices // 2) * master.shape[1]

    local_count = jnp.sum(counts).astype(f32).reshape(1)
    class_rows = rows + 1
    stem_shard, self_shard, class_shard = round_shards(local_count, master, rows, class_rows)

    if stem_short:
        half = n_dp // 2
        got = lax.ppermute(stem_shard, "dp", [(i, i + half) for i in range(half)])
        stem_shard = jnp.where(lax.axis_index("dp") < half, stem_shard, got)
        stem_me = jnp.bitwise_and(me, devices // 2 - 1)
        stem_order = z_order + middle[:-1] + [core]
        stem_count = devices // 2
    else:
        stem_me, stem_order, stem_count = me, z_order + middle + [core], devices
    self_state = gather_pieces([(self_shard, [0])], z_order + middle + [core], z_bits)
    stem_state = gather_pieces([(stem_shard, [0])], stem_order, z_bits)
    class_shard, _ = lax.optimization_barrier((class_shard, self_state[len(self_state) // 2][0]))
    class_state = gather_pieces([(class_shard, [0])], z_order + middle[::-1] + [core], z_bits)

    arrays = lambda state: ([a for a, _ in state], [r for _, r in state])
    stem = unpack_stem(stem_me, *arrays(stem_state), rows, stem_count, padded)
    selfw = unpack_self(me, *arrays(self_state), rows, devices)
    saved_s, saved_l = self_forward(patches_small, patches_large, stem, selfw, padded)
    *classw, total = unpack_class(me, *arrays(class_state), rows, devices)

    live = jnp.concatenate([jnp.arange(ns) < counts[0, 0], jnp.arange(nl) < counts[0, 1]]).astype(f32)
    live = jnp.pad(live, (0, BATCH - ns - nl)).reshape(BATCH, 1) / total[0, 0]
    labels = jnp.pad(jnp.concatenate([labels_small, labels_large]), (0, BATCH - ns - nl)).reshape(BATCH, 1)
    d_s, d_l, *class_grads, g_svec, g_head_w, g_head_b, loss = class_block(
        saved_s[9], saved_l[9], classw, stem, labels, live, valid
    )

    order = [core] + middle[::-1] + z_order
    rels = slots_of(order)
    grad_class = reduce_slots(*pack(pack_class_kernel, "pack_class", me, class_grads, rels, rows), order, z_bits)

    *self_grads, g_patch_w, g_patch_b, g_pos = self_backward(
        patches_small, patches_large, saved_s, saved_l, d_s, d_l, selfw
    )
    stem_grads = (g_patch_w, g_patch_b, g_pos, g_svec, g_head_w, g_head_b)
    tiles = [pltpu.VMEM((8, D, LANES), f32)]
    if stem_short:
        stem_order = [core] + middle[:-1] + z_order
        keep, send = pack(pack_stem_kernel, "pack_stem", stem_me, stem_grads, slots_of(stem_order), rows, tiles)
        part = reduce_slots(keep, send, stem_order, z_bits)
        got = lax.ppermute(part.astype(bf16), "dp", [(i + half, i) for i in range(half)])
        grad_stem = jnp.where(lax.axis_index("dp") < half, part + got.astype(f32), 0.0)
    else:
        grad_stem = reduce_slots(*pack(pack_stem_kernel, "pack_stem", me, stem_grads, rels, rows, tiles), order, z_bits)
    grad_self = reduce_slots(*pack(pack_self_kernel, "pack_self", me, self_grads, rels, rows), order, z_bits)

    count_f = step[0].astype(f32)
    rates = jnp.stack([1.0 - beta_one**count_f, 1.0 - beta_two**count_f])
    gradients, new_first, new_second, update, sums = adam(
        me, rates, master, first_moment, second_moment, (grad_stem, grad_self, grad_class), rows
    )
    sums = jnp.concatenate([sums[:6], loss, sums[7:]], 0)
    for bit in range(bits):
        sums = sums + exchange(sums, bit, z_bits)
    new_master, norms = apply_update(me, sums, master, update)
    return (
        sums[6, 0],
        gradients,
        new_first,
        new_second,
        new_master,
        norms[0, :, :SEGMENTS],
        norms[1, :, :SEGMENTS],
        norms[2, :, :SEGMENTS],
    )


def solution(mesh):
    return jax.shard_map(
        on_device,
        mesh=mesh,
        in_specs=(
            P(None, AXES),
            P(None, AXES),
            P(None, AXES),
            P(AXES, None, None),
            P(AXES, None, None),
            P(AXES),
            P(AXES),
            P(AXES, None),
            P(),
        ),
        out_specs=(
            P(),
            P(None, AXES),
            P(None, AXES),
            P(None, AXES),
            P(None, AXES),
            P(),
            P(),
            P(),
        ),
        check_vma=False,
    )
```

```python
import functools
import math

import jax
import jax.numpy as jnp
import numpy as np
from jax import lax
from jax.experimental import pallas as pl
from jax.experimental.pallas import tpu as pltpu
from jax.sharding import PartitionSpec as P

D = 384
HEADS = 8
WIDTH = D // HEADS
FF = 1536
CLASSES = 1000
CLASS_PAD = 1024
PATCH_IN = 768
GRID_SMALL = 14
GRID_LARGE = 24
LANES = 128
SEGMENTS = 16

LOG2E = 1.4426950408889634
SCALE = WIDTH**-0.5
NEG = -1e30
smooth = 0.1
beta_one = 0.9
beta_two = 0.999
adam_eps = 1e-06
decay_rate = 0.01
learn_rate = 0.3
norm_eps = 1e-06

f32 = jnp.float32
bf16 = jnp.bfloat16
AXES = ("dp", "fsdp")
VMEM_BYTES = 60 << 20


def shapes_of():
    dim = D
    tail = [(dim,), (dim,), (dim, FF), (FF,), (FF, dim), (dim,), (dim,)]
    stem = [
        (PATCH_IN, dim),
        (dim,),
        (GRID_SMALL * GRID_SMALL, dim),
        (dim,),
        (dim,),
        (dim,),
        (dim, CLASSES),
        (CLASSES,),
    ]
    selfb = [
        (dim,),
        (dim,),
        (dim, 3 * dim),
        (2 * dim,),
        (HEADS, HEADS),
        (HEADS, HEADS),
        (dim, dim),
        (dim,),
        (dim,),
    ] + tail
    classb = [
        (dim,),
        (dim,),
        (dim, dim),
        (dim,),
        (dim, 2 * dim),
        (dim,),
        (dim, dim),
        (dim,),
        (dim,),
    ] + tail
    return [stem, selfb, classb]


def segment_bounds():
    starts = np.zeros((3, SEGMENTS), np.int32)
    ends = np.zeros((3, SEGMENTS), np.int32)
    real = np.zeros((3, SEGMENTS), np.float32)
    for group, shapes in enumerate(shapes_of()):
        offset = 0
        for number, shape in enumerate(shapes):
            count = int(np.prod(shape))
            starts[group, number] = offset
            ends[group, number] = offset + count
            real[group, number] = 1.0
            offset += count
    return starts, ends, real


STARTS, ENDS, REAL = segment_bounds()


def row_of(group, number):
    return int(STARTS[group, number]) // LANES


def rows_used(group):
    return -(-int(ENDS[group].max()) // LANES)


def resize_table():
    rows = np.arange(GRID_LARGE).astype(np.float32) * np.float32((GRID_SMALL - 1) / (GRID_LARGE - 1))
    cols = np.arange(GRID_SMALL).astype(np.float32)
    line = np.maximum(np.float32(0.0), np.float32(1.0) - np.abs(rows[:, None] - cols[None, :]))
    return (line[:, None, :, None] * line[None, :, None, :]).reshape(GRID_LARGE**2, GRID_SMALL**2)


def nn(a, b):
    return lax.dot_general(a, b, (((1,), (0,)), ((), ())), preferred_element_type=f32)


def nt(a, b):
    return lax.dot_general(a, b, (((1,), (1,)), ((), ())), preferred_element_type=f32)


def tn(a, b):
    return lax.dot_general(a, b, (((0,), (0,)), ((), ())), preferred_element_type=f32)


def colsum(value):
    return jnp.sum(value, 0, keepdims=True)


def split(value):
    high = value.astype(bf16)
    return high, (value - high.astype(f32)).astype(bf16)


def stats(value):
    centred = value - jnp.mean(value, -1, keepdims=True)
    inverse = lax.rsqrt(jnp.mean(centred * centred, -1, keepdims=True) + 1e-06)
    return centred * inverse, inverse


def norm_back(d_out, unit, inverse, gain):
    inner = d_out * gain
    first = jnp.mean(inner, -1, keepdims=True)
    second = jnp.mean(inner * unit, -1, keepdims=True)
    return inverse * (inner - first - unit * second)


def gelu_pair(upper):
    cdf = 0.5 * (1.0 + lax.erf(upper * (0.5**0.5)))
    density = jnp.exp(-0.5 * upper * upper) * 0.3989422804014327
    return upper * cdf, cdf + upper * density


def head_mask(rows):
    lane = lax.broadcasted_iota(jnp.int32, (rows, D), 1)
    row = lax.broadcasted_iota(jnp.int32, (rows, D), 0)
    return (lane // WIDTH) == lax.rem(row, HEADS)


VM = pl.BlockSpec(memory_space=pltpu.VMEM)
SM = pl.BlockSpec(memory_space=pltpu.SMEM)


def params(**kw):
    return pltpu.CompilerParams(vmem_limit_bytes=VMEM_BYTES, **kw)


def sds(shape, dtype):
    return jax.ShapeDtypeStruct(shape, dtype)


def call(kernel, args, after, in_specs, **kw):
    n, m = len(args), len(after)

    def wrapped(*refs):
        kernel(*refs[:n], *refs[n + m :])

    specs = list(in_specs) + [pl.BlockSpec(memory_space=pl.ANY)] * m
    return pl.pallas_call(wrapped, in_specs=specs, compiler_params=params(), **kw)(*args, *after)


def log2(n):
    return n.bit_length() - 1


def exchange(value, bit, z_bits):
    if bit < z_bits:
        n = lax.axis_size("fsdp")
        return lax.ppermute(value, "fsdp", [(i, i ^ (1 << bit)) for i in range(n)])
    n = lax.axis_size("dp")
    return lax.ppermute(value, "dp", [(i, i ^ (1 << (bit - z_bits))) for i in range(n)])


def exchange_z(value, k):
    n = lax.axis_size("fsdp")
    return lax.ppermute(value, "fsdp", [(i, i ^ k) for i in range(n)])


def tied(values, after):
    if after is None:
        return values
    return lax.optimization_barrier((*values, after))[:-1]


def gather_z(value, rel, after=None):
    n = lax.axis_size("fsdp")
    got = tied([exchange_z(value, k) for k in range(1, n)], after)
    return [(jnp.concatenate([value, *got], 0), [r | k for k in range(n) for r in rel])]


def gather_bit(state, bit, z_bits, after=None):
    got = tied([exchange(a, bit, z_bits) for a, _ in state], after)
    return state + [(a, [r | (1 << bit) for r in rel]) for a, (_, rel) in zip(got, state)]


def put_matrix(flat, row, out_ref, rows, cols):
    step = cols // LANES
    for j in range(step):
        out_ref[:, LANES * j : LANES * (j + 1)] = flat[pl.ds(row + j, rows, stride=step), :].astype(bf16)


def put_row(flat, row, out_ref, at, cols):
    for j in range(cols // LANES):
        out_ref[at : at + 1, LANES * j : LANES * (j + 1)] = flat[row + j : row + j + 1, :]


def fill_flat(me, piece_refs, rels, rows, flat):
    for ref, rel in zip(piece_refs, rels):
        for k, r in enumerate(rel):
            flat[pl.ds(rows * jnp.bitwise_xor(me, r), rows), :] = ref[k, 0:rows, :].astype(f32)


def unpack_stem_kernel(rels, rows, me_ref, resize_ref, *refs):
    n = len(rels)
    pieces, (patch_w, vec, pos_small, pos_large, head_w, head_b), (flat, tiles) = refs[:n], refs[n : n + 6], refs[n + 6 :]
    fill_flat(me_ref[0], pieces, rels, rows, flat)
    put_matrix(flat, row_of(0, 0), patch_w, PATCH_IN, D)
    vec[...] = jnp.zeros_like(vec)
    for at, number in enumerate((1, 3, 4, 5)):
        put_row(flat, row_of(0, number), vec, at, D)
    bias = vec[0:1, :]
    small = GRID_SMALL**2
    pos_small[...] = jnp.zeros_like(pos_small)
    for j in range(D // LANES):
        pos_small[0:small, LANES * j : LANES * (j + 1)] = flat[pl.ds(row_of(0, 2) + j, small, stride=D // LANES), :]
    pos_large[...] = (
        lax.dot_general(
            resize_ref[...], pos_small[...], (((1,), (0,)), ((), ())),
            preferred_element_type=f32, precision=lax.Precision.HIGHEST,
        )
        + bias
    )
    pos_small[...] += bias
    lane = lax.broadcasted_iota(jnp.int32, (24, LANES), 1)
    base = row_of(0, 6)
    for rho in range(16):
        first, shift = (CLASSES * rho) // LANES, (CLASSES * rho) % LANES
        parts = [flat[pl.ds(base + first + t, 24, stride=125), :] for t in range(9)]
        if shift:
            parts = [pltpu.roll(p, LANES - shift, 1) for p in parts]
        for t in range(8):
            value = jnp.where(lane < LANES - shift, parts[t], parts[t + 1]) if shift else parts[t]
            if t == 7:
                value = jnp.where(lane < CLASSES - 7 * LANES, value, 0.0)
            tiles[t, pl.ds(rho, 24, stride=16), :] = value
    for t in range(8):
        head_w[:, LANES * t : LANES * (t + 1)] = tiles[t].astype(bf16)
    put_row(flat, row_of(0, 7), head_b, 0, CLASS_PAD)


def unpack_stem(me, pieces, rels, rows, count, padded):
    resize = np.zeros((GRID_LARGE**2, padded), np.float32)
    resize[:, : GRID_SMALL**2] = resize_table()
    return pl.pallas_call(
        functools.partial(unpack_stem_kernel, rels, rows),
        out_shape=[
            sds((PATCH_IN, D), bf16),
            sds((8, D), f32),
            sds((padded, D), f32),
            sds((GRID_LARGE**2, D), f32),
            sds((D, CLASS_PAD), bf16),
            sds((1, CLASS_PAD), f32),
        ],
        in_specs=[SM] + [VM] * (1 + len(pieces)),
        out_specs=[VM] * 6,
        scratch_shapes=[pltpu.VMEM((count * rows, LANES), f32), pltpu.VMEM((8, D, LANES), f32)],
        compiler_params=params(),
        name="unpack_stem",
    )(me, jnp.asarray(resize), *pieces)


SG1, SB1, SBQ, SBV, SBO, SLS1, SG2, SB2, SC2, SLS2 = range(10)
CG1, CB1, CBQ, CBV, CBO, CLS1, CG2, CB2, CC2, CLS2 = range(10)


def unpack_low_kernel(rels, rows, me_ref, *refs):
    n = len(rels)
    pieces = refs[:n]
    wqkv, vec, pre_col, post_col, pre_row, post_row, flat = refs[n:]
    fill_flat(me_ref[0], pieces, rels, rows, flat)
    put_matrix(flat, row_of(1, 2), wqkv, D, 3 * D)
    vec[...] = jnp.zeros_like(vec)
    bq = row_of(1, 3)
    for at, row in ((SG1, row_of(1, 0)), (SB1, row_of(1, 1)), (SBQ, bq), (SBV, bq + D // LANES)):
        put_row(flat, row, vec, at, D)
    mix = jnp.broadcast_to(flat[row_of(1, 4) : row_of(1, 4) + 1, :], (HEADS, LANES))
    lane = lax.broadcasted_iota(jnp.int32, (HEADS, LANES), 1)
    row = lax.broadcasted_iota(jnp.int32, (HEADS, LANES), 0)
    pick_pre = jnp.where((lane < 64) & (lane // HEADS == row), mix, 0.0).astype(bf16)
    pick_post = jnp.where((lane >= 64) & (lane % HEADS == row), mix, 0.0).astype(bf16)
    table_lane = lax.broadcasted_iota(jnp.int32, (LANES, D), 0)
    table_col = lax.broadcasted_iota(jnp.int32, (LANES, D), 1) // WIDTH
    spread_pre = jnp.where(table_lane % HEADS == table_col, 1.0, 0.0).astype(bf16)
    spread_post = jnp.where((table_lane - 64) // HEADS == table_col, 1.0, 0.0).astype(bf16)
    factor = SCALE * LOG2E
    pre_row[...] = nn(pick_pre, spread_pre) * factor
    post_row[...] = nn(pick_post, spread_post)
    column = lambda a, b: lax.dot_general(a, b, (((0,), (1,)), ((), ())), preferred_element_type=f32)
    pre_col[...] = column(spread_pre, pick_pre) * factor
    post_col[...] = column(spread_post, pick_post)


def unpack_low(me, pieces, rels, rows, count):
    return pl.pallas_call(
        functools.partial(unpack_low_kernel, rels, rows),
        out_shape=[
            sds((D, 3 * D), bf16),
            sds((16, D), f32),
            sds((D, HEADS), f32),
            sds((D, HEADS), f32),
            sds((HEADS, D), f32),
            sds((HEADS, D), f32),
        ],
        in_specs=[SM] + [VM] * len(pieces),
        out_specs=[VM] * 6,
        scratch_shapes=[pltpu.VMEM((count * rows, LANES), f32)],
        compiler_params=params(),
        name="unpack_low",
    )(me, *pieces)


def unpack_feed_kernel(rels, rows, me_ref, *refs):
    n = len(rels)
    pieces = refs[:n]
    wo, w1, w2, vec, c1, flat = refs[n:]
    fill_flat(me_ref[0], pieces, rels, rows, flat)
    put_matrix(flat, row_of(1, 6), wo, D, D)
    put_matrix(flat, row_of(1, 11), w1, D, FF)
    put_matrix(flat, row_of(1, 13), w2, FF, D)
    vec[...] = jnp.zeros_like(vec)
    for at, number in ((SBO, 7), (SLS1, 8), (SG2, 9), (SB2, 10), (SC2, 14), (SLS2, 15)):
        put_row(flat, row_of(1, number), vec, at, D)
    put_row(flat, row_of(1, 12), c1, 0, FF)


def unpack_feed(me, pieces, rels, rows, count):
    return pl.pallas_call(
        functools.partial(unpack_feed_kernel, rels, rows),
        out_shape=[
            sds((D, D), bf16),
            sds((D, FF), bf16),
            sds((FF, D), bf16),
            sds((16, D), f32),
            sds((1, FF), f32),
        ],
        in_specs=[SM] + [VM] * len(pieces),
        out_specs=[VM] * 5,
        scratch_shapes=[pltpu.VMEM((count * rows, LANES), f32)],
        compiler_params=params(),
        name="unpack_feed",
    )(me, *pieces)


def unpack_class_kernel(rels, rows, me_ref, *refs):
    n = len(rels)
    pieces = refs[:n]
    wq, wkv, wo, w1, w2, vec, c1, total, flat = refs[n:]
    fill_flat(me_ref[0], pieces, rels, rows, flat)
    put_matrix(flat, row_of(2, 2), wq, D, D)
    put_matrix(flat, row_of(2, 4), wkv, D, 2 * D)
    put_matrix(flat, row_of(2, 6), wo, D, D)
    put_matrix(flat, row_of(2, 11), w1, D, FF)
    put_matrix(flat, row_of(2, 13), w2, FF, D)
    vec[...] = jnp.zeros_like(vec)
    for at, number in (
        (CG1, 0), (CB1, 1), (CBQ, 3), (CBV, 5), (CBO, 7), (CLS1, 8), (CG2, 9), (CB2, 10), (CC2, 14), (CLS2, 15),
    ):
        put_row(flat, row_of(2, number), vec, at, D)
    put_row(flat, row_of(2, 12), c1, 0, FF)
    count = jnp.zeros((1, LANES), f32)
    for ref, rel in zip(pieces, rels):
        for k in range(len(rel)):
            count = count + ref[k].astype(f32)[rows : rows + 1, :]
    total[...] = count


def unpack_class(me, pieces, rels, rows, count):
    return pl.pallas_call(
        functools.partial(unpack_class_kernel, rels, rows),
        out_shape=[
            sds((D, D), bf16),
            sds((D, 2 * D), bf16),
            sds((D, D), bf16),
            sds((D, FF), bf16),
            sds((FF, D), bf16),
            sds((16, D), f32),
            sds((1, FF), f32),
            sds((1, LANES), f32),
        ],
        in_specs=[SM] + [VM] * len(pieces),
        out_specs=[VM] * 8,
        scratch_shapes=[pltpu.VMEM((count * rows, LANES), f32)],
        compiler_params=params(),
        name="unpack_class",
    )(me, *pieces)


def const_spec(a):
    return pl.BlockSpec(a.shape, lambda i, nd=len(a.shape): (0,) * nd, pipeline_mode=pl.Buffered(1))


def cost(flops, read):
    return pl.CostEstimate(flops=int(flops), bytes_accessed=int(read), transcendentals=0)


class Steps:
    def __init__(self, ns, nl, padded, large_len):
        self.count = math.gcd(ns, nl)
        self.small, self.large = ns // self.count, nl // self.count
        self.padded, self.large_len = padded, large_len
        self.split = self.small * padded
        self.rows = self.split + self.large * large_len
        self.grid = (self.count,)

    def specs(self, cols):
        index = lambda i: (i, 0, 0)
        return [
            pl.BlockSpec((self.small, self.padded, cols), index),
            pl.BlockSpec((self.large, self.large_len, cols), index),
        ]

    def shapes(self, cols, kind):
        n = self.count
        return [sds((n * self.small, self.padded, cols), kind), sds((n * self.large, self.large_len, cols), kind)]

    def join(self, pair):
        cols = pair[0].shape[-1]
        return jnp.concatenate([ref[...].reshape(-1, cols) for ref in pair], 0)

    def put(self, pair, value):
        cols = value.shape[-1]
        pair[0][...] = value[: self.split].reshape(self.small, self.padded, cols)
        pair[1][...] = value[self.split :].reshape(self.large, self.large_len, cols)


def embed_kernel(steps, valid, ps, plg, patch_w, pos_small, pos_large, wqkv, vec, *outs):
    tok_o, qkv_o, tokens = outs[:2], outs[2:4], outs[4]
    row = lambda at: vec[at : at + 1, :]
    for i in range(steps.small):
        base = steps.padded * i
        tokens[base : base + steps.padded, :] = pos_small[...]
        tokens[base : base + valid, :] += nn(ps[i], patch_w[...])
    for i in range(steps.large):
        base = steps.split + steps.large_len * i
        tokens[base : base + steps.large_len, :] = nn(plg[i], patch_w[...]) + pos_large[...]
    tok = tokens[...]
    steps.put(tok_o, tok)
    unit, _ = stats(tok)
    a1 = (unit * row(SG1) + row(SB1)).astype(bf16)
    bias = jnp.concatenate([row(SBQ), jnp.zeros((1, D), f32), row(SBV)], 1)
    steps.put(qkv_o, (nn(a1, wqkv[...]) + bias).astype(bf16))


def embed(ps, plg, patch_w, pos_small, pos_large, wqkv, vec, padded, after):
    ns, valid, _ = ps.shape
    nl, large_len, _ = plg.shape
    steps = Steps(ns, nl, padded, large_len)
    weights = (patch_w, pos_small, pos_large, wqkv, vec)
    index = lambda i: (i, 0, 0)
    out = call(
        functools.partial(embed_kernel, steps, valid),
        (ps, plg, *weights),
        after,
        grid=steps.grid,
        out_shape=steps.shapes(D, f32) + steps.shapes(3 * D, bf16),
        in_specs=[
            pl.BlockSpec((steps.small, valid, PATCH_IN), index),
            pl.BlockSpec((steps.large, large_len, PATCH_IN), index),
        ]
        + [const_spec(a) for a in weights],
        out_specs=steps.specs(D) + steps.specs(3 * D),
        scratch_shapes=[pltpu.VMEM((steps.rows, D), f32)],
        cost_estimate=cost(12e9, 20e6),
        name="embed",
    )
    return out[:2], out[2:]


def attend_kernel(valid, qkv_ref, pre_col, post_col, att_ref, lse_ref, q_t, kk, v_t, acc):
    per, length = qkv_ref.shape[0], qkv_ref.shape[1]
    for i in range(per):
        q_t[i] = qkv_ref[i, :, 0:D].astype(f32).T
        kk[i, :, 0:D] = qkv_ref[i, :, D : 2 * D]
        kk[i, :, D:] = qkv_ref[i, :, D : 2 * D]
        v_t[i] = qkv_ref[i, :, 2 * D :].astype(f32).T.astype(bf16)
    for g in range(HEADS):
        pre, post = pre_col[:, g : g + 1], post_col[:, g : g + 1]
        for i in range(per):
            high, low = split(q_t[i] * pre)
            mixed = nn(kk[i], jnp.concatenate([high, low], 0))
            if valid < length:
                mixed = jnp.where(lax.broadcasted_iota(jnp.int32, mixed.shape, 0) < valid, mixed, NEG)
            top = jnp.max(mixed, 0, keepdims=True)
            raw = jnp.exp2(mixed - top)
            weight = colsum(raw)
            lse_ref[i, g : g + 1, :] = top + jnp.log2(weight)
            part = nn(v_t[i], raw.astype(bf16)) * post * (1.0 / weight)
            acc[i] = part if g == 0 else acc[i] + part
    for i in range(per):
        att_ref[i] = acc[i].T.astype(bf16)


def attend(qkv, pre_col, post_col, valid, per, flops, after):
    n, length, _ = qkv.shape
    spec = lambda *tail: pl.BlockSpec((per,) + tail, lambda i: (i, 0, 0))
    return call(
        functools.partial(attend_kernel, valid),
        (qkv, pre_col, post_col),
        after,
        grid=(n // per,),
        out_shape=[sds((n, length, D), bf16), sds((n, HEADS, length), f32)],
        in_specs=[spec(length, 3 * D), const_spec(pre_col), const_spec(post_col)],
        out_specs=[spec(length, D), spec(HEADS, length)],
        scratch_shapes=[
            pltpu.VMEM((per, D, length), f32),
            pltpu.VMEM((per, length, 2 * D), bf16),
            pltpu.VMEM((per, D, length), bf16),
            pltpu.VMEM((per, D, length), f32),
        ],
        cost_estimate=cost(flops, 10e6),
        name="attend",
    )


def feed_kernel(steps, tok_s, tok_l, att_s, att_l, wo, w1, w2, vec, c1, *outs):
    branch_o, mid_o, act_o, slope_o, lower_o, out_o = [outs[2 * i : 2 * i + 2] for i in range(6)]
    row = lambda at: vec[at : at + 1, :]
    branch = nn(steps.join((att_s, att_l)), wo[...]) + row(SBO)
    steps.put(branch_o, branch.astype(bf16))
    mid = steps.join((tok_s, tok_l)) + row(SLS1) * branch
    steps.put(mid_o, mid)
    unit, _ = stats(mid)
    n2 = (unit * row(SG2) + row(SB2)).astype(bf16)
    act, slope = gelu_pair(nn(n2, w1[...]) + c1[...])
    act = act.astype(bf16)
    steps.put(act_o, act)
    steps.put(slope_o, slope.astype(bf16))
    lower = nn(act, w2[...]) + row(SC2)
    steps.put(lower_o, lower.astype(bf16))
    steps.put(out_o, mid + row(SLS2) * lower)


FEED_OUT = [(D, bf16), (D, f32), (FF, bf16), (FF, bf16), (D, bf16), (D, f32)]


def feed(tok, att, weights, after):
    (ns, padded, _), (nl, large_len, _) = tok[0].shape, tok[1].shape
    steps = Steps(ns, nl, padded, large_len)
    out = call(
        functools.partial(feed_kernel, steps),
        (*tok, *att, *weights),
        after,
        grid=steps.grid,
        out_shape=[shape for entry in FEED_OUT for shape in steps.shapes(*entry)],
        in_specs=steps.specs(D) * 2 + [const_spec(a) for a in weights],
        out_specs=[spec for cols, _ in FEED_OUT for spec in steps.specs(cols)],
        cost_estimate=cost(20e9, 30e6),
        name="feed",
    )
    return [out[2 * i : 2 * i + 2] for i in range(6)]


BATCH = 8


def class_kernel(
    ns, nl, valid, out_s, out_l, wq, wkv, wo, w1, w2, vec, c1, svec, head_w, head_b, total, counts, labels_s, labels_l,
    d_s, d_l, g_wq, g_wkv, g_wo, g_w1, g_w2, g_vec, g_c1, g_svec, g_head_w, g_head_b, loss_o,
    a_s, a_l, p_s, p_l, z_ref, y_ref, b_ref, ps_ref, pc_ref, da_ref,
):
    row = lambda at: vec[at : at + 1, :]
    mask8 = head_mask(HEADS)
    mask64 = head_mask(HEADS * BATCH)
    cls = svec[1:2, :]
    unit_cls, inv_cls = stats(cls)
    a_cls = (unit_cls * row(CG1) + row(CB1)).astype(bf16)
    a_cls_f = a_cls.astype(f32)
    query = (nn(a_cls, wq[...]) + row(CBQ)).astype(bf16).astype(f32)
    q_diag = jnp.where(mask8, query, 0.0).astype(bf16)
    u_nat = nt(q_diag, wkv[:, 0:D]) * SCALE
    u_hi, u_lo = split(u_nat * LOG2E)
    u16 = jnp.concatenate([u_hi, u_lo], 0)
    s_cls = jnp.sum(u_nat * LOG2E * a_cls_f, -1, keepdims=True)
    z_ref[...] = jnp.zeros_like(z_ref)
    ps_ref[...] = jnp.zeros_like(ps_ref)

    def forward(i, src, a_ref, p_ref, slot):
        unit, _ = stats(src[i])
        a = (unit * row(CG1) + row(CB1)).astype(bf16)
        a_ref[i] = a
        s16 = nt(u16, a)
        s = s16[0:HEADS] + s16[HEADS:]
        keep = valid if a.shape[0] != GRID_LARGE**2 else a.shape[0]
        if keep < a.shape[0]:
            s = jnp.where(lax.broadcasted_iota(jnp.int32, s.shape, 1) < keep, s, NEG)
        top = jnp.maximum(jnp.max(s, -1, keepdims=True), s_cls)
        e = jnp.exp2(s - top)
        e_cls = jnp.exp2(s_cls - top)
        inverse = 1.0 / (jnp.sum(e, -1, keepdims=True) + e_cls)
        p, p_cls = e * inverse, e_cls * inverse
        p_ref[i] = p
        low, low_cls = p.astype(bf16), p_cls.astype(bf16).astype(f32)
        z_ref[pl.ds(slot * HEADS, HEADS), :] = nn(low, a) + low_cls * a_cls_f
        ps_ref[pl.ds(slot * HEADS, HEADS), :] = jnp.sum(low.astype(f32), -1, keepdims=True) + low_cls
        pc_ref[pl.ds(slot * HEADS, HEADS), :] = p_cls

    for i in range(ns):
        forward(i, out_s, a_s, p_s, i)
    for i in range(nl):
        forward(i, out_l, a_l, p_l, ns + i)

    z_hi, z_lo = split(z_ref[...])
    o_all = nn(jnp.concatenate([z_hi, z_lo], 0), wkv[:, D:])
    o_all = o_all[0 : HEADS * BATCH] + o_all[HEADS * BATCH :] + ps_ref[...] * row(CBV)
    att = jnp.sum(jnp.where(mask64, o_all, 0.0).reshape(BATCH, HEADS, D), 1).astype(bf16)
    branch = nn(att, wo[...]) + row(CBO)
    mid = cls + row(CLS1) * branch
    unit_mid, inv_mid = stats(mid)
    n2 = (unit_mid * row(CG2) + row(CB2)).astype(bf16)
    upper = nn(n2, w1[...]) + c1[...]
    act, slope = gelu_pair(upper)
    act = act.astype(bf16)
    lower = nn(act, w2[...]) + row(CC2)
    c_tok = mid + row(CLS2) * lower
    unit_c, inv_c = stats(c_tok)
    final = (unit_c * svec[2:3, :] + svec[3:4, :]).astype(bf16)
    logits = nn(final, head_w[...]) + head_b[...]
    lane = lax.broadcasted_iota(jnp.int32, logits.shape, 1)
    inside = lane < CLASSES
    logits = jnp.where(inside, logits, NEG)
    shifted = logits - jnp.max(logits, -1, keepdims=True)
    raw = jnp.exp(shifted)
    weight = jnp.sum(raw, -1, keepdims=True)
    logp = shifted - jnp.log(weight)
    image = lax.broadcasted_iota(jnp.int32, (BATCH, 1), 0)
    label = jnp.zeros((BATCH, 1), jnp.int32)
    for i in range(ns):
        label = jnp.where(image == i, labels_s[i], label)
    for i in range(nl):
        label = jnp.where(image == ns + i, labels_l[i], label)
    alive = ((image < ns) & (image < counts[0, 0])) | ((image >= ns) & (image - ns < counts[0, 1]))
    hit = lane == label
    picked = jnp.sum(jnp.where(hit, logp, 0.0), -1, keepdims=True)
    mean = jnp.sum(jnp.where(inside, logp, 0.0), -1, keepdims=True) * (1.0 / CLASSES)
    each = -((1.0 - smooth) * picked + smooth * mean)
    scaled = jnp.where(alive, 1.0, 0.0) / total[0:1, 0:1]
    loss_o[...] = jnp.broadcast_to(colsum(scaled * each), loss_o.shape)
    target = jnp.where(hit, 1.0 - smooth, 0.0) + smooth / CLASSES
    d_logits = jnp.where(inside, scaled * (raw / weight - target), 0.0).astype(bf16)

    d_final = nt(d_logits, head_w[...])
    g_head_w[...] = tn(final, d_logits)
    g_head_b[...] = colsum(d_logits.astype(f32))
    g_svec[...] = jnp.zeros_like(g_svec)
    g_svec[2:3, :] = colsum(d_final * unit_c)
    g_svec[3:4, :] = colsum(d_final)
    d_c = norm_back(d_final, unit_c, inv_c, svec[2:3, :])
    g_vec[...] = jnp.zeros_like(g_vec)
    g_vec[CLS2 : CLS2 + 1, :] = colsum(d_c * lower)
    d_lower = (d_c * row(CLS2)).astype(bf16)
    g_vec[CC2 : CC2 + 1, :] = colsum(d_lower.astype(f32))
    g_w2[...] = tn(act, d_lower)
    d_upper = (slope * nt(d_lower, w2[...])).astype(bf16)
    g_c1[...] = colsum(d_upper.astype(f32))
    g_w1[...] = tn(n2, d_upper)
    d_n2 = nt(d_upper, w1[...])
    g_vec[CG2 : CG2 + 1, :] = colsum(d_n2 * unit_mid)
    g_vec[CB2 : CB2 + 1, :] = colsum(d_n2)
    d_mid = d_c + norm_back(d_n2, unit_mid, inv_mid, row(CG2))
    g_vec[CLS1 : CLS1 + 1, :] = colsum(d_mid * branch)
    d_branch = (d_mid * row(CLS1)).astype(bf16)
    g_vec[CBO : CBO + 1, :] = colsum(d_branch.astype(f32))
    g_wo[...] = tn(att, d_branch)
    d_att = nt(d_branch, wo[...]).astype(bf16).astype(f32)
    d_diag = jnp.where(mask64, jnp.broadcast_to(d_att[:, None, :], (BATCH, HEADS, D)).reshape(BATCH * HEADS, D), 0.0)
    g_vec[CBV : CBV + 1, :] = colsum(d_diag * ps_ref[...])
    shift = jnp.sum(d_diag * row(CBV), -1, keepdims=True)
    d_diag_low = d_diag.astype(bf16)
    y_ref[...] = nt(d_diag_low, wkv[:, D:])
    g_wkv[:, D:] = tn(jnp.concatenate([z_hi, z_lo], 0), jnp.concatenate([d_diag_low, d_diag_low], 0))
    z_ref[:, 0:1] = shift
    b_ref[...] = jnp.zeros_like(b_ref)
    da_ref[...] = jnp.zeros_like(da_ref)
    un_hi, un_lo = split(u_nat)

    def backward(i, src, a_ref, p_ref, d_ref, slot):
        unit, inverse = stats(src[i])
        a = a_ref[i]
        here = pl.ds(slot * HEADS, HEADS)
        y = y_ref[here, :]
        y_hi, y_lo = split(y)
        d16 = nt(jnp.concatenate([y_hi, y_lo], 0), a)
        offset = z_ref[here, 0:1]
        d_p = d16[0:HEADS] + d16[HEADS:] + offset
        d_p_cls = jnp.sum(y * a_cls_f, -1, keepdims=True) + offset
        p, p_cls = p_ref[i], pc_ref[here, :]
        delta = jnp.sum(p * d_p, -1, keepdims=True) + p_cls * d_p_cls
        d_score = (p * (d_p - delta)).astype(bf16)
        d_score_cls = (p_cls * (d_p_cls - delta)).astype(bf16).astype(f32)
        low = p.astype(bf16)
        b_ref[...] += nn(d_score, a) + d_score_cls * a_cls_f
        da_ref[...] += d_score_cls * u_nat + p_cls.astype(bf16).astype(f32) * y
        left = jnp.concatenate([d_score.astype(f32), d_score.astype(f32), low.astype(f32), low.astype(f32)], 0)
        d_a = tn(left.astype(bf16), jnp.concatenate([un_hi, un_lo, y_hi, y_lo], 0))
        g_vec[CG1 : CG1 + 1, :] += colsum(d_a * unit)
        g_vec[CB1 : CB1 + 1, :] += colsum(d_a)
        d_ref[i] = norm_back(d_a, unit, inverse, row(CG1))

    for i in range(ns):
        backward(i, out_s, a_s, p_s, d_s, i)
    for i in range(nl):
        backward(i, out_l, a_l, p_l, d_l, ns + i)

    b_hi, b_lo = split(b_ref[...])
    bw = nn(jnp.concatenate([b_hi, b_lo], 0), wkv[:, 0:D])
    bw = bw[0:HEADS] + bw[HEADS:]
    d_query = (colsum(jnp.where(mask8, bw, 0.0)) * SCALE).astype(bf16)
    g_vec[CBQ : CBQ + 1, :] = d_query.astype(f32)
    q_scaled = q_diag.astype(f32) * SCALE
    qs_hi, qs_lo = split(q_scaled)
    g_wkv[:, 0:D] = tn(
        jnp.concatenate([b_hi, b_hi, b_lo, b_lo], 0), jnp.concatenate([qs_hi, qs_lo, qs_hi, qs_lo], 0)
    )
    first = lax.broadcasted_iota(jnp.int32, (16, D), 0) == 0
    spread_a = jnp.where(first, jnp.broadcast_to(a_cls_f, (16, D)), 0.0).astype(bf16)
    spread_q = jnp.where(first, jnp.broadcast_to(d_query.astype(f32), (16, D)), 0.0).astype(bf16)
    g_wq[...] = tn(spread_a, spread_q)
    d_a_cls = colsum(da_ref[...]) + nt(d_query, wq[...])
    g_vec[CG1 : CG1 + 1, :] += d_a_cls * unit_cls
    g_vec[CB1 : CB1 + 1, :] += d_a_cls
    g_svec[1:2, :] = colsum(d_mid) + norm_back(d_a_cls, unit_cls, inv_cls, row(CG1))


def class_block(out_s, out_l, classw, stem, total, counts, labels_s, labels_l, valid):
    ns, padded, _ = out_s.shape
    nl, large_len, _ = out_l.shape
    wq, wkv, wo, w1, w2, vec, c1 = classw
    _, svec, _, _, head_w, head_b = stem
    args = (out_s, out_l, wq, wkv, wo, w1, w2, vec, c1, svec, head_w, head_b, total, counts, labels_s, labels_l)
    return pl.pallas_call(
        functools.partial(class_kernel, ns, nl, valid),
        out_shape=[
            sds((ns, padded, D), f32),
            sds((nl, large_len, D), f32),
            sds((D, D), f32),
            sds((D, 2 * D), f32),
            sds((D, D), f32),
            sds((D, FF), f32),
            sds((FF, D), f32),
            sds((16, D), f32),
            sds((1, FF), f32),
            sds((8, D), f32),
            sds((D, CLASS_PAD), f32),
            sds((1, CLASS_PAD), f32),
            sds((1, LANES), f32),
        ],
        in_specs=[VM] * (len(args) - 3) + [SM] * 3,
        out_specs=[VM] * 13,
        scratch_shapes=[
            pltpu.VMEM((ns, padded, D), bf16),
            pltpu.VMEM((nl, large_len, D), bf16),
            pltpu.VMEM((ns, HEADS, padded), f32),
            pltpu.VMEM((nl, HEADS, large_len), f32),
            pltpu.VMEM((BATCH * HEADS, D), f32),
            pltpu.VMEM((BATCH * HEADS, D), f32),
            pltpu.VMEM((HEADS, D), f32),
            pltpu.VMEM((BATCH * HEADS, 1), f32),
            pltpu.VMEM((BATCH * HEADS, 1), f32),
            pltpu.VMEM((HEADS, D), f32),
        ],
        compiler_params=params(),
        cost_estimate=pl.CostEstimate(flops=10_000_000_000, bytes_accessed=60_000_000, transcendentals=0),
        name="class_block",
    )(*args)


def feed_back_kernel(steps, *refs):
    ins, (wo, w1, w2, vec), refs = [refs[2 * i : 2 * i + 2] for i in range(7)], refs[14:18], refs[18:]
    d_mid_o, d_att_o, sums = refs[:2], refs[2:4], refs[4:]
    g_wo, g_w1, g_w2, g_vec, g_c1 = sums
    row = lambda at: vec[at : at + 1, :]

    @pl.when(pl.program_id(0) == 0)
    def _():
        for ref in sums:
            ref[...] = jnp.zeros_like(ref)

    def add(at, value):
        g_vec[at : at + 1, :] += value

    d_out_r, mid_r, act_r, slope_r, lower_r, branch_r, att_r = ins
    d_out = steps.join(d_out_r)
    add(SLS2, colsum(d_out * steps.join(lower_r).astype(f32)))
    d_lower = (d_out * row(SLS2)).astype(bf16)
    add(SC2, colsum(d_lower.astype(f32)))
    unit, inverse = stats(steps.join(mid_r))
    n2 = (unit * row(SG2) + row(SB2)).astype(bf16)
    g_w2[...] += tn(steps.join(act_r), d_lower)
    d_upper = (nt(d_lower, w2[...]) * steps.join(slope_r).astype(f32)).astype(bf16)
    g_w1[...] += tn(n2, d_upper)
    g_c1[...] += colsum(d_upper.astype(f32))
    d_n2 = nt(d_upper, w1[...])
    add(SG2, colsum(d_n2 * unit))
    add(SB2, colsum(d_n2))
    d_mid = d_out + norm_back(d_n2, unit, inverse, row(SG2))
    steps.put(d_mid_o, d_mid)
    add(SLS1, colsum(d_mid * steps.join(branch_r).astype(f32)))
    d_branch = (d_mid * row(SLS1)).astype(bf16)
    add(SBO, colsum(d_branch.astype(f32)))
    g_wo[...] += tn(steps.join(att_r), d_branch)
    steps.put(d_att_o, nt(d_branch, wo[...]).astype(bf16))


def sum_specs(shapes):
    return [pl.BlockSpec(s.shape, lambda i: (0, 0), pipeline_mode=pl.Buffered(1)) for s in shapes]


def feed_back(pairs, weights, after):
    (ns, padded, _), (nl, large_len, _) = pairs[0][0].shape, pairs[0][1].shape
    steps = Steps(ns, nl, padded, large_len)
    sums = [sds((D, D), f32), sds((D, FF), f32), sds((FF, D), f32), sds((16, D), f32), sds((1, FF), f32)]
    out = call(
        functools.partial(feed_back_kernel, steps),
        (*[a for pair in pairs for a in pair], *weights),
        after,
        grid=steps.grid,
        out_shape=steps.shapes(D, f32) + steps.shapes(D, bf16) + sums,
        in_specs=[spec for pair in pairs for spec in steps.specs(pair[0].shape[2])] + [const_spec(a) for a in weights],
        out_specs=steps.specs(D) * 2 + sum_specs(sums),
        cost_estimate=cost(35e9, 30e6),
        name="feed_back",
    )
    return out[:2], out[2:4], out[4:]


def attend_back_kernel(valid, qkv_ref, d_att_ref, lse_ref, pre_col, post_col, pre_row, post_row, d_qkv_ref, g_pre, g_post,
                       q_t, kk, k_t, do_t, dq_t, d_k, d_v):
    per, length = qkv_ref.shape[0], qkv_ref.shape[1]
    for i in range(per):
        q_t[i] = qkv_ref[i, :, 0:D].astype(f32).T
        kk[i, :, 0:D] = qkv_ref[i, :, D : 2 * D]
        kk[i, :, D:] = qkv_ref[i, :, D : 2 * D]
        k_t[i] = qkv_ref[i, :, D : 2 * D].astype(f32).T.astype(bf16)
        do_t[i] = d_att_ref[i].astype(f32).T

    @pl.when(pl.program_id(0) == 0)
    def _():
        g_pre[...] = jnp.zeros_like(g_pre)
        g_post[...] = jnp.zeros_like(g_post)

    for g in range(HEADS):
        pre, post = pre_col[:, g : g + 1], post_col[:, g : g + 1]
        for i in range(per):
            q, k, v = qkv_ref[i, :, 0:D], qkv_ref[i, :, D : 2 * D], qkv_ref[i, :, 2 * D :]
            high, low = split(q_t[i] * pre)
            mixed = nn(kk[i], jnp.concatenate([high, low], 0))
            d_p = nn(v, (do_t[i] * post).astype(bf16))
            p = jnp.exp2(mixed - lse_ref[i, g : g + 1, :])
            if valid < length:
                p = jnp.where(lax.broadcasted_iota(jnp.int32, p.shape, 0) < valid, p, 0.0)
            delta = colsum(p * d_p)
            d_mixed = (p * (d_p - delta)).astype(bf16)
            r = nn(p.astype(bf16), d_att_ref[i])
            t = nn(d_mixed, q)
            u = nn(k_t[i], d_mixed)
            d_v_part, d_k_part, d_q_part = r * post_row[g : g + 1, :], t * pre_row[g : g + 1, :], u * pre
            d_v[i] = d_v_part if g == 0 else d_v[i] + d_v_part
            d_k[i] = d_k_part if g == 0 else d_k[i] + d_k_part
            dq_t[i] = d_q_part if g == 0 else dq_t[i] + d_q_part
            g_post[g : g + 1, :] += colsum(r * v.astype(f32))
            g_pre[g : g + 1, :] += colsum(t * k.astype(f32))
    inverse = 1.0 / LOG2E
    for i in range(per):
        d_qkv_ref[i, :, 0:D] = (dq_t[i].T * inverse).astype(bf16)
        d_qkv_ref[i, :, D : 2 * D] = (d_k[i] * inverse).astype(bf16)
        d_qkv_ref[i, :, 2 * D :] = d_v[i].astype(bf16)


def attend_back(qkv, d_att, lse, mixes, valid, first, count, per, flops, after):
    length = qkv.shape[1]
    spec = lambda *tail: pl.BlockSpec((per,) + tail, lambda i: (i + first // per, 0, 0))
    sums = [sds((HEADS, D), f32)] * 2
    return call(
        functools.partial(attend_back_kernel, valid),
        (qkv, d_att, lse, *mixes),
        after,
        grid=(count // per,),
        out_shape=[sds((count, length, 3 * D), bf16)] + sums,
        in_specs=[spec(length, 3 * D), spec(length, D), spec(HEADS, length)] + [const_spec(a) for a in mixes],
        out_specs=[pl.BlockSpec((per, length, 3 * D), lambda i: (i, 0, 0))] + sum_specs(sums),
        scratch_shapes=[
            pltpu.VMEM((per, D, length), f32),
            pltpu.VMEM((per, length, 2 * D), bf16),
            pltpu.VMEM((per, D, length), bf16),
            pltpu.VMEM((per, D, length), f32),
            pltpu.VMEM((per, D, length), f32),
            pltpu.VMEM((per, length, D), f32),
            pltpu.VMEM((per, length, D), f32),
        ],
        cost_estimate=cost(flops, 10e6),
        name="attend_back",
    )


def embed_back_kernel(steps, valid, ps, plg, resize, *refs):
    tok_r, dq_s, d_mid_r, refs = refs[:2], refs[2], refs[3:5], refs[5:]
    dq_l, (wqkv, vec), refs = refs[: steps.large * steps.count], refs[steps.large * steps.count :][:2], refs[steps.large * steps.count + 2 :]
    g_wqkv, g_vec, g_patch_w, g_patch_b, g_pos, pos_large, d_qkv = refs
    row = lambda at: vec[at : at + 1, :]
    step = pl.program_id(0)

    @pl.when(step == 0)
    def _():
        for ref in refs[:-1]:
            ref[...] = jnp.zeros_like(ref)

    d_qkv[: steps.split, :] = dq_s[...].reshape(steps.split, 3 * D)
    for k in range(steps.count):

        @pl.when(step == k)
        def _(k=k):
            for i in range(steps.large):
                base = steps.split + steps.large_len * i
                d_qkv[base : base + steps.large_len, :] = dq_l[k * steps.large + i][0]

    def add(at, value):
        g_vec[at : at + 1, :] += value

    add(SBQ, colsum(d_qkv[:, 0:D].astype(f32)))
    add(SBV, colsum(d_qkv[:, 2 * D :].astype(f32)))
    unit, inverse = stats(steps.join(tok_r))
    a1 = (unit * row(SG1) + row(SB1)).astype(bf16)
    g_wqkv[...] += tn(a1, d_qkv[...])
    d_a1 = nt(d_qkv[...], wqkv[...])
    add(SG1, colsum(d_a1 * unit))
    add(SB1, colsum(d_a1))
    d_tok = steps.join(d_mid_r) + norm_back(d_a1, unit, inverse, row(SG1))
    g_patch_b[0:1, :] += colsum(d_tok)
    for i in range(steps.small):
        mine = d_tok[steps.padded * i : steps.padded * i + valid, :]
        g_pos[...] += mine
        g_patch_w[...] += tn(ps[i], mine.astype(bf16))
    for i in range(steps.large):
        base = steps.split + steps.large_len * i
        mine = d_tok[base : base + steps.large_len, :]
        pos_large[...] += mine
        g_patch_w[...] += tn(plg[i], mine.astype(bf16))

    @pl.when(step == steps.count - 1)
    def _():
        g_pos[...] += lax.dot_general(
            resize[...], pos_large[...], (((1,), (0,)), ((), ())),
            preferred_element_type=f32, precision=lax.Precision.HIGHEST,
        )


def embed_back(ps, plg, tok, dq_s, d_mid, dq_l, wqkv, vec, after):
    ns, valid, _ = ps.shape
    nl, large_len, _ = plg.shape
    steps = Steps(ns, nl, tok[0].shape[1], large_len)
    resize = jnp.asarray(resize_table().T.copy())
    sums = [
        sds((D, 3 * D), f32),
        sds((16, D), f32),
        sds((PATCH_IN, D), f32),
        sds((8, D), f32),
        sds((valid, D), f32),
    ]
    index = lambda i: (i, 0, 0)
    return call(
        functools.partial(embed_back_kernel, steps, valid),
        (ps, plg, resize, *tok, dq_s, *d_mid, *dq_l, wqkv, vec),
        after,
        grid=steps.grid,
        out_shape=sums,
        in_specs=[
            pl.BlockSpec((steps.small, valid, PATCH_IN), index),
            pl.BlockSpec((steps.large, large_len, PATCH_IN), index),
            const_spec(resize),
            *steps.specs(D),
            steps.specs(3 * D)[0],
            *steps.specs(D),
        ]
        + [const_spec(a) for a in dq_l]
        + [const_spec(wqkv), const_spec(vec)],
        out_specs=sum_specs(sums),
        scratch_shapes=[pltpu.VMEM((large_len, D), f32), pltpu.VMEM((steps.rows, 3 * D), bf16)],
        cost_estimate=cost(20e9, 30e6),
        name="embed_back",
    )


def take_matrix(flat, row, src, rows, cols):
    step = cols // LANES
    for j in range(step):
        flat[pl.ds(row + j, rows, stride=step), :] = src[0:rows, LANES * j : LANES * (j + 1)]


def take_row(flat, row, src, at, cols):
    for j in range(cols // LANES):
        flat[row + j : row + j + 1, :] = src[at : at + 1, LANES * j : LANES * (j + 1)]


def slots_of(order):
    rels = [0]
    for bit in reversed(order):
        rels = rels + [r | (1 << bit) for r in rels]
    return rels


def emit_slots(me, flat, rows, rels, keep_ref, send_ref, offset=0):
    half = len(rels) // 2
    for k, r in enumerate(rels):
        value = flat[pl.ds(offset + rows * jnp.bitwise_xor(me, r), keep_ref.shape[1]), :]
        if k < half:
            keep_ref[k] = value
        else:
            send_ref[k - half] = value.astype(bf16)


def pack_class_kernel(rels, rows, me_ref, wq, wkv, wo, w1, w2, vec, c1, keep, send, flat):
    used = rows_used(2)
    flat[used:, :] = jnp.zeros((flat.shape[0] - used, LANES), f32)
    take_matrix(flat, row_of(2, 2), wq, D, D)
    take_matrix(flat, row_of(2, 4), wkv, D, 2 * D)
    take_matrix(flat, row_of(2, 6), wo, D, D)
    take_matrix(flat, row_of(2, 11), w1, D, FF)
    take_matrix(flat, row_of(2, 13), w2, FF, D)
    for at, number in (
        (CG1, 0), (CB1, 1), (CBQ, 3), (CBV, 5), (CBO, 7), (CLS1, 8), (CG2, 9), (CB2, 10), (CC2, 14), (CLS2, 15),
    ):
        take_row(flat, row_of(2, number), vec, at, D)
    take_row(flat, row_of(2, 12), c1, 0, FF)
    emit_slots(me_ref[0], flat, rows, rels, keep, send)


def take_head(flat, base, head_w, head_b, tiles, groups):
    for t in range(8):
        tiles[t] = head_w[:, LANES * t : LANES * (t + 1)]
    lane = lax.broadcasted_iota(jnp.int32, (groups, LANES), 1)
    for rho in range(16):
        first, shift = (CLASSES * rho) // LANES, (CLASSES * rho) % LANES
        parts = [tiles[t, pl.ds(rho, groups, stride=16), :] for t in range(8)]
        if shift:
            parts = [pltpu.roll(p, shift, 1) for p in parts]
        for t in range(9 if shift + CLASSES > CLASS_PAD else 8):
            if shift:
                value = jnp.where(lane >= shift, parts[t] if t < 8 else 0.0, parts[t - 1] if t > 0 else 0.0)
            else:
                value = parts[t]
            here = pl.ds(base + first + t, groups, stride=125)
            flat[here, :] = flat[here, :] + value
    if head_b is not None:
        take_row(flat, base + row_of(0, 7) - row_of(0, 6), head_b, 0, CLASS_PAD)


HEAD_GROUPS = D // 16


def pack_feed_kernel(rels, rows, offset, quarter_rows, me_ref, wo, w1, w2, vec, c1, head_w, head_b, keep, send, flat, tiles):
    used, first = rows_used(1), row_of(1, 6)
    flat[0 : offset + first, :] = jnp.zeros((offset + first, LANES), f32)
    flat[offset + used :, :] = jnp.zeros((flat.shape[0] - used - offset, LANES), f32)
    take_head(flat, offset + row_of(0, 6) - quarter_rows, head_w, head_b, tiles, HEAD_GROUPS)
    boundary = quarter_rows - first
    flat[offset + first : offset + quarter_rows, :] = jnp.zeros((boundary, LANES), f32)
    take_matrix(flat, offset + first, wo, D, D)
    flat[offset + first : offset + quarter_rows, :] = jnp.zeros((boundary, LANES), f32)
    take_matrix(flat, offset + row_of(1, 11), w1, D, FF)
    take_matrix(flat, offset + row_of(1, 13), w2, FF, D)
    for at, number in ((SBO, 7), (SLS1, 8), (SG2, 9), (SB2, 10), (SC2, 14), (SLS2, 15)):
        take_row(flat, offset + row_of(1, number), vec, at, D)
    take_row(flat, offset + row_of(1, 12), c1, 0, FF)
    emit_slots(me_ref[0], flat, rows, rels, keep, send, offset)


def pack_late_kernel(
    rels, rows, quarter_rows, me_ref, wqkv, vec, pre, post, wo, patch_w, patch_b, pos, svec, head_w, keep, send, flat, tiles
):
    padded_rows = keep.shape[1] // 2
    for g in range(2):
        pack_late_group(g, quarter_rows, wqkv, vec, pre, post, wo, patch_w, patch_b, pos, svec, head_w, flat, tiles)
        here = pl.ds(g * padded_rows, padded_rows)
        emit_slots(me_ref[0], flat, rows, rels, keep.at[:, here], send.at[:, here])


def pack_late_group(g, quarter_rows, wqkv, vec, pre, post, wo, patch_w, patch_b, pos, svec, head_w, flat, tiles):
    if g == 0:
        first = row_of(0, 6)
        flat[first:, :] = jnp.zeros((flat.shape[0] - first, LANES), f32)
        take_matrix(flat, row_of(0, 0), patch_w, PATCH_IN, D)
        take_row(flat, row_of(0, 1), patch_b, 0, D)
        take_matrix(flat, row_of(0, 2), pos, GRID_SMALL**2, D)
        for at, number in ((1, 3), (2, 4), (3, 5)):
            take_row(flat, row_of(0, number), svec, at, D)
        take_head(flat, first, head_w, None, tiles, 8)
        return
    first = row_of(1, 6)
    take_matrix(flat, row_of(1, 2), wqkv, D, 3 * D)
    take_matrix(flat, first, wo, 24, D)
    bq = row_of(1, 3)
    for at, row in ((SG1, row_of(1, 0)), (SB1, row_of(1, 1)), (SBQ, bq), (SBV, bq + D // LANES)):
        take_row(flat, row, vec, at, D)
    table_col = lax.broadcasted_iota(jnp.int32, (D, LANES), 0) // WIDTH
    table_lane = lax.broadcasted_iota(jnp.int32, (D, LANES), 1)
    lane = lax.broadcasted_iota(jnp.int32, (HEADS, LANES), 1)
    row = lax.broadcasted_iota(jnp.int32, (HEADS, LANES), 0)
    exact = lambda a, b: lax.dot_general(
        a, b, (((1,), (0,)), ((), ())), preferred_element_type=f32, precision=lax.Precision.HIGHEST
    )
    sum_pre = exact(pre[...], jnp.where(table_lane % HEADS == table_col, 1.0, 0.0))
    sum_post = exact(post[...], jnp.where((table_lane - 64) // HEADS == table_col, 1.0, 0.0))
    line = colsum(jnp.where((lane < 64) & (lane // HEADS == row), sum_pre * SCALE, 0.0))
    line = line + colsum(jnp.where((lane >= 64) & (lane % HEADS == row), sum_post, 0.0))
    flat[row_of(1, 4) : row_of(1, 4) + 1, :] = line


def pack(kernel, name, me, arrays, rels, padded_rows, flat_rows, extra=()):
    half = len(rels) // 2
    return pl.pallas_call(
        kernel,
        out_shape=[sds((half, padded_rows, LANES), f32), sds((half, padded_rows, LANES), bf16)],
        in_specs=[SM] + [VM] * len(arrays),
        out_specs=[VM] * 2,
        scratch_shapes=[pltpu.VMEM((flat_rows, LANES), f32), *extra],
        compiler_params=params(),
        name=name,
    )(me, *arrays)


class Chain:
    def __init__(self, keep, send, order, z_bits, z_last=False):
        self.keep, self.send, self.order, self.z_bits, self.z_last = keep, send, list(order), z_bits, z_last
        self.total = None
        self.done = False

    def finish(self, total):
        self.total = self.send = total
        self.done = True

    def step(self, after=None):
        if self.order:
            (got,) = tied((exchange(self.send, self.order.pop(0), self.z_bits),), after)
            total = self.keep + got.astype(f32)
            if self.order:
                half = total.shape[0] // 2
                self.keep, self.send = total[:half], total[half:].astype(bf16)
            elif self.z_last:
                self.keep, self.send = total[0], total[1:].astype(bf16)
            else:
                self.finish(total[0])
        elif not self.done:
            got = [exchange_z(self.send[k - 1], k) for k in range(1, self.send.shape[0] + 1)]
            total = self.keep
            for part in tied(tuple(got), after):
                total = total + part.astype(f32)
            self.finish(total)


def bounds_table():
    table = np.zeros((8, LANES), np.int32)
    table[0:3, :SEGMENTS] = STARTS // 64
    table[3:6, :SEGMENTS] = -(-ENDS // 64)
    return table


def pick(group, values):
    return jnp.where(group == 0, values[0], jnp.where(group == 1, values[1], values[2]))


def segment_sums(square, group, first_row, bounds):
    rows = square.shape[0]
    lane = lax.broadcasted_iota(jnp.int32, (rows, LANES), 1)
    left = jnp.sum(jnp.where(lane < 64, square, 0.0), -1, keepdims=True)
    right = jnp.sum(jnp.where(lane < 64, 0.0, square), -1, keepdims=True)
    place = 2 * (first_row + lax.broadcasted_iota(jnp.int32, (rows, LANES), 0))
    low, high = bounds[group : group + 1, :], bounds[3 + group : 4 + group, :]
    one = jnp.where((place >= low) & (place < high), left, 0.0)
    two = jnp.where((place + 1 >= low) & (place + 1 < high), right, 0.0)
    return colsum(one + two)


def adam_kernel(rows, me_ref, step_ref, bounds, master, first, second, g0, g1, g2, grad_o, first_o, second_o, update_o, sums_o):
    shard = rows * LANES
    for g, ref in enumerate((g0, g1, g2)):
        grad_o[g : g + 1, :] = ref[0:rows, :].reshape(1, shard)
    grad = grad_o[...]
    weight = master[...]
    new_first = beta_one * first[...] + (1.0 - beta_one) * grad
    new_second = beta_two * second[...] + (1.0 - beta_two) * grad * grad
    first_o[...] = new_first
    second_o[...] = new_second
    power = jnp.full((1, LANES), step_ref[0], jnp.int32).astype(f32)
    scale_one = (1.0 / (1.0 - jnp.power(f32(beta_one), power)))[:, 0:1]
    scale_two = (1.0 / (1.0 - jnp.power(f32(beta_two), power)))[:, 0:1]
    update = new_first * scale_one / (jnp.sqrt(new_second * scale_two) + adam_eps) + decay_rate * weight
    update_o[...] = update
    sums_o[...] = jnp.zeros_like(sums_o)
    first_row = me_ref[0] * rows
    for g in range(3):
        part = update_o[g : g + 1, :].reshape(rows, LANES)
        sums_o[3 + g : 4 + g, :] = segment_sums(part * part, g, first_row, bounds)


def adam(me, step, master, first, second, grads, rows):
    shape = master.shape
    return pl.pallas_call(
        functools.partial(adam_kernel, rows),
        out_shape=[sds(shape, f32)] * 4 + [sds((8, LANES), f32)],
        in_specs=[SM, SM] + [VM] * 7,
        out_specs=[VM] * 5,
        compiler_params=params(),
        name="adam",
    )(me, step, jnp.asarray(bounds_table()), master, first, second, *grads)


def apply_kernel(me_ref, sums, master, update, new_o, weight_o, norm_o, trust_o):
    shard = master.shape[1]
    roots = jnp.sqrt(sums[...])
    weight_norms, update_norms = roots[0:3, :], roots[3:6, :]
    lane = lax.broadcasted_iota(jnp.int32, (3, LANES), 1)
    group3 = lax.broadcasted_iota(jnp.int32, (3, LANES), 0)
    used = pick(group3, [int(REAL[g].sum()) for g in range(3)])
    trust = jnp.where(lane < used, weight_norms / (update_norms + norm_eps), 1.0)
    weight_o[...] = weight_norms[:, 0:SEGMENTS]
    norm_o[...] = update_norms[:, 0:SEGMENTS]
    trust_o[...] = trust[:, 0:SEGMENTS]
    position = me_ref[0] * shard + lax.broadcasted_iota(jnp.int32, (3, shard), 1)
    group = lax.broadcasted_iota(jnp.int32, (3, 1), 0)
    ratio = jnp.broadcast_to(trust[:, 0:1], (3, shard))
    for s in range(1, SEGMENTS):
        low = pick(group, [int(STARTS[g, s]) if REAL[g, s] > 0 else 2**30 for g in range(3)])
        ratio = jnp.where(position >= low, trust[:, s : s + 1], ratio)
    new_o[...] = master[...] - learn_rate * ratio * update[...]


def apply_update(me, sums, master, update):
    return pl.pallas_call(
        apply_kernel,
        out_shape=[sds(master.shape, f32)] + [sds((3, SEGMENTS), f32)] * 3,
        in_specs=[SM] + [VM] * 3,
        out_specs=[VM] * 4,
        compiler_params=params(),
        name="apply_update",
    )(me, sums, master, update)


def round_kernel(rows, counts, master, stem, selfb, classb):
    for g, ref in enumerate((stem, selfb, classb)):
        ref[0, 0:rows, :] = master[g : g + 1, :].reshape(rows, LANES).astype(bf16)
        tail = ref.shape[1] - rows
        count = counts[0, 0] + counts[0, 1] if g == 2 else 0
        ref[0, rows:, :] = jnp.full((tail, LANES), count, jnp.int32).astype(f32).astype(bf16)


def round_shards(counts, master, rows, padded_rows):
    return pl.pallas_call(
        functools.partial(round_kernel, rows),
        out_shape=[sds((1, padded_rows, LANES), bf16)] * 3,
        in_specs=[SM, VM],
        out_specs=[VM] * 3,
        compiler_params=params(),
        name="round_shards",
    )(counts, master)


def weight_kernel(rows, me_ref, bounds, master, sums_o):
    sums_o[...] = jnp.zeros_like(sums_o)
    for g in range(3):
        part = master[g : g + 1, :].reshape(rows, LANES)
        sums_o[g : g + 1, :] = segment_sums(part * part, g, me_ref[0] * rows, bounds)


def weight_sums(me, master, rows):
    return pl.pallas_call(
        functools.partial(weight_kernel, rows),
        out_shape=sds((8, LANES), f32),
        in_specs=[SM, VM, VM],
        out_specs=VM,
        compiler_params=params(),
        name="weight_sums",
    )(me, jnp.asarray(bounds_table()), master)


def on_device(
    master,
    first_moment,
    second_moment,
    patches_small,
    patches_large,
    labels_small,
    labels_large,
    counts,
    step,
):
    rows = master.shape[1] // LANES
    padded_rows = -(-(rows + 1) // 8) * 8
    n_dp, n_z = lax.axis_size("dp"), lax.axis_size("fsdp")
    z_bits, bits = log2(n_z), log2(n_dp) + log2(n_z)
    devices = n_dp * n_z
    half, quarter = devices // 2, devices // 4
    assert row_of(0, 7) + CLASS_PAD // LANES <= half * rows
    assert row_of(1, 6) <= quarter * rows <= row_of(1, 6) + 64
    ns, valid, _ = patches_small.shape
    nl = patches_large.shape[0]
    padded = -(-valid // 16) * 16
    small_per = 2 if ns % 2 == 0 else 1
    me = lax.axis_index(AXES).astype(jnp.int32).reshape(1)
    me_half = jnp.bitwise_and(me, half - 1)
    me_quarter = jnp.bitwise_and(me, quarter - 1)
    dp = lax.axis_index("dp")
    n_quarter = n_dp // 4
    in_half, quarter_id = dp < n_dp // 2, dp // n_quarter

    core, second, top = z_bits, bits - 2, bits - 1
    inner = list(range(core + 1, second))
    arrays = lambda state: ([a for a, _ in state], [r for _, r in state])

    old_sums = weight_sums(me, master, rows)
    stem_shard, self_shard, class_shard = round_shards(counts, master, rows, padded_rows)
    up = n_dp // 2
    got = lax.ppermute(stem_shard, "dp", [(i, i + up) for i in range(up)])
    others = [lax.ppermute(self_shard, "dp", [(i, i ^ (a * n_quarter)) for i in range(n_dp)]) for a in (1, 2, 3)]
    stem_state = gather_z(jnp.where(in_half, stem_shard, got), [0])

    def of_quarter(b):
        value = self_shard
        for a in (1, 2, 3):
            value = jnp.where(quarter_id == (a ^ b), others[a - 1], value)
        return value

    first_state = gather_z(of_quarter(0), [0])
    rest = jnp.concatenate([of_quarter(b) for b in (1, 2, 3)], 0)
    for bit in inner:
        first_state = gather_bit(first_state, bit, z_bits)
    for bit in [*inner, second]:
        stem_state = gather_bit(stem_state, bit, z_bits)
    rest, class_shard, _ = lax.optimization_barrier((rest, class_shard, first_state[0][0]))
    first_state = gather_bit(first_state, core, z_bits)
    stem_state = gather_bit(stem_state, core, z_bits)
    class_all = lax.all_gather(class_shard[0], AXES, axis=0, tiled=False)

    patch_w, svec, pos_small, pos_large, head_w, head_b = stem = unpack_stem(
        me_half, *arrays(stem_state), rows, half, padded
    )
    wqkv, vec, pre_col, post_col, pre_row, post_row = unpack_low(me_quarter, *arrays(first_state), rows, quarter)
    tok, (qkv_s, qkv_l) = embed(
        patches_small, patches_large, patch_w, pos_small, pos_large, wqkv, vec, padded, [old_sums]
    )
    att_s, lse_s = attend(qkv_s, pre_col, post_col, valid, small_per, 20e9, [])
    rest_state = gather_z(rest, [quarter, 2 * quarter, 3 * quarter], att_s)
    rest_all = rest_state[0][0]
    for bit in [*inner, core]:
        rest_state = gather_bit(rest_state, bit, z_bits)
    att_l, lse_l = attend(qkv_l, pre_col, post_col, qkv_l.shape[1], 1, 30e9, [rest_all, att_s])
    wo, w1, w2, vec_feed, c1 = unpack_feed(me_quarter, *arrays(first_state + rest_state), rows, devices)
    att = (att_s, att_l)
    branch, mid, act, slope, lower, out = feed(tok, att, (wo, w1, w2, vec_feed, c1), [])
    *classw, total = unpack_class(jnp.zeros_like(me), [class_all], [list(range(devices))], rows, devices)

    d_out_s, d_out_l, *class_grads, g_svec, g_head_w, g_head_b, loss = class_block(
        *out, classw, stem, total, counts, labels_small, labels_large, valid
    )

    z_order = list(range(z_bits - 1, -1, -1))
    near_far = list(range(z_bits))
    class_order = [core, top, second] + inner + near_far
    feed_order = [core] + near_far + [top, second] + inner
    class_rels, feed_rels = slots_of(class_order), slots_of(feed_order)
    tail = 8 * (padded_rows // 8 - rows // 8)

    class_chain = Chain(
        *pack(
            functools.partial(pack_class_kernel, class_rels, rows), "pack_class", me, class_grads, class_rels,
            padded_rows, devices * rows + tail,
        ),
        class_order, z_bits,
    )
    d_mid, (d_att_s, d_att_l), (g_wo, g_w1, g_w2, g_vec_feed, g_c1) = feed_back(
        ((d_out_s, d_out_l), mid, act, slope, lower, branch, att), (wo, w1, w2, vec_feed), [class_chain.send]
    )
    class_chain.step(d_att_s)
    quarter_rows = quarter * rows
    offset = -(-max(0, quarter_rows - row_of(0, 6)) // 8) * 8
    tiles = [pltpu.VMEM((8, D, LANES), f32)]
    feed_chain = Chain(
        *pack(
            functools.partial(pack_feed_kernel, feed_rels, rows, offset, quarter_rows), "pack_feed", me,
            (g_wo, g_w1, g_w2, g_vec_feed, g_c1, g_head_w, g_head_b), feed_rels, padded_rows,
            offset + devices * rows + tail, tiles,
        ),
        feed_order, z_bits,
    )
    chains = (class_chain, feed_chain)
    mixes = (pre_col, post_col, pre_row, post_row)
    dq_s, pre_sum, post_sum = attend_back(
        qkv_s, d_att_s, lse_s, mixes, valid, 0, ns, small_per, 25e9, [chain.send for chain in chains]
    )
    part, dq_l = dq_s, []
    for i in range(nl):
        for chain in chains:
            chain.step(part)
        wait = [part] + [chain.send for chain in chains]
        part, pre_l, post_l = attend_back(qkv_l, d_att_l, lse_l, mixes, qkv_l.shape[1], i, 1, 1, 25e9, wait)
        dq_l.append(part)
        pre_sum, post_sum = pre_sum + pre_l, post_sum + post_l
    for chain in chains:
        chain.step(part)
    g_wqkv, g_vec, g_patch_w, g_patch_b, g_pos = embed_back(
        patches_small, patches_large, tok, dq_s, d_mid, dq_l, wqkv, vec,
        [chain.send for chain in chains],
    )
    for chain in chains:
        while not chain.done:
            chain.step(g_vec)

    late_rels = slots_of([core] + inner + z_order)
    late_chain = Chain(
        *pack(
            functools.partial(pack_late_kernel, late_rels, rows, quarter_rows), "pack_late", me_quarter,
            (g_wqkv, g_vec, pre_sum, post_sum, g_wo, g_patch_w, g_patch_b, g_pos, g_svec, g_head_w), late_rels,
            2 * padded_rows, row_of(0, 6) + 1024, tiles,
        ),
        [core] + inner, z_bits, True,
    )
    while not late_chain.done:
        late_chain.step()
    part = late_chain.total
    send = part.astype(bf16)
    for a in (1, 2, 3):
        got = lax.ppermute(send, "dp", [(i + a * n_quarter, i) for i in range(n_quarter)])
        part = part + got.astype(f32)
    head_part = lax.ppermute(feed_chain.total, "dp", [(i, i + n_quarter) for i in range(n_quarter)])
    first = quarter_id == 0
    grad_stem = jnp.where(first, part[:padded_rows], head_part)
    grad_self = jnp.where(first, part[padded_rows:], feed_chain.total)

    gradients, new_first, new_second, update, sums = adam(
        me, step, master, first_moment, second_moment, (grad_stem, grad_self, class_chain.total), rows
    )
    line = lax.broadcasted_iota(jnp.int32, (8, 1), 0)
    sums = sums + old_sums + jnp.where(line == 6, loss, 0.0)
    for bit in range(bits):
        sums = sums + exchange(sums, bit, z_bits)
    new_master, weight_norms, update_norms, trust_ratios = apply_update(me, sums, master, update)
    return sums[6, 0], gradients, new_first, new_second, new_master, weight_norms, update_norms, trust_ratios


def solution(mesh):
    return jax.shard_map(
        on_device,
        mesh=mesh,
        in_specs=(
            P(None, AXES),
            P(None, AXES),
            P(None, AXES),
            P(AXES, None, None),
            P(AXES, None, None),
            P(AXES),
            P(AXES),
            P(AXES, None),
            P(),
        ),
        out_specs=(
            P(),
            P(None, AXES),
            P(None, AXES),
            P(None, AXES),
            P(None, AXES),
            P(),
            P(),
            P(),
        ),
        check_vma=False,
    )
```

```python
import functools
import math

import jax
import jax.numpy as jnp
import numpy as np
from jax import lax
from jax.experimental import pallas as pl
from jax.experimental.pallas import tpu as pltpu
from jax.sharding import PartitionSpec as P

D = 384
HEADS = 8
WIDTH = D // HEADS
FF = 1536
CLASSES = 1000
CLASS_PAD = 1024
PATCH_IN = 768
GRID_SMALL = 14
GRID_LARGE = 24
LANES = 128
SEGMENTS = 16

LOG2E = 1.4426950408889634
SCALE = WIDTH**-0.5
NEG = -1e30
smooth = 0.1
beta_one = 0.9
beta_two = 0.999
adam_eps = 1e-06
decay_rate = 0.01
learn_rate = 0.3
norm_eps = 1e-06

f32 = jnp.float32
bf16 = jnp.bfloat16
AXES = ("dp", "fsdp")
VMEM_BYTES = 60 << 20


def shapes_of():
    dim = D
    tail = [(dim,), (dim,), (dim, FF), (FF,), (FF, dim), (dim,), (dim,)]
    stem = [
        (PATCH_IN, dim),
        (dim,),
        (GRID_SMALL * GRID_SMALL, dim),
        (dim,),
        (dim,),
        (dim,),
        (dim, CLASSES),
        (CLASSES,),
    ]
    selfb = [
        (dim,),
        (dim,),
        (dim, 3 * dim),
        (2 * dim,),
        (HEADS, HEADS),
        (HEADS, HEADS),
        (dim, dim),
        (dim,),
        (dim,),
    ] + tail
    classb = [
        (dim,),
        (dim,),
        (dim, dim),
        (dim,),
        (dim, 2 * dim),
        (dim,),
        (dim, dim),
        (dim,),
        (dim,),
    ] + tail
    return [stem, selfb, classb]


def segment_bounds():
    starts = np.zeros((3, SEGMENTS), np.int32)
    ends = np.zeros((3, SEGMENTS), np.int32)
    real = np.zeros((3, SEGMENTS), np.float32)
    for group, shapes in enumerate(shapes_of()):
        offset = 0
        for number, shape in enumerate(shapes):
            count = int(np.prod(shape))
            starts[group, number] = offset
            ends[group, number] = offset + count
            real[group, number] = 1.0
            offset += count
    return starts, ends, real


STARTS, ENDS, REAL = segment_bounds()


def row_of(group, number):
    return int(STARTS[group, number]) // LANES


def rows_used(group):
    return -(-int(ENDS[group].max()) // LANES)


def resize_table():
    rows = np.arange(GRID_LARGE).astype(np.float32) * np.float32((GRID_SMALL - 1) / (GRID_LARGE - 1))
    cols = np.arange(GRID_SMALL).astype(np.float32)
    line = np.maximum(np.float32(0.0), np.float32(1.0) - np.abs(rows[:, None] - cols[None, :]))
    return (line[:, None, :, None] * line[None, :, None, :]).reshape(GRID_LARGE**2, GRID_SMALL**2)


def nn(a, b):
    return lax.dot_general(a, b, (((1,), (0,)), ((), ())), preferred_element_type=f32)


def nt(a, b):
    return lax.dot_general(a, b, (((1,), (1,)), ((), ())), preferred_element_type=f32)


def tn(a, b):
    return lax.dot_general(a, b, (((0,), (0,)), ((), ())), preferred_element_type=f32)


def colsum(value):
    return jnp.sum(value, 0, keepdims=True)


def split(value):
    high = value.astype(bf16)
    return high, (value - high.astype(f32)).astype(bf16)


def stats(value):
    centred = value - jnp.mean(value, -1, keepdims=True)
    inverse = lax.rsqrt(jnp.mean(centred * centred, -1, keepdims=True) + 1e-06)
    return centred * inverse, inverse


def norm_back(d_out, unit, inverse, gain):
    inner = d_out * gain
    first = jnp.mean(inner, -1, keepdims=True)
    second = jnp.mean(inner * unit, -1, keepdims=True)
    return inverse * (inner - first - unit * second)


def gelu_pair(upper):
    cdf = 0.5 * (1.0 + lax.erf(upper * (0.5**0.5)))
    density = jnp.exp(-0.5 * upper * upper) * 0.3989422804014327
    return upper * cdf, cdf + upper * density


def head_mask(rows):
    lane = lax.broadcasted_iota(jnp.int32, (rows, D), 1)
    row = lax.broadcasted_iota(jnp.int32, (rows, D), 0)
    return (lane // WIDTH) == lax.rem(row, HEADS)


VM = pl.BlockSpec(memory_space=pltpu.VMEM)
SM = pl.BlockSpec(memory_space=pltpu.SMEM)


def params(**kw):
    return pltpu.CompilerParams(vmem_limit_bytes=VMEM_BYTES, **kw)


def sds(shape, dtype):
    return jax.ShapeDtypeStruct(shape, dtype)


def call(kernel, args, after, in_specs, **kw):
    n, m = len(args), len(after)

    def wrapped(*refs):
        kernel(*refs[:n], *refs[n + m :])

    specs = list(in_specs) + [pl.BlockSpec(memory_space=pl.ANY)] * m
    return pl.pallas_call(wrapped, in_specs=specs, compiler_params=params(), **kw)(*args, *after)


def log2(n):
    return n.bit_length() - 1


def exchange(value, bit, z_bits):
    if bit < z_bits:
        n = lax.axis_size("fsdp")
        return lax.ppermute(value, "fsdp", [(i, i ^ (1 << bit)) for i in range(n)])
    n = lax.axis_size("dp")
    return lax.ppermute(value, "dp", [(i, i ^ (1 << (bit - z_bits))) for i in range(n)])


def exchange_z(value, k):
    n = lax.axis_size("fsdp")
    return lax.ppermute(value, "fsdp", [(i, i ^ k) for i in range(n)])


def tied(values, after):
    if after is None:
        return values
    return lax.optimization_barrier((*values, after))[:-1]


def gather_z(value, rel, after=None):
    n = lax.axis_size("fsdp")
    got = tied([exchange_z(value, k) for k in range(1, n)], after)
    return [(jnp.concatenate([value, *got], 0), [r | k for k in range(n) for r in rel])]


def gather_bit(state, bit, z_bits, after=None):
    got = tied([exchange(a, bit, z_bits) for a, _ in state], after)
    return state + [(a, [r | (1 << bit) for r in rel]) for a, (_, rel) in zip(got, state)]


def put_matrix(flat, row, out_ref, rows, cols):
    step = cols // LANES
    for j in range(step):
        out_ref[:, LANES * j : LANES * (j + 1)] = flat[pl.ds(row + j, rows, stride=step), :].astype(bf16)


def put_row(flat, row, out_ref, at, cols):
    for j in range(cols // LANES):
        out_ref[at : at + 1, LANES * j : LANES * (j + 1)] = flat[row + j : row + j + 1, :]


def fill_flat(me, piece_refs, rels, rows, flat):
    for ref, rel in zip(piece_refs, rels):
        for k, r in enumerate(rel):
            flat[pl.ds(rows * jnp.bitwise_xor(me, r), rows), :] = ref[k].astype(f32)[0:rows]


def unpack_stem_kernel(rels, rows, me_ref, resize_ref, *refs):
    n = len(rels)
    pieces, (patch_w, vec, pos_small, pos_large, head_w, head_b), (flat, tiles) = refs[:n], refs[n : n + 6], refs[n + 6 :]
    fill_flat(me_ref[0], pieces, rels, rows, flat)
    put_matrix(flat, row_of(0, 0), patch_w, PATCH_IN, D)
    vec[...] = jnp.zeros_like(vec)
    for at, number in enumerate((1, 3, 4, 5)):
        put_row(flat, row_of(0, number), vec, at, D)
    bias = vec[0:1, :]
    small = GRID_SMALL**2
    pos_small[...] = jnp.zeros_like(pos_small)
    for j in range(D // LANES):
        pos_small[0:small, LANES * j : LANES * (j + 1)] = flat[pl.ds(row_of(0, 2) + j, small, stride=D // LANES), :]
    pos_large[...] = (
        lax.dot_general(
            resize_ref[...], pos_small[...], (((1,), (0,)), ((), ())),
            preferred_element_type=f32, precision=lax.Precision.HIGHEST,
        )
        + bias
    )
    pos_small[...] += bias
    lane = lax.broadcasted_iota(jnp.int32, (24, LANES), 1)
    base = row_of(0, 6)
    for rho in range(16):
        first, shift = (CLASSES * rho) // LANES, (CLASSES * rho) % LANES
        parts = [flat[pl.ds(base + first + t, 24, stride=125), :] for t in range(9)]
        if shift:
            parts = [pltpu.roll(p, LANES - shift, 1) for p in parts]
        for t in range(8):
            value = jnp.where(lane < LANES - shift, parts[t], parts[t + 1]) if shift else parts[t]
            if t == 7:
                value = jnp.where(lane < CLASSES - 7 * LANES, value, 0.0)
            tiles[t, pl.ds(rho, 24, stride=16), :] = value
    for t in range(8):
        head_w[:, LANES * t : LANES * (t + 1)] = tiles[t, 0:D, :].astype(bf16)
    put_row(flat, row_of(0, 7), head_b, 0, CLASS_PAD)


def unpack_stem(me, pieces, rels, rows, count, padded):
    resize = np.zeros((GRID_LARGE**2, padded), np.float32)
    resize[:, : GRID_SMALL**2] = resize_table()
    return pl.pallas_call(
        functools.partial(unpack_stem_kernel, rels, rows),
        out_shape=[
            sds((PATCH_IN, D), bf16),
            sds((8, D), f32),
            sds((padded, D), f32),
            sds((GRID_LARGE**2, D), f32),
            sds((D, CLASS_PAD), bf16),
            sds((1, CLASS_PAD), f32),
        ],
        in_specs=[SM] + [VM] * (1 + len(pieces)),
        out_specs=[VM] * 6,
        scratch_shapes=[pltpu.VMEM((count * rows, LANES), f32), pltpu.VMEM((8, D + 16, LANES), f32)],
        compiler_params=params(),
        name="unpack_stem",
    )(me, jnp.asarray(resize), *pieces)


SG1, SB1, SBQ, SBV, SBO, SLS1, SG2, SB2, SC2, SLS2 = range(10)
CG1, CB1, CBQ, CBV, CBO, CLS1, CG2, CB2, CC2, CLS2 = range(10)


def unpack_low_kernel(rels, rows, me_ref, *refs):
    n = len(rels)
    pieces = refs[:n]
    wqkv, vec, pre_col, post_col, pre_row, post_row, flat = refs[n:]
    fill_flat(me_ref[0], pieces, rels, rows, flat)
    put_matrix(flat, row_of(1, 2), wqkv, D, 3 * D)
    vec[...] = jnp.zeros_like(vec)
    bq = row_of(1, 3)
    for at, row in ((SG1, row_of(1, 0)), (SB1, row_of(1, 1)), (SBQ, bq), (SBV, bq + D // LANES)):
        put_row(flat, row, vec, at, D)
    mix = jnp.broadcast_to(flat[row_of(1, 4) : row_of(1, 4) + 1, :], (HEADS, LANES))
    lane = lax.broadcasted_iota(jnp.int32, (HEADS, LANES), 1)
    row = lax.broadcasted_iota(jnp.int32, (HEADS, LANES), 0)
    pick_pre = jnp.where((lane < 64) & (lane // HEADS == row), mix, 0.0).astype(bf16)
    pick_post = jnp.where((lane >= 64) & (lane % HEADS == row), mix, 0.0).astype(bf16)
    table_lane = lax.broadcasted_iota(jnp.int32, (LANES, D), 0)
    table_col = lax.broadcasted_iota(jnp.int32, (LANES, D), 1) // WIDTH
    spread_pre = jnp.where(table_lane % HEADS == table_col, 1.0, 0.0).astype(bf16)
    spread_post = jnp.where((table_lane - 64) // HEADS == table_col, 1.0, 0.0).astype(bf16)
    factor = SCALE * LOG2E
    pre_row[...] = nn(pick_pre, spread_pre) * factor
    post_row[...] = nn(pick_post, spread_post)
    column = lambda a, b: lax.dot_general(a, b, (((0,), (1,)), ((), ())), preferred_element_type=f32)
    pre_col[...] = column(spread_pre, pick_pre) * factor
    post_col[...] = column(spread_post, pick_post)


def unpack_low(me, pieces, rels, rows, count):
    return pl.pallas_call(
        functools.partial(unpack_low_kernel, rels, rows),
        out_shape=[
            sds((D, 3 * D), bf16),
            sds((16, D), f32),
            sds((D, HEADS), f32),
            sds((D, HEADS), f32),
            sds((HEADS, D), f32),
            sds((HEADS, D), f32),
        ],
        in_specs=[SM] + [VM] * len(pieces),
        out_specs=[VM] * 6,
        scratch_shapes=[pltpu.VMEM((count * rows, LANES), f32)],
        compiler_params=params(),
        name="unpack_low",
    )(me, *pieces)


def unpack_feed_kernel(rels, rows, me_ref, *refs):
    n = len(rels)
    pieces = refs[:n]
    wo, w1, w2, vec, c1, flat = refs[n:]
    fill_flat(me_ref[0], pieces, rels, rows, flat)
    put_matrix(flat, row_of(1, 6), wo, D, D)
    put_matrix(flat, row_of(1, 11), w1, D, FF)
    put_matrix(flat, row_of(1, 13), w2, FF, D)
    vec[...] = jnp.zeros_like(vec)
    for at, number in ((SBO, 7), (SLS1, 8), (SG2, 9), (SB2, 10), (SC2, 14), (SLS2, 15)):
        put_row(flat, row_of(1, number), vec, at, D)
    put_row(flat, row_of(1, 12), c1, 0, FF)


def unpack_feed(me, pieces, rels, rows, count):
    return pl.pallas_call(
        functools.partial(unpack_feed_kernel, rels, rows),
        out_shape=[
            sds((D, D), bf16),
            sds((D, FF), bf16),
            sds((FF, D), bf16),
            sds((16, D), f32),
            sds((1, FF), f32),
        ],
        in_specs=[SM] + [VM] * len(pieces),
        out_specs=[VM] * 5,
        scratch_shapes=[pltpu.VMEM((count * rows, LANES), f32)],
        compiler_params=params(),
        name="unpack_feed",
    )(me, *pieces)


def unpack_class_kernel(rels, rows, me_ref, *refs):
    n = len(rels)
    pieces = refs[:n]
    wq, wkv, wo, w1, w2, vec, c1, total, flat = refs[n:]
    fill_flat(me_ref[0], pieces, rels, rows, flat)
    put_matrix(flat, row_of(2, 2), wq, D, D)
    put_matrix(flat, row_of(2, 4), wkv, D, 2 * D)
    put_matrix(flat, row_of(2, 6), wo, D, D)
    put_matrix(flat, row_of(2, 11), w1, D, FF)
    put_matrix(flat, row_of(2, 13), w2, FF, D)
    vec[...] = jnp.zeros_like(vec)
    for at, number in (
        (CG1, 0), (CB1, 1), (CBQ, 3), (CBV, 5), (CBO, 7), (CLS1, 8), (CG2, 9), (CB2, 10), (CC2, 14), (CLS2, 15),
    ):
        put_row(flat, row_of(2, number), vec, at, D)
    put_row(flat, row_of(2, 12), c1, 0, FF)
    count = jnp.zeros((1, LANES), f32)
    for ref, rel in zip(pieces, rels):
        for k in range(len(rel)):
            count = count + ref[k].astype(f32)[rows : rows + 1, :]
    total[...] = count


def const_spec(a):
    return pl.BlockSpec(a.shape, lambda i, nd=len(a.shape): (0,) * nd, pipeline_mode=pl.Buffered(1))


def cost(flops, read):
    return pl.CostEstimate(flops=int(flops), bytes_accessed=int(read), transcendentals=0)


class Steps:
    def __init__(self, ns, nl, padded, large_len):
        self.count = math.gcd(ns, nl)
        self.small, self.large = ns // self.count, nl // self.count
        self.padded, self.large_len = padded, large_len
        self.split = self.small * padded
        self.rows = self.split + self.large * large_len
        self.grid = (self.count,)

    def specs(self, cols):
        index = lambda i: (i, 0, 0)
        return [
            pl.BlockSpec((self.small, self.padded, cols), index),
            pl.BlockSpec((self.large, self.large_len, cols), index),
        ]

    def shapes(self, cols, kind):
        n = self.count
        return [sds((n * self.small, self.padded, cols), kind), sds((n * self.large, self.large_len, cols), kind)]

    def join(self, pair):
        cols = pair[0].shape[-1]
        return jnp.concatenate([ref[...].reshape(-1, cols) for ref in pair], 0)

    def put(self, pair, value):
        cols = value.shape[-1]
        pair[0][...] = value[: self.split].reshape(self.small, self.padded, cols)
        pair[1][...] = value[self.split :].reshape(self.large, self.large_len, cols)


def embed_kernel(steps, valid, ps, plg, patch_w, pos_small, pos_large, wqkv, vec, *outs):
    tok_o, qkv_o, tokens = outs[:2], outs[2:4], outs[4]
    row = lambda at: vec[at : at + 1, :]
    for i in range(steps.small):
        base = steps.padded * i
        tokens[base : base + steps.padded, :] = pos_small[...]
        tokens[base : base + valid, :] += nn(ps[i], patch_w[...])
    for i in range(steps.large):
        base = steps.split + steps.large_len * i
        tokens[base : base + steps.large_len, :] = nn(plg[i], patch_w[...]) + pos_large[...]
    tok = tokens[...]
    steps.put(tok_o, tok)
    unit, _ = stats(tok)
    a1 = (unit * row(SG1) + row(SB1)).astype(bf16)
    bias = jnp.concatenate([row(SBQ), jnp.zeros((1, D), f32), row(SBV)], 1)
    steps.put(qkv_o, (nn(a1, wqkv[...]) + bias).astype(bf16))


def embed(ps, plg, patch_w, pos_small, pos_large, wqkv, vec, padded, after):
    ns, valid, _ = ps.shape
    nl, large_len, _ = plg.shape
    steps = Steps(ns, nl, padded, large_len)
    weights = (patch_w, pos_small, pos_large, wqkv, vec)
    index = lambda i: (i, 0, 0)
    out = call(
        functools.partial(embed_kernel, steps, valid),
        (ps, plg, *weights),
        after,
        grid=steps.grid,
        out_shape=steps.shapes(D, f32) + steps.shapes(3 * D, bf16),
        in_specs=[
            pl.BlockSpec((steps.small, valid, PATCH_IN), index),
            pl.BlockSpec((steps.large, large_len, PATCH_IN), index),
        ]
        + [const_spec(a) for a in weights],
        out_specs=steps.specs(D) + steps.specs(3 * D),
        scratch_shapes=[pltpu.VMEM((steps.rows, D), f32)],
        cost_estimate=cost(12e9, 20e6),
        name="embed",
    )
    return out[:2], out[2:]


def attend_kernel(valid, qkv_ref, pre_col, post_col, att_ref, lse_ref, q_t, kk, v_t, acc):
    per, length = qkv_ref.shape[0], qkv_ref.shape[1]
    for i in range(per):
        q_t[i] = qkv_ref[i, :, 0:D].astype(f32).T
        kk[i, :, 0:D] = qkv_ref[i, :, D : 2 * D]
        kk[i, :, D:] = qkv_ref[i, :, D : 2 * D]
        v_t[i] = qkv_ref[i, :, 2 * D :].astype(f32).T.astype(bf16)
    for g in range(HEADS):
        pre, post = pre_col[:, g : g + 1], post_col[:, g : g + 1]
        for i in range(per):
            high, low = split(q_t[i] * pre)
            mixed = nn(kk[i], jnp.concatenate([high, low], 0))
            if valid < length:
                mixed = jnp.where(lax.broadcasted_iota(jnp.int32, mixed.shape, 0) < valid, mixed, NEG)
            top = jnp.max(mixed, 0, keepdims=True)
            raw = jnp.exp2(mixed - top)
            weight = colsum(raw)
            lse_ref[i, g : g + 1, :] = top + jnp.log2(weight)
            part = nn(v_t[i], raw.astype(bf16)) * post * (1.0 / weight)
            acc[i] = part if g == 0 else acc[i] + part
    for i in range(per):
        att_ref[i] = acc[i].T.astype(bf16)


def attend(qkv, pre_col, post_col, valid, per, flops, after):
    n, length, _ = qkv.shape
    spec = lambda *tail: pl.BlockSpec((per,) + tail, lambda i: (i, 0, 0))
    return call(
        functools.partial(attend_kernel, valid),
        (qkv, pre_col, post_col),
        after,
        grid=(n // per,),
        out_shape=[sds((n, length, D), bf16), sds((n, HEADS, length), f32)],
        in_specs=[spec(length, 3 * D), const_spec(pre_col), const_spec(post_col)],
        out_specs=[spec(length, D), spec(HEADS, length)],
        scratch_shapes=[
            pltpu.VMEM((per, D, length), f32),
            pltpu.VMEM((per, length, 2 * D), bf16),
            pltpu.VMEM((per, D, length), bf16),
            pltpu.VMEM((per, D, length), f32),
        ],
        cost_estimate=cost(flops, 10e6),
        name="attend",
    )


def feed_kernel(steps, tok_s, tok_l, att_s, att_l, wo, w1, w2, vec, c1, *outs):
    branch_o, mid_o, act_o, slope_o, lower_o, out_o = [outs[2 * i : 2 * i + 2] for i in range(6)]
    row = lambda at: vec[at : at + 1, :]
    branch = nn(steps.join((att_s, att_l)), wo[...]) + row(SBO)
    steps.put(branch_o, branch.astype(bf16))
    mid = steps.join((tok_s, tok_l)) + row(SLS1) * branch
    steps.put(mid_o, mid)
    unit, _ = stats(mid)
    n2 = (unit * row(SG2) + row(SB2)).astype(bf16)
    act, slope = gelu_pair(nn(n2, w1[...]) + c1[...])
    act = act.astype(bf16)
    steps.put(act_o, act)
    steps.put(slope_o, slope.astype(bf16))
    lower = nn(act, w2[...]) + row(SC2)
    steps.put(lower_o, lower.astype(bf16))
    steps.put(out_o, mid + row(SLS2) * lower)


FEED_OUT = [(D, bf16), (D, f32), (FF, bf16), (FF, bf16), (D, bf16), (D, f32)]


def feed(tok, att, weights, after):
    (ns, padded, _), (nl, large_len, _) = tok[0].shape, tok[1].shape
    steps = Steps(ns, nl, padded, large_len)
    out = call(
        functools.partial(feed_kernel, steps),
        (*tok, *att, *weights),
        after,
        grid=steps.grid,
        out_shape=[shape for entry in FEED_OUT for shape in steps.shapes(*entry)],
        in_specs=steps.specs(D) * 2 + [const_spec(a) for a in weights],
        out_specs=[spec for cols, _ in FEED_OUT for spec in steps.specs(cols)],
        cost_estimate=cost(20e9, 30e6),
        name="feed",
    )
    return [out[2 * i : 2 * i + 2] for i in range(6)]


BATCH = 8


def class_kernel(
    ns, nl, valid, out_s, out_l, wq, wkv, wo, w1, w2, vec, c1, svec, head_w, head_b, total, counts, labels_s, labels_l,
    d_s, d_l, g_wq, g_wkv, g_wo, g_w1, g_w2, g_vec, g_c1, g_svec, g_head_w, g_head_b, loss_o,
    a_s, a_l, p_s, p_l, z_ref, y_ref, b_ref, ps_ref, pc_ref, da_ref,
):
    row = lambda at: vec[at : at + 1, :]
    mask8 = head_mask(HEADS)
    mask64 = head_mask(HEADS * BATCH)
    cls = svec[1:2, :]
    unit_cls, inv_cls = stats(cls)
    a_cls = (unit_cls * row(CG1) + row(CB1)).astype(bf16)
    a_cls_f = a_cls.astype(f32)
    query = (nn(a_cls, wq[...]) + row(CBQ)).astype(bf16).astype(f32)
    q_diag = jnp.where(mask8, query, 0.0).astype(bf16)
    u_nat = nt(q_diag, wkv[:, 0:D]) * SCALE
    u_hi, u_lo = split(u_nat * LOG2E)
    u16 = jnp.concatenate([u_hi, u_lo], 0)
    s_cls = jnp.sum(u_nat * LOG2E * a_cls_f, -1, keepdims=True)
    z_ref[...] = jnp.zeros_like(z_ref)
    ps_ref[...] = jnp.zeros_like(ps_ref)

    def forward(i, src, a_ref, p_ref, slot):
        unit, _ = stats(src[i])
        a = (unit * row(CG1) + row(CB1)).astype(bf16)
        a_ref[i] = a
        s16 = nt(u16, a)
        s = s16[0:HEADS] + s16[HEADS:]
        keep = valid if a.shape[0] != GRID_LARGE**2 else a.shape[0]
        if keep < a.shape[0]:
            s = jnp.where(lax.broadcasted_iota(jnp.int32, s.shape, 1) < keep, s, NEG)
        top = jnp.maximum(jnp.max(s, -1, keepdims=True), s_cls)
        e = jnp.exp2(s - top)
        e_cls = jnp.exp2(s_cls - top)
        inverse = 1.0 / (jnp.sum(e, -1, keepdims=True) + e_cls)
        p, p_cls = e * inverse, e_cls * inverse
        p_ref[i] = p
        low, low_cls = p.astype(bf16), p_cls.astype(bf16).astype(f32)
        z_ref[pl.ds(slot * HEADS, HEADS), :] = nn(low, a) + low_cls * a_cls_f
        ps_ref[pl.ds(slot * HEADS, HEADS), :] = jnp.sum(low.astype(f32), -1, keepdims=True) + low_cls
        pc_ref[pl.ds(slot * HEADS, HEADS), :] = p_cls

    for i in range(ns):
        forward(i, out_s, a_s, p_s, i)
    for i in range(nl):
        forward(i, out_l, a_l, p_l, ns + i)

    z_hi, z_lo = split(z_ref[...])
    o_all = nn(jnp.concatenate([z_hi, z_lo], 0), wkv[:, D:])
    o_all = o_all[0 : HEADS * BATCH] + o_all[HEADS * BATCH :] + ps_ref[...] * row(CBV)
    att = jnp.sum(jnp.where(mask64, o_all, 0.0).reshape(BATCH, HEADS, D), 1).astype(bf16)
    branch = nn(att, wo[...]) + row(CBO)
    mid = cls + row(CLS1) * branch
    unit_mid, inv_mid = stats(mid)
    n2 = (unit_mid * row(CG2) + row(CB2)).astype(bf16)
    upper = nn(n2, w1[...]) + c1[...]
    act, slope = gelu_pair(upper)
    act = act.astype(bf16)
    lower = nn(act, w2[...]) + row(CC2)
    c_tok = mid + row(CLS2) * lower
    unit_c, inv_c = stats(c_tok)
    final = (unit_c * svec[2:3, :] + svec[3:4, :]).astype(bf16)
    logits = nn(final, head_w[...]) + head_b[...]
    lane = lax.broadcasted_iota(jnp.int32, logits.shape, 1)
    inside = lane < CLASSES
    logits = jnp.where(inside, logits, NEG)
    shifted = logits - jnp.max(logits, -1, keepdims=True)
    raw = jnp.exp(shifted)
    weight = jnp.sum(raw, -1, keepdims=True)
    logp = shifted - jnp.log(weight)
    image = lax.broadcasted_iota(jnp.int32, (BATCH, 1), 0)
    label = jnp.zeros((BATCH, 1), jnp.int32)
    for i in range(ns):
        label = jnp.where(image == i, labels_s[i], label)
    for i in range(nl):
        label = jnp.where(image == ns + i, labels_l[i], label)
    alive = ((image < ns) & (image < counts[0, 0])) | ((image >= ns) & (image - ns < counts[0, 1]))
    hit = lane == label
    picked = jnp.sum(jnp.where(hit, logp, 0.0), -1, keepdims=True)
    mean = jnp.sum(jnp.where(inside, logp, 0.0), -1, keepdims=True) * (1.0 / CLASSES)
    each = -((1.0 - smooth) * picked + smooth * mean)
    scaled = jnp.where(alive, 1.0, 0.0) / total[0:1, 0:1]
    loss_o[...] = jnp.broadcast_to(colsum(scaled * each), loss_o.shape)
    target = jnp.where(hit, 1.0 - smooth, 0.0) + smooth / CLASSES
    d_logits = jnp.where(inside, scaled * (raw / weight - target), 0.0).astype(bf16)

    d_final = nt(d_logits, head_w[...])
    g_head_w[...] = tn(final, d_logits)
    g_head_b[...] = colsum(d_logits.astype(f32))
    g_svec[...] = jnp.zeros_like(g_svec)
    g_svec[2:3, :] = colsum(d_final * unit_c)
    g_svec[3:4, :] = colsum(d_final)
    d_c = norm_back(d_final, unit_c, inv_c, svec[2:3, :])
    g_vec[...] = jnp.zeros_like(g_vec)
    g_vec[CLS2 : CLS2 + 1, :] = colsum(d_c * lower)
    d_lower = (d_c * row(CLS2)).astype(bf16)
    g_vec[CC2 : CC2 + 1, :] = colsum(d_lower.astype(f32))
    g_w2[...] = tn(act, d_lower)
    d_upper = (slope * nt(d_lower, w2[...])).astype(bf16)
    g_c1[...] = colsum(d_upper.astype(f32))
    g_w1[...] = tn(n2, d_upper)
    d_n2 = nt(d_upper, w1[...])
    g_vec[CG2 : CG2 + 1, :] = colsum(d_n2 * unit_mid)
    g_vec[CB2 : CB2 + 1, :] = colsum(d_n2)
    d_mid = d_c + norm_back(d_n2, unit_mid, inv_mid, row(CG2))
    g_vec[CLS1 : CLS1 + 1, :] = colsum(d_mid * branch)
    d_branch = (d_mid * row(CLS1)).astype(bf16)
    g_vec[CBO : CBO + 1, :] = colsum(d_branch.astype(f32))
    g_wo[...] = tn(att, d_branch)
    d_att = nt(d_branch, wo[...]).astype(bf16).astype(f32)
    d_diag = jnp.where(mask64, jnp.broadcast_to(d_att[:, None, :], (BATCH, HEADS, D)).reshape(BATCH * HEADS, D), 0.0)
    g_vec[CBV : CBV + 1, :] = colsum(d_diag * ps_ref[...])
    shift = jnp.sum(d_diag * row(CBV), -1, keepdims=True)
    d_diag_low = d_diag.astype(bf16)
    y_ref[...] = nt(d_diag_low, wkv[:, D:])
    g_wkv[:, D:] = tn(jnp.concatenate([z_hi, z_lo], 0), jnp.concatenate([d_diag_low, d_diag_low], 0))
    z_ref[:, 0:1] = shift
    b_ref[...] = jnp.zeros_like(b_ref)
    da_ref[...] = jnp.zeros_like(da_ref)
    un_hi, un_lo = split(u_nat)

    def backward(i, src, a_ref, p_ref, d_ref, slot):
        unit, inverse = stats(src[i])
        a = a_ref[i]
        here = pl.ds(slot * HEADS, HEADS)
        y = y_ref[here, :]
        y_hi, y_lo = split(y)
        d16 = nt(jnp.concatenate([y_hi, y_lo], 0), a)
        offset = z_ref[here, 0:1]
        d_p = d16[0:HEADS] + d16[HEADS:] + offset
        d_p_cls = jnp.sum(y * a_cls_f, -1, keepdims=True) + offset
        p, p_cls = p_ref[i], pc_ref[here, :]
        delta = jnp.sum(p * d_p, -1, keepdims=True) + p_cls * d_p_cls
        d_score = (p * (d_p - delta)).astype(bf16)
        d_score_cls = (p_cls * (d_p_cls - delta)).astype(bf16).astype(f32)
        low = p.astype(bf16)
        b_ref[...] += nn(d_score, a) + d_score_cls * a_cls_f
        da_ref[...] += d_score_cls * u_nat + p_cls.astype(bf16).astype(f32) * y
        left = jnp.concatenate([d_score.astype(f32), d_score.astype(f32), low.astype(f32), low.astype(f32)], 0)
        d_a = tn(left.astype(bf16), jnp.concatenate([un_hi, un_lo, y_hi, y_lo], 0))
        g_vec[CG1 : CG1 + 1, :] += colsum(d_a * unit)
        g_vec[CB1 : CB1 + 1, :] += colsum(d_a)
        d_ref[i] = norm_back(d_a, unit, inverse, row(CG1))

    for i in range(ns):
        backward(i, out_s, a_s, p_s, d_s, i)
    for i in range(nl):
        backward(i, out_l, a_l, p_l, d_l, ns + i)

    b_hi, b_lo = split(b_ref[...])
    bw = nn(jnp.concatenate([b_hi, b_lo], 0), wkv[:, 0:D])
    bw = bw[0:HEADS] + bw[HEADS:]
    d_query = (colsum(jnp.where(mask8, bw, 0.0)) * SCALE).astype(bf16)
    g_vec[CBQ : CBQ + 1, :] = d_query.astype(f32)
    q_scaled = q_diag.astype(f32) * SCALE
    qs_hi, qs_lo = split(q_scaled)
    g_wkv[:, 0:D] = tn(
        jnp.concatenate([b_hi, b_hi, b_lo, b_lo], 0), jnp.concatenate([qs_hi, qs_lo, qs_hi, qs_lo], 0)
    )
    first = lax.broadcasted_iota(jnp.int32, (16, D), 0) == 0
    spread_a = jnp.where(first, jnp.broadcast_to(a_cls_f, (16, D)), 0.0).astype(bf16)
    spread_q = jnp.where(first, jnp.broadcast_to(d_query.astype(f32), (16, D)), 0.0).astype(bf16)
    g_wq[...] = tn(spread_a, spread_q)
    d_a_cls = colsum(da_ref[...]) + nt(d_query, wq[...])
    g_vec[CG1 : CG1 + 1, :] += d_a_cls * unit_cls
    g_vec[CB1 : CB1 + 1, :] += d_a_cls
    g_svec[1:2, :] = colsum(d_mid) + norm_back(d_a_cls, unit_cls, inv_cls, row(CG1))


CLASS_WEIGHTS = [(D, D), (D, 2 * D), (D, D), (D, FF), (FF, D)]


def class_step_kernel(ns, nl, valid, unpack_rels, pack_rels, rows, n, me_ref, from_ref, counts, labels_s, labels_l, *refs):
    pieces, (out_s, out_l, svec, head_w, head_b), refs = refs[:n], refs[n : n + 5], refs[n + 5 :]
    (d_s, d_l, g_svec, g_head_w, g_head_b, loss, keep, send), refs = refs[:8], refs[8:]
    weights, total, grads, flat, work = refs[:7], refs[7], refs[8:15], refs[15], refs[16:]
    unpack_class_kernel(unpack_rels, rows, from_ref, *pieces, *weights, total, flat)
    class_kernel(
        ns, nl, valid, out_s, out_l, *weights, svec, head_w, head_b, total, counts, labels_s, labels_l,
        d_s, d_l, *grads, g_svec, g_head_w, g_head_b, loss, *work,
    )
    pack_class_kernel(pack_rels, rows, me_ref, *grads, keep, send, flat)


def class_step(me, unpack_me, pieces, unpack_rels, pack_rels, out, stem, counts, labels_s, labels_l, valid, rows, padded_rows):
    (ns, padded, _), (nl, large_len, _) = out[0].shape, out[1].shape
    _, svec, _, _, head_w, head_b = stem
    args = (me, unpack_me, counts, labels_s, labels_l, *pieces, *out, svec, head_w, head_b)
    half = len(pack_rels) // 2
    vectors = [pltpu.VMEM((16, D), f32), pltpu.VMEM((1, FF), f32)]
    return pl.pallas_call(
        functools.partial(
            class_step_kernel, ns, nl, valid, unpack_rels, pack_rels, rows, len(pieces)
        ),
        out_shape=[
            sds((ns, padded, D), f32),
            sds((nl, large_len, D), f32),
            sds((8, D), f32),
            sds((D, CLASS_PAD), f32),
            sds((1, CLASS_PAD), f32),
            sds((1, LANES), f32),
            sds((half, padded_rows, LANES), f32),
            sds((half, padded_rows, LANES), bf16),
        ],
        in_specs=[SM] * 5 + [VM] * (len(args) - 5),
        out_specs=[VM] * 8,
        scratch_shapes=[pltpu.VMEM(shape, bf16) for shape in CLASS_WEIGHTS]
        + vectors
        + [pltpu.VMEM((1, LANES), f32)]
        + [pltpu.VMEM(shape, f32) for shape in CLASS_WEIGHTS]
        + vectors
        + [
            pltpu.VMEM((len(pack_rels) * rows + padded_rows - rows + 8, LANES), f32),
            pltpu.VMEM((ns, padded, D), bf16),
            pltpu.VMEM((nl, large_len, D), bf16),
            pltpu.VMEM((ns, HEADS, padded), f32),
            pltpu.VMEM((nl, HEADS, large_len), f32),
            pltpu.VMEM((BATCH * HEADS, D), f32),
            pltpu.VMEM((BATCH * HEADS, D), f32),
            pltpu.VMEM((HEADS, D), f32),
            pltpu.VMEM((BATCH * HEADS, 1), f32),
            pltpu.VMEM((BATCH * HEADS, 1), f32),
            pltpu.VMEM((HEADS, D), f32),
        ],
        compiler_params=params(),
        cost_estimate=cost(25e9, 40e6),
        name="class_step",
    )(*args)


def feed_back_kernel(steps, *refs):
    ins, (wo, w1, w2, vec), refs = [refs[2 * i : 2 * i + 2] for i in range(7)], refs[14:18], refs[18:]
    d_mid_o, d_att_o, sums = refs[:2], refs[2:4], refs[4:]
    g_wo, g_w1, g_w2, g_vec, g_c1 = sums
    row = lambda at: vec[at : at + 1, :]

    @pl.when(pl.program_id(0) == 0)
    def _():
        for ref in sums:
            ref[...] = jnp.zeros_like(ref)

    def add(at, value):
        g_vec[at : at + 1, :] += value

    d_out_r, mid_r, act_r, slope_r, lower_r, branch_r, att_r = ins
    d_out = steps.join(d_out_r)
    add(SLS2, colsum(d_out * steps.join(lower_r).astype(f32)))
    d_lower = (d_out * row(SLS2)).astype(bf16)
    add(SC2, colsum(d_lower.astype(f32)))
    unit, inverse = stats(steps.join(mid_r))
    n2 = (unit * row(SG2) + row(SB2)).astype(bf16)
    g_w2[...] += tn(steps.join(act_r), d_lower)
    d_upper = (nt(d_lower, w2[...]) * steps.join(slope_r).astype(f32)).astype(bf16)
    g_w1[...] += tn(n2, d_upper)
    g_c1[...] += colsum(d_upper.astype(f32))
    d_n2 = nt(d_upper, w1[...])
    add(SG2, colsum(d_n2 * unit))
    add(SB2, colsum(d_n2))
    d_mid = d_out + norm_back(d_n2, unit, inverse, row(SG2))
    steps.put(d_mid_o, d_mid)
    add(SLS1, colsum(d_mid * steps.join(branch_r).astype(f32)))
    d_branch = (d_mid * row(SLS1)).astype(bf16)
    add(SBO, colsum(d_branch.astype(f32)))
    g_wo[...] += tn(steps.join(att_r), d_branch)
    steps.put(d_att_o, nt(d_branch, wo[...]).astype(bf16))


def sum_specs(shapes):
    return [pl.BlockSpec(s.shape, lambda i: (0, 0), pipeline_mode=pl.Buffered(1)) for s in shapes]


def feed_back(pairs, weights, after):
    (ns, padded, _), (nl, large_len, _) = pairs[0][0].shape, pairs[0][1].shape
    steps = Steps(ns, nl, padded, large_len)
    sums = [sds((D, D), f32), sds((D, FF), f32), sds((FF, D), f32), sds((16, D), f32), sds((1, FF), f32)]
    out = call(
        functools.partial(feed_back_kernel, steps),
        (*[a for pair in pairs for a in pair], *weights),
        after,
        grid=steps.grid,
        out_shape=steps.shapes(D, f32) + steps.shapes(D, bf16) + sums,
        in_specs=[spec for pair in pairs for spec in steps.specs(pair[0].shape[2])] + [const_spec(a) for a in weights],
        out_specs=steps.specs(D) * 2 + sum_specs(sums),
        cost_estimate=cost(35e9, 30e6),
        name="feed_back",
    )
    return out[:2], out[2:4], out[4:]


def attend_back_kernel(valid, qkv_ref, d_att_ref, lse_ref, pre_col, post_col, pre_row, post_row, d_qkv_ref, g_pre, g_post,
                       q_t, kk, k_t, do_t, dq_t, d_k, d_v):
    per, length = qkv_ref.shape[0], qkv_ref.shape[1]
    for i in range(per):
        q_t[i] = qkv_ref[i, :, 0:D].astype(f32).T
        kk[i, :, 0:D] = qkv_ref[i, :, D : 2 * D]
        kk[i, :, D:] = qkv_ref[i, :, D : 2 * D]
        k_t[i] = qkv_ref[i, :, D : 2 * D].astype(f32).T.astype(bf16)
        do_t[i] = d_att_ref[i].astype(f32).T

    @pl.when(pl.program_id(0) == 0)
    def _():
        g_pre[...] = jnp.zeros_like(g_pre)
        g_post[...] = jnp.zeros_like(g_post)

    for g in range(HEADS):
        pre, post = pre_col[:, g : g + 1], post_col[:, g : g + 1]
        for i in range(per):
            q, k, v = qkv_ref[i, :, 0:D], qkv_ref[i, :, D : 2 * D], qkv_ref[i, :, 2 * D :]
            high, low = split(q_t[i] * pre)
            mixed = nn(kk[i], jnp.concatenate([high, low], 0))
            d_p = nn(v, (do_t[i] * post).astype(bf16))
            p = jnp.exp2(mixed - lse_ref[i, g : g + 1, :])
            if valid < length:
                p = jnp.where(lax.broadcasted_iota(jnp.int32, p.shape, 0) < valid, p, 0.0)
            delta = colsum(p * d_p)
            d_mixed = (p * (d_p - delta)).astype(bf16)
            r = nn(p.astype(bf16), d_att_ref[i])
            t = nn(d_mixed, q)
            u = nn(k_t[i], d_mixed)
            d_v_part, d_k_part, d_q_part = r * post_row[g : g + 1, :], t * pre_row[g : g + 1, :], u * pre
            d_v[i] = d_v_part if g == 0 else d_v[i] + d_v_part
            d_k[i] = d_k_part if g == 0 else d_k[i] + d_k_part
            dq_t[i] = d_q_part if g == 0 else dq_t[i] + d_q_part
            g_post[g : g + 1, :] += colsum(r * v.astype(f32))
            g_pre[g : g + 1, :] += colsum(t * k.astype(f32))
    inverse = 1.0 / LOG2E
    for i in range(per):
        d_qkv_ref[i, :, 0:D] = (dq_t[i].T * inverse).astype(bf16)
        d_qkv_ref[i, :, D : 2 * D] = (d_k[i] * inverse).astype(bf16)
        d_qkv_ref[i, :, 2 * D :] = d_v[i].astype(bf16)


def attend_back(qkv, d_att, lse, mixes, valid, first, count, per, flops, after):
    length = qkv.shape[1]
    spec = lambda *tail: pl.BlockSpec((per,) + tail, lambda i: (i + first // per, 0, 0))
    sums = [sds((HEADS, D), f32)] * 2
    return call(
        functools.partial(attend_back_kernel, valid),
        (qkv, d_att, lse, *mixes),
        after,
        grid=(count // per,),
        out_shape=[sds((count, length, 3 * D), bf16)] + sums,
        in_specs=[spec(length, 3 * D), spec(length, D), spec(HEADS, length)] + [const_spec(a) for a in mixes],
        out_specs=[pl.BlockSpec((per, length, 3 * D), lambda i: (i, 0, 0))] + sum_specs(sums),
        scratch_shapes=[
            pltpu.VMEM((per, D, length), f32),
            pltpu.VMEM((per, length, 2 * D), bf16),
            pltpu.VMEM((per, D, length), bf16),
            pltpu.VMEM((per, D, length), f32),
            pltpu.VMEM((per, D, length), f32),
            pltpu.VMEM((per, length, D), f32),
            pltpu.VMEM((per, length, D), f32),
        ],
        cost_estimate=cost(flops, 10e6),
        name="attend_back",
    )


def embed_back_kernel(steps, valid, late, me_ref, ps, plg, resize, *refs):
    tok_r, dq_s, d_mid_r, refs = refs[:2], refs[2], refs[3:5], refs[5:]
    n = steps.large * steps.count
    dq_l, (wqkv, vec, pre, post, g_wo, g_svec, g_head_w), refs = refs[:n], refs[n : n + 7], refs[n + 7 :]
    (keep, send), sums, (d_qkv, flat, tiles) = refs[:2], refs[2:8], refs[8:]
    g_wqkv, g_vec, g_patch_w, g_patch_b, g_pos, pos_large = sums
    row = lambda at: vec[at : at + 1, :]
    step = pl.program_id(0)

    @pl.when(step == 0)
    def _():
        for ref in sums:
            ref[...] = jnp.zeros_like(ref)

    d_qkv[: steps.split, :] = dq_s[...].reshape(steps.split, 3 * D)
    for k in range(steps.count):

        @pl.when(step == k)
        def _(k=k):
            for i in range(steps.large):
                base = steps.split + steps.large_len * i
                d_qkv[base : base + steps.large_len, :] = dq_l[k * steps.large + i][0]

    def add(at, value):
        g_vec[at : at + 1, :] += value

    add(SBQ, colsum(d_qkv[:, 0:D].astype(f32)))
    add(SBV, colsum(d_qkv[:, 2 * D :].astype(f32)))
    unit, inverse = stats(steps.join(tok_r))
    a1 = (unit * row(SG1) + row(SB1)).astype(bf16)
    g_wqkv[...] += tn(a1, d_qkv[...])
    d_a1 = nt(d_qkv[...], wqkv[...])
    add(SG1, colsum(d_a1 * unit))
    add(SB1, colsum(d_a1))
    d_tok = steps.join(d_mid_r) + norm_back(d_a1, unit, inverse, row(SG1))
    g_patch_b[0:1, :] += colsum(d_tok)
    for i in range(steps.small):
        mine = d_tok[steps.padded * i : steps.padded * i + valid, :]
        g_pos[...] += mine
        g_patch_w[...] += tn(ps[i], mine.astype(bf16))
    for i in range(steps.large):
        base = steps.split + steps.large_len * i
        mine = d_tok[base : base + steps.large_len, :]
        pos_large[...] += mine
        g_patch_w[...] += tn(plg[i], mine.astype(bf16))

    @pl.when(step == steps.count - 1)
    def _():
        g_pos[...] += lax.dot_general(
            resize[...], pos_large[...], (((1,), (0,)), ((), ())),
            preferred_element_type=f32, precision=lax.Precision.HIGHEST,
        )
        pack_late_kernel(
            *late, me_ref, g_wqkv, g_vec, pre, post, g_wo, g_patch_w, g_patch_b, g_pos, g_svec, g_head_w,
            keep, send, flat, tiles,
        )


def embed_back(me, ps, plg, tok, dq_s, d_mid, dq_l, wqkv, vec, others, late, padded_rows, after):
    ns, valid, _ = ps.shape
    nl, large_len, _ = plg.shape
    steps = Steps(ns, nl, tok[0].shape[1], large_len)
    resize = jnp.asarray(resize_table().T.copy())
    sums = [
        sds((D, 3 * D), f32),
        sds((16, D), f32),
        sds((PATCH_IN, D), f32),
        sds((8, D), f32),
        sds((valid, D), f32),
    ]
    index = lambda i: (i, 0, 0)
    half = len(late[0]) // 2
    outs = [sds((half, 2 * padded_rows, LANES), f32), sds((half, 2 * padded_rows, LANES), bf16)]
    return call(
        functools.partial(embed_back_kernel, steps, valid, late),
        (me, ps, plg, resize, *tok, dq_s, *d_mid, *dq_l, wqkv, vec, *others),
        after,
        grid=steps.grid,
        out_shape=outs,
        in_specs=[
            SM,
            pl.BlockSpec((steps.small, valid, PATCH_IN), index),
            pl.BlockSpec((steps.large, large_len, PATCH_IN), index),
            const_spec(resize),
            *steps.specs(D),
            steps.specs(3 * D)[0],
            *steps.specs(D),
        ]
        + [const_spec(a) for a in (*dq_l, wqkv, vec, *others)],
        out_specs=[const_spec(a) for a in outs],
        scratch_shapes=[pltpu.VMEM(a.shape, f32) for a in sums]
        + [
            pltpu.VMEM((large_len, D), f32),
            pltpu.VMEM((steps.rows, 3 * D), bf16),
            pltpu.VMEM((row_of(0, 6) + 1280, LANES), f32),
            pltpu.VMEM((8, D + 16, LANES), f32),
        ],
        cost_estimate=cost(20e9, 30e6),
        name="embed_back",
    )


def take_matrix(flat, row, src, rows, cols):
    step = cols // LANES
    for j in range(step):
        flat[pl.ds(row + j, rows, stride=step), :] = src[0:rows, LANES * j : LANES * (j + 1)]


def take_row(flat, row, src, at, cols):
    for j in range(cols // LANES):
        flat[row + j : row + j + 1, :] = src[at : at + 1, LANES * j : LANES * (j + 1)]


def slots_of(order):
    rels = [0]
    for bit in reversed(order):
        rels = rels + [r | (1 << bit) for r in rels]
    return rels


def emit_slots(me, flat, rows, rels, keep_ref, send_ref, offset=0):
    half = len(rels) // 2
    for k, r in enumerate(rels):
        value = flat[pl.ds(offset + rows * jnp.bitwise_xor(me, r), keep_ref.shape[1]), :]
        if k < half:
            keep_ref[k] = value
        else:
            send_ref[k - half] = value.astype(bf16)


def pack_class_kernel(rels, rows, me_ref, wq, wkv, wo, w1, w2, vec, c1, keep, send, flat):
    used = rows_used(2)
    flat[used:, :] = jnp.zeros((flat.shape[0] - used, LANES), f32)
    take_matrix(flat, row_of(2, 2), wq, D, D)
    take_matrix(flat, row_of(2, 4), wkv, D, 2 * D)
    take_matrix(flat, row_of(2, 6), wo, D, D)
    take_matrix(flat, row_of(2, 11), w1, D, FF)
    take_matrix(flat, row_of(2, 13), w2, FF, D)
    for at, number in (
        (CG1, 0), (CB1, 1), (CBQ, 3), (CBV, 5), (CBO, 7), (CLS1, 8), (CG2, 9), (CB2, 10), (CC2, 14), (CLS2, 15),
    ):
        take_row(flat, row_of(2, number), vec, at, D)
    take_row(flat, row_of(2, 12), c1, 0, FF)
    emit_slots(me_ref[0], flat, rows, rels, keep, send)


def take_head(flat, base, head_w, head_b, tiles, groups):
    for t in range(8):
        tiles[t, 0:D, :] = head_w[:, LANES * t : LANES * (t + 1)]
    lane = lax.broadcasted_iota(jnp.int32, (groups, LANES), 1)
    for rho in range(16):
        first, shift = (CLASSES * rho) // LANES, (CLASSES * rho) % LANES
        parts = [tiles[t, pl.ds(rho, groups, stride=16), :] for t in range(8)]
        if shift:
            parts = [pltpu.roll(p, shift, 1) for p in parts]
        for t in range(9 if shift + CLASSES > CLASS_PAD else 8):
            if shift:
                value = jnp.where(lane >= shift, parts[t] if t < 8 else 0.0, parts[t - 1] if t > 0 else 0.0)
            else:
                value = parts[t]
            here = pl.ds(base + first + t, groups, stride=125)
            flat[here, :] = flat[here, :] + value
    if head_b is not None:
        take_row(flat, base + row_of(0, 7) - row_of(0, 6), head_b, 0, CLASS_PAD)


HEAD_GROUPS = D // 16


def pack_feed_kernel(rels, rows, offset, quarter_rows, me_ref, wo, w1, w2, vec, c1, head_w, head_b, keep, send, flat, tiles):
    used, first = rows_used(1), row_of(1, 6)
    flat[0 : offset + first, :] = jnp.zeros((offset + first, LANES), f32)
    flat[offset + used :, :] = jnp.zeros((flat.shape[0] - used - offset, LANES), f32)
    take_head(flat, offset + row_of(0, 6) - quarter_rows, head_w, head_b, tiles, HEAD_GROUPS)
    boundary = quarter_rows - first
    flat[offset + first : offset + quarter_rows, :] = jnp.zeros((boundary, LANES), f32)
    take_matrix(flat, offset + first, wo, D, D)
    flat[offset + first : offset + quarter_rows, :] = jnp.zeros((boundary, LANES), f32)
    take_matrix(flat, offset + row_of(1, 11), w1, D, FF)
    take_matrix(flat, offset + row_of(1, 13), w2, FF, D)
    for at, number in ((SBO, 7), (SLS1, 8), (SG2, 9), (SB2, 10), (SC2, 14), (SLS2, 15)):
        take_row(flat, offset + row_of(1, number), vec, at, D)
    take_row(flat, offset + row_of(1, 12), c1, 0, FF)
    emit_slots(me_ref[0], flat, rows, rels, keep, send, offset)


def pack_late_kernel(
    rels, rows, quarter_rows, me_ref, wqkv, vec, pre, post, wo, patch_w, patch_b, pos, svec, head_w, keep, send, flat, tiles
):
    padded_rows = keep.shape[1] // 2
    for g in range(2):
        pack_late_group(g, quarter_rows, wqkv, vec, pre, post, wo, patch_w, patch_b, pos, svec, head_w, flat, tiles)
        here = pl.ds(g * padded_rows, padded_rows)
        emit_slots(me_ref[0], flat, rows, rels, keep.at[:, here], send.at[:, here])


def pack_late_group(g, quarter_rows, wqkv, vec, pre, post, wo, patch_w, patch_b, pos, svec, head_w, flat, tiles):
    if g == 0:
        first = row_of(0, 6)
        flat[first:, :] = jnp.zeros((flat.shape[0] - first, LANES), f32)
        take_matrix(flat, row_of(0, 0), patch_w, PATCH_IN, D)
        take_row(flat, row_of(0, 1), patch_b, 0, D)
        take_matrix(flat, row_of(0, 2), pos, GRID_SMALL**2, D)
        for at, number in ((1, 3), (2, 4), (3, 5)):
            take_row(flat, row_of(0, number), svec, at, D)
        take_head(flat, first, head_w, None, tiles, 8)
        return
    first = row_of(1, 6)
    take_matrix(flat, row_of(1, 2), wqkv, D, 3 * D)
    take_matrix(flat, first, wo, 24, D)
    bq = row_of(1, 3)
    for at, row in ((SG1, row_of(1, 0)), (SB1, row_of(1, 1)), (SBQ, bq), (SBV, bq + D // LANES)):
        take_row(flat, row, vec, at, D)
    table_col = lax.broadcasted_iota(jnp.int32, (D, LANES), 0) // WIDTH
    table_lane = lax.broadcasted_iota(jnp.int32, (D, LANES), 1)
    lane = lax.broadcasted_iota(jnp.int32, (HEADS, LANES), 1)
    row = lax.broadcasted_iota(jnp.int32, (HEADS, LANES), 0)
    exact = lambda a, b: lax.dot_general(
        a, b, (((1,), (0,)), ((), ())), preferred_element_type=f32, precision=lax.Precision.HIGHEST
    )
    sum_pre = exact(pre[...], jnp.where(table_lane % HEADS == table_col, 1.0, 0.0))
    sum_post = exact(post[...], jnp.where((table_lane - 64) // HEADS == table_col, 1.0, 0.0))
    line = colsum(jnp.where((lane < 64) & (lane // HEADS == row), sum_pre * SCALE, 0.0))
    line = line + colsum(jnp.where((lane >= 64) & (lane % HEADS == row), sum_post, 0.0))
    flat[row_of(1, 4) : row_of(1, 4) + 1, :] = line


def pack(kernel, name, me, arrays, rels, padded_rows, flat_rows, extra=()):
    half = len(rels) // 2
    return pl.pallas_call(
        kernel,
        out_shape=[sds((half, padded_rows, LANES), f32), sds((half, padded_rows, LANES), bf16)],
        in_specs=[SM] + [VM] * len(arrays),
        out_specs=[VM] * 2,
        scratch_shapes=[pltpu.VMEM((flat_rows, LANES), f32), *extra],
        compiler_params=params(),
        name=name,
    )(me, *arrays)


class Chain:
    def __init__(self, keep, send, order, z_bits, z_last=False):
        self.keep, self.send, self.order, self.z_bits, self.z_last = keep, send, list(order), z_bits, z_last
        self.total = None
        self.done = False

    def finish(self, total):
        self.total = self.send = total
        self.done = True

    def step(self, after=None):
        if self.order:
            (got,) = tied((exchange(self.send, self.order.pop(0), self.z_bits),), after)
            total = self.keep + got.astype(f32)
            if self.order:
                half = total.shape[0] // 2
                self.keep, self.send = total[:half], total[half:].astype(bf16)
            elif self.z_last:
                self.keep, self.send = total[0], total[1:].astype(bf16)
            else:
                self.finish(total[0])
        elif not self.done:
            got = [exchange_z(self.send[k - 1], k) for k in range(1, self.send.shape[0] + 1)]
            total = self.keep
            for part in tied(tuple(got), after):
                total = total + part.astype(f32)
            self.finish(total)


def bounds_table():
    table = np.zeros((8, LANES), np.int32)
    table[0:3, :SEGMENTS] = STARTS // 64
    table[3:6, :SEGMENTS] = -(-ENDS // 64)
    return table


def pick(group, values):
    return jnp.where(group == 0, values[0], jnp.where(group == 1, values[1], values[2]))


def segment_sums(square, group, first_row, bounds):
    rows = square.shape[0]
    lane = lax.broadcasted_iota(jnp.int32, (rows, LANES), 1)
    left = jnp.sum(jnp.where(lane < 64, square, 0.0), -1, keepdims=True)
    right = jnp.sum(jnp.where(lane < 64, 0.0, square), -1, keepdims=True)
    place = 2 * (first_row + lax.broadcasted_iota(jnp.int32, (rows, LANES), 0))
    low, high = bounds[group : group + 1, :], bounds[3 + group : 4 + group, :]
    one = jnp.where((place >= low) & (place < high), left, 0.0)
    two = jnp.where((place + 1 >= low) & (place + 1 < high), right, 0.0)
    return colsum(one + two)


def adam_kernel(rows, me_ref, step_ref, bounds, master, first, second, g0, g1, g2, grad_o, first_o, second_o, update_o, sums_o):
    shard = rows * LANES
    for g, ref in enumerate((g0, g1, g2)):
        grad_o[g : g + 1, :] = ref[0:rows, :].reshape(1, shard)
    grad = grad_o[...]
    weight = master[...]
    new_first = beta_one * first[...] + (1.0 - beta_one) * grad
    new_second = beta_two * second[...] + (1.0 - beta_two) * grad * grad
    first_o[...] = new_first
    second_o[...] = new_second
    power = jnp.full((1, LANES), step_ref[0], jnp.int32).astype(f32)
    scale_one = (1.0 / (1.0 - jnp.power(f32(beta_one), power)))[:, 0:1]
    scale_two = (1.0 / (1.0 - jnp.power(f32(beta_two), power)))[:, 0:1]
    update = new_first * scale_one / (jnp.sqrt(new_second * scale_two) + adam_eps) + decay_rate * weight
    update_o[...] = update
    sums_o[...] = jnp.zeros_like(sums_o)
    first_row = me_ref[0] * rows
    for g in range(3):
        part = update_o[g : g + 1, :].reshape(rows, LANES)
        sums_o[3 + g : 4 + g, :] = segment_sums(part * part, g, first_row, bounds)


def adam(me, step, master, first, second, grads, rows):
    shape = master.shape
    return pl.pallas_call(
        functools.partial(adam_kernel, rows),
        out_shape=[sds(shape, f32)] * 4 + [sds((8, LANES), f32)],
        in_specs=[SM, SM] + [VM] * 7,
        out_specs=[VM] * 5,
        compiler_params=params(),
        name="adam",
    )(me, step, jnp.asarray(bounds_table()), master, first, second, *grads)


def apply_kernel(me_ref, sums, bounds, master, update, new_o, weight_o, norm_o, trust_o):
    shard = master.shape[1]
    roots = jnp.sqrt(sums[...])
    weight_norms, update_norms = roots[0:3, :], roots[3:6, :]
    lane = lax.broadcasted_iota(jnp.int32, (3, LANES), 1)
    group3 = lax.broadcasted_iota(jnp.int32, (3, LANES), 0)
    used = pick(group3, [int(REAL[g].sum()) for g in range(3)])
    trust = jnp.where(lane < used, weight_norms / (update_norms + norm_eps), 1.0)
    weight_o[...] = weight_norms[:, 0:SEGMENTS]
    norm_o[...] = update_norms[:, 0:SEGMENTS]
    trust_o[...] = trust[:, 0:SEGMENTS]
    rows = shard // LANES
    place = 2 * (me_ref[0] * rows + lax.broadcasted_iota(jnp.int32, (rows, LANES), 0))
    lane = lax.broadcasted_iota(jnp.int32, (rows, LANES), 1)
    for g in range(3):
        low, high, mine = bounds[g : g + 1, :], bounds[3 + g : 4 + g, :], trust[g : g + 1, :]
        left = jnp.sum(jnp.where((place >= low) & (place < high), mine, 0.0), -1, keepdims=True)
        right = jnp.sum(jnp.where((place + 1 >= low) & (place + 1 < high), mine, 0.0), -1, keepdims=True)
        ratio = jnp.where(lane < 64, left, right).reshape(1, shard)
        new_o[g : g + 1, :] = master[g : g + 1, :] - learn_rate * ratio * update[g : g + 1, :]


def apply_update(me, sums, master, update):
    return pl.pallas_call(
        apply_kernel,
        out_shape=[sds(master.shape, f32)] + [sds((3, SEGMENTS), f32)] * 3,
        in_specs=[SM] + [VM] * 4,
        out_specs=[VM] * 4,
        compiler_params=params(),
        name="apply_update",
    )(me, sums, jnp.asarray(bounds_table()), master, update)


def round_kernel(rows, counts, master, stem, selfb, classb, lines):
    tail = lines.shape[0] - rows
    for g, ref in enumerate((stem, selfb, classb)):
        lines[0:rows, :] = master[g : g + 1, :].reshape(rows, LANES)
        count = counts[0, 0] + counts[0, 1] if g == 2 else 0
        lines[rows:, :] = jnp.full((tail, LANES), count, jnp.int32).astype(f32)
        ref[0] = lines[...].astype(bf16)


def round_shards(counts, master, rows, padded_rows):
    return pl.pallas_call(
        functools.partial(round_kernel, rows),
        out_shape=[sds((1, padded_rows, LANES), bf16)] * 3,
        in_specs=[SM, VM],
        out_specs=[VM] * 3,
        scratch_shapes=[pltpu.VMEM((padded_rows, LANES), f32)],
        compiler_params=params(),
        name="round_shards",
    )(counts, master)


def weight_kernel(rows, me_ref, bounds, master, sums_o):
    sums_o[...] = jnp.zeros_like(sums_o)
    for g in range(3):
        part = master[g : g + 1, :].reshape(rows, LANES)
        sums_o[g : g + 1, :] = segment_sums(part * part, g, me_ref[0] * rows, bounds)


def weight_sums(me, master, rows):
    return pl.pallas_call(
        functools.partial(weight_kernel, rows),
        out_shape=sds((8, LANES), f32),
        in_specs=[SM, VM, VM],
        out_specs=VM,
        compiler_params=params(),
        name="weight_sums",
    )(me, jnp.asarray(bounds_table()), master)


def on_device(
    master,
    first_moment,
    second_moment,
    patches_small,
    patches_large,
    labels_small,
    labels_large,
    counts,
    step,
):
    rows = master.shape[1] // LANES
    padded_rows = -(-(rows + 1) // 16) * 16
    n_dp, n_z = lax.axis_size("dp"), lax.axis_size("fsdp")
    z_bits, bits = log2(n_z), log2(n_dp) + log2(n_z)
    devices = n_dp * n_z
    half, quarter = devices // 2, devices // 4
    assert row_of(0, 7) + CLASS_PAD // LANES <= half * rows
    assert row_of(1, 6) <= quarter * rows <= row_of(1, 6) + 64
    ns, valid, _ = patches_small.shape
    nl = patches_large.shape[0]
    padded = -(-valid // 16) * 16
    small_per = 2 if ns % 2 == 0 else 1
    me = lax.axis_index(AXES).astype(jnp.int32).reshape(1)
    me_half = jnp.bitwise_and(me, half - 1)
    me_quarter = jnp.bitwise_and(me, quarter - 1)
    dp = lax.axis_index("dp")
    n_quarter = n_dp // 4
    in_half, quarter_id = dp < n_dp // 2, dp // n_quarter

    core, second, top = z_bits, bits - 2, bits - 1
    inner = list(range(core + 1, second))
    arrays = lambda state: ([a for a, _ in state], [r for _, r in state])

    old_sums = weight_sums(me, master, rows)
    stem_shard, self_shard, class_shard = round_shards(counts, master, rows, padded_rows)
    up = n_dp // 2
    got = lax.ppermute(stem_shard, "dp", [(i, i + up) for i in range(up)])
    (got,) = tied((got,), old_sums)
    others = [lax.ppermute(self_shard, "dp", [(i, i ^ (a * n_quarter)) for i in range(n_dp)]) for a in (1, 2, 3)]
    stem_state = gather_z(jnp.where(in_half, stem_shard, got), [0])

    def of_quarter(b):
        value = self_shard
        for a in (1, 2, 3):
            value = jnp.where(quarter_id == (a ^ b), others[a - 1], value)
        return value

    first_state = gather_z(of_quarter(0), [0])
    rest = jnp.concatenate([of_quarter(b) for b in (1, 2, 3)], 0)
    for bit in inner:
        first_state = gather_bit(first_state, bit, z_bits)
    for bit in [*inner, second]:
        stem_state = gather_bit(stem_state, bit, z_bits)
    rest, class_shard, _ = lax.optimization_barrier((rest, class_shard, first_state[0][0]))
    first_state = gather_bit(first_state, core, z_bits)
    stem_state = gather_bit(stem_state, core, z_bits)
    class_all = lax.all_gather(class_shard[0], AXES, axis=0, tiled=False)

    patch_w, svec, pos_small, pos_large, head_w, head_b = stem = unpack_stem(
        me_half, *arrays(stem_state), rows, half, padded
    )
    wqkv, vec, pre_col, post_col, pre_row, post_row = unpack_low(me_quarter, *arrays(first_state), rows, quarter)
    tok, (qkv_s, qkv_l) = embed(
        patches_small, patches_large, patch_w, pos_small, pos_large, wqkv, vec, padded, []
    )
    att_s, lse_s = attend(qkv_s, pre_col, post_col, valid, small_per, 20e9, [])
    rest_state = gather_z(rest, [quarter, 2 * quarter, 3 * quarter], att_s)
    rest_all = rest_state[0][0]
    for bit in [*inner, core]:
        rest_state = gather_bit(rest_state, bit, z_bits)
    att_l, lse_l = attend(qkv_l, pre_col, post_col, qkv_l.shape[1], 1, 30e9, [rest_all, att_s])
    wo, w1, w2, vec_feed, c1 = unpack_feed(me_quarter, *arrays(first_state + rest_state), rows, devices)
    att = (att_s, att_l)
    branch, mid, act, slope, lower, out = feed(tok, att, (wo, w1, w2, vec_feed, c1), [])
    z_order = list(range(z_bits - 1, -1, -1))
    near_far = list(range(z_bits))
    class_order = [core, top, second] + inner + near_far
    feed_order = [core] + near_far + [top, second] + inner
    class_rels, feed_rels = slots_of(class_order), slots_of(feed_order)
    tail = padded_rows - rows + 8

    d_out_s, d_out_l, g_svec, g_head_w, g_head_b, loss, keep, send = class_step(
        me, jnp.zeros_like(me), [class_all], [list(range(devices))], class_rels, out, stem, counts, labels_small,
        labels_large, valid, rows, padded_rows,
    )
    class_chain = Chain(keep, send, class_order, z_bits)
    d_mid, (d_att_s, d_att_l), (g_wo, g_w1, g_w2, g_vec_feed, g_c1) = feed_back(
        ((d_out_s, d_out_l), mid, act, slope, lower, branch, att), (wo, w1, w2, vec_feed), [class_chain.send]
    )
    class_chain.step(d_att_s)
    quarter_rows = quarter * rows
    offset = -(-max(0, quarter_rows - row_of(0, 6)) // 8) * 8
    tiles = [pltpu.VMEM((8, D + 16, LANES), f32)]
    feed_chain = Chain(
        *pack(
            functools.partial(pack_feed_kernel, feed_rels, rows, offset, quarter_rows), "pack_feed", me,
            (g_wo, g_w1, g_w2, g_vec_feed, g_c1, g_head_w, g_head_b), feed_rels, padded_rows,
            offset + devices * rows + tail, tiles,
        ),
        feed_order, z_bits,
    )
    chains = (class_chain, feed_chain)
    mixes = (pre_col, post_col, pre_row, post_row)
    dq_s, pre_sum, post_sum = attend_back(
        qkv_s, d_att_s, lse_s, mixes, valid, 0, ns, small_per, 25e9, [chain.send for chain in chains]
    )
    part, dq_l = dq_s, []
    for i in range(nl):
        for chain in chains:
            chain.step(part)
        wait = [part] + [chain.send for chain in chains]
        part, pre_l, post_l = attend_back(qkv_l, d_att_l, lse_l, mixes, qkv_l.shape[1], i, 1, 1, 25e9, wait)
        dq_l.append(part)
        pre_sum, post_sum = pre_sum + pre_l, post_sum + post_l
    for chain in chains:
        chain.step(part)
    late_rels = slots_of([core] + inner + z_order)
    keep, send = embed_back(
        me_quarter, patches_small, patches_large, tok, dq_s, d_mid, dq_l, wqkv, vec,
        (pre_sum, post_sum, g_wo, g_svec, g_head_w), (late_rels, rows, quarter_rows), padded_rows,
        [chain.send for chain in chains],
    )
    for chain in chains:
        while not chain.done:
            chain.step(send)
    late_chain = Chain(keep, send, [core] + inner, z_bits, True)
    while not late_chain.done:
        late_chain.step()
    part = late_chain.total
    send = part.astype(bf16)
    for a in (1, 2, 3):
        got = lax.ppermute(send, "dp", [(i + a * n_quarter, i) for i in range(n_quarter)])
        part = part + got.astype(f32)
    head_part = lax.ppermute(feed_chain.total, "dp", [(i, i + n_quarter) for i in range(n_quarter)])
    first = quarter_id == 0
    grad_stem = jnp.where(first, part[:padded_rows], head_part)
    grad_self = jnp.where(first, part[padded_rows:], feed_chain.total)

    gradients, new_first, new_second, update, sums = adam(
        me, step, master, first_moment, second_moment, (grad_stem, grad_self, class_chain.total), rows
    )
    line = lax.broadcasted_iota(jnp.int32, (8, 1), 0)
    sums = sums + old_sums + jnp.where(line == 6, loss, 0.0)
    for bit in range(bits):
        sums = sums + exchange(sums, bit, z_bits)
    new_master, weight_norms, update_norms, trust_ratios = apply_update(me, sums, master, update)
    return sums[6, 0], gradients, new_first, new_second, new_master, weight_norms, update_norms, trust_ratios


def solution(mesh):
    return jax.shard_map(
        on_device,
        mesh=mesh,
        in_specs=(
            P(None, AXES),
            P(None, AXES),
            P(None, AXES),
            P(AXES, None, None),
            P(AXES, None, None),
            P(AXES),
            P(AXES),
            P(AXES, None),
            P(),
        ),
        out_specs=(
            P(),
            P(None, AXES),
            P(None, AXES),
            P(None, AXES),
            P(None, AXES),
            P(),
            P(),
            P(),
        ),
        check_vma=False,
    )
```

```python
import functools
import math

import jax
import jax.numpy as jnp
import numpy as np
from jax import lax
from jax.experimental import pallas as pl
from jax.experimental.pallas import tpu as pltpu
from jax.sharding import PartitionSpec as P

D = 384
HEADS = 8
WIDTH = D // HEADS
FF = 1536
CLASSES = 1000
CLASS_PAD = 1024
PATCH_IN = 768
GRID_SMALL = 14
GRID_LARGE = 24
LANES = 128
SEGMENTS = 16

LOG2E = 1.4426950408889634
SCALE = WIDTH**-0.5
NEG = -1e30
smooth = 0.1
beta_one = 0.9
beta_two = 0.999
adam_eps = 1e-06
decay_rate = 0.01
learn_rate = 0.3
norm_eps = 1e-06

f32 = jnp.float32
bf16 = jnp.bfloat16
AXES = ("dp", "fsdp")
VMEM_BYTES = 60 << 20


def shapes_of():
    dim = D
    tail = [(dim,), (dim,), (dim, FF), (FF,), (FF, dim), (dim,), (dim,)]
    stem = [
        (PATCH_IN, dim),
        (dim,),
        (GRID_SMALL * GRID_SMALL, dim),
        (dim,),
        (dim,),
        (dim,),
        (dim, CLASSES),
        (CLASSES,),
    ]
    selfb = [
        (dim,),
        (dim,),
        (dim, 3 * dim),
        (2 * dim,),
        (HEADS, HEADS),
        (HEADS, HEADS),
        (dim, dim),
        (dim,),
        (dim,),
    ] + tail
    classb = [
        (dim,),
        (dim,),
        (dim, dim),
        (dim,),
        (dim, 2 * dim),
        (dim,),
        (dim, dim),
        (dim,),
        (dim,),
    ] + tail
    return [stem, selfb, classb]


def segment_bounds():
    starts = np.zeros((3, SEGMENTS), np.int32)
    ends = np.zeros((3, SEGMENTS), np.int32)
    real = np.zeros((3, SEGMENTS), np.float32)
    for group, shapes in enumerate(shapes_of()):
        offset = 0
        for number, shape in enumerate(shapes):
            count = int(np.prod(shape))
            starts[group, number] = offset
            ends[group, number] = offset + count
            real[group, number] = 1.0
            offset += count
    return starts, ends, real


STARTS, ENDS, REAL = segment_bounds()


def row_of(group, number):
    return int(STARTS[group, number]) // LANES


def rows_used(group):
    return -(-int(ENDS[group].max()) // LANES)


def resize_table():
    rows = np.arange(GRID_LARGE).astype(np.float32) * np.float32((GRID_SMALL - 1) / (GRID_LARGE - 1))
    cols = np.arange(GRID_SMALL).astype(np.float32)
    line = np.maximum(np.float32(0.0), np.float32(1.0) - np.abs(rows[:, None] - cols[None, :]))
    return (line[:, None, :, None] * line[None, :, None, :]).reshape(GRID_LARGE**2, GRID_SMALL**2)


def nn(a, b):
    return lax.dot_general(a, b, (((1,), (0,)), ((), ())), preferred_element_type=f32)


def nt(a, b):
    return lax.dot_general(a, b, (((1,), (1,)), ((), ())), preferred_element_type=f32)


def tn(a, b):
    return lax.dot_general(a, b, (((0,), (0,)), ((), ())), preferred_element_type=f32)


def colsum(value):
    return jnp.sum(value, 0, keepdims=True)


def split(value):
    high = value.astype(bf16)
    return high, (value - high.astype(f32)).astype(bf16)


def stats(value):
    centred = value - jnp.mean(value, -1, keepdims=True)
    inverse = lax.rsqrt(jnp.mean(centred * centred, -1, keepdims=True) + 1e-06)
    return centred * inverse, inverse


def norm_back(d_out, unit, inverse, gain):
    inner = d_out * gain
    first = jnp.mean(inner, -1, keepdims=True)
    second = jnp.mean(inner * unit, -1, keepdims=True)
    return inverse * (inner - first - unit * second)


def gelu_pair(upper):
    cdf = 0.5 * (1.0 + lax.erf(upper * (0.5**0.5)))
    density = jnp.exp(-0.5 * upper * upper) * 0.3989422804014327
    return upper * cdf, cdf + upper * density


def head_mask(rows):
    lane = lax.broadcasted_iota(jnp.int32, (rows, D), 1)
    row = lax.broadcasted_iota(jnp.int32, (rows, D), 0)
    return (lane // WIDTH) == lax.rem(row, HEADS)


VM = pl.BlockSpec(memory_space=pltpu.VMEM)
SM = pl.BlockSpec(memory_space=pltpu.SMEM)


def params(**kw):
    return pltpu.CompilerParams(vmem_limit_bytes=VMEM_BYTES, **kw)


def sds(shape, dtype):
    return jax.ShapeDtypeStruct(shape, dtype)


def call(kernel, args, after, in_specs, **kw):
    n, m = len(args), len(after)

    def wrapped(*refs):
        kernel(*refs[:n], *refs[n + m :])

    specs = list(in_specs) + [pl.BlockSpec(memory_space=pl.ANY)] * m
    return pl.pallas_call(wrapped, in_specs=specs, compiler_params=params(), **kw)(*args, *after)


def log2(n):
    return n.bit_length() - 1


def exchange(value, bit, z_bits):
    if bit < z_bits:
        n = lax.axis_size("fsdp")
        return lax.ppermute(value, "fsdp", [(i, i ^ (1 << bit)) for i in range(n)])
    n = lax.axis_size("dp")
    return lax.ppermute(value, "dp", [(i, i ^ (1 << (bit - z_bits))) for i in range(n)])


def exchange_z(value, k):
    n = lax.axis_size("fsdp")
    return lax.ppermute(value, "fsdp", [(i, i ^ k) for i in range(n)])


def tied(values, after):
    if after is None:
        return values
    return lax.optimization_barrier((*values, after))[:-1]


def gather_z(value, rel, after=None):
    n = lax.axis_size("fsdp")
    got = tied([exchange_z(value, k) for k in range(1, n)], after)
    return [(jnp.concatenate([value, *got], 0), [r | k for k in range(n) for r in rel])]


def gather_bit(state, bit, z_bits, after=None):
    got = tied([exchange(a, bit, z_bits) for a, _ in state], after)
    return state + [(a, [r | (1 << bit) for r in rel]) for a, (_, rel) in zip(got, state)]


def put_matrix(flat, row, out_ref, rows, cols):
    step = cols // LANES
    for j in range(step):
        out_ref[:, LANES * j : LANES * (j + 1)] = flat[pl.ds(row + j, rows, stride=step), :].astype(bf16)


def put_row(flat, row, out_ref, at, cols):
    for j in range(cols // LANES):
        out_ref[at : at + 1, LANES * j : LANES * (j + 1)] = flat[row + j : row + j + 1, :]


def fill_flat(me, piece_refs, rels, rows, flat):
    for ref, rel in zip(piece_refs, rels):
        for k, r in enumerate(rel):
            flat[pl.ds(rows * jnp.bitwise_xor(me, r), rows), :] = ref[k].astype(f32)[0:rows]


def unpack_stem_kernel(rels, rows, me_ref, resize_ref, *refs):
    n = len(rels)
    pieces, (patch_w, vec, pos_small, pos_large, head_w, head_b), (flat, tiles) = refs[:n], refs[n : n + 6], refs[n + 6 :]
    fill_flat(me_ref[0], pieces, rels, rows, flat)
    put_matrix(flat, row_of(0, 0), patch_w, PATCH_IN, D)
    vec[...] = jnp.zeros_like(vec)
    for at, number in enumerate((1, 3, 4, 5)):
        put_row(flat, row_of(0, number), vec, at, D)
    bias = vec[0:1, :]
    small = GRID_SMALL**2
    pos_small[...] = jnp.zeros_like(pos_small)
    for j in range(D // LANES):
        pos_small[0:small, LANES * j : LANES * (j + 1)] = flat[pl.ds(row_of(0, 2) + j, small, stride=D // LANES), :]
    pos_large[...] = (
        lax.dot_general(
            resize_ref[...], pos_small[...], (((1,), (0,)), ((), ())),
            preferred_element_type=f32, precision=lax.Precision.HIGHEST,
        )
        + bias
    )
    pos_small[...] += bias
    lane = lax.broadcasted_iota(jnp.int32, (24, LANES), 1)
    base = row_of(0, 6)
    for rho in range(16):
        first, shift = (CLASSES * rho) // LANES, (CLASSES * rho) % LANES
        parts = [flat[pl.ds(base + first + t, 24, stride=125), :] for t in range(9)]
        if shift:
            parts = [pltpu.roll(p, LANES - shift, 1) for p in parts]
        for t in range(8):
            value = jnp.where(lane < LANES - shift, parts[t], parts[t + 1]) if shift else parts[t]
            if t == 7:
                value = jnp.where(lane < CLASSES - 7 * LANES, value, 0.0)
            tiles[t, pl.ds(rho, 24, stride=16), :] = value
    for t in range(8):
        head_w[:, LANES * t : LANES * (t + 1)] = tiles[t, 0:D, :].astype(bf16)
    put_row(flat, row_of(0, 7), head_b, 0, CLASS_PAD)


def unpack_stem(me, pieces, rels, rows, count, padded):
    resize = np.zeros((GRID_LARGE**2, padded), np.float32)
    resize[:, : GRID_SMALL**2] = resize_table()
    return pl.pallas_call(
        functools.partial(unpack_stem_kernel, rels, rows),
        out_shape=[
            sds((PATCH_IN, D), bf16),
            sds((8, D), f32),
            sds((padded, D), f32),
            sds((GRID_LARGE**2, D), f32),
            sds((D, CLASS_PAD), bf16),
            sds((1, CLASS_PAD), f32),
        ],
        in_specs=[SM] + [VM] * (1 + len(pieces)),
        out_specs=[VM] * 6,
        scratch_shapes=[pltpu.VMEM((count * rows, LANES), f32), pltpu.VMEM((8, D + 16, LANES), f32)],
        compiler_params=params(),
        name="unpack_stem",
    )(me, jnp.asarray(resize), *pieces)


SG1, SB1, SBQ, SBV, SBO, SLS1, SG2, SB2, SC2, SLS2 = range(10)
CG1, CB1, CBQ, CBV, CBO, CLS1, CG2, CB2, CC2, CLS2 = range(10)


def unpack_low_kernel(rels, rows, me_ref, *refs):
    n = len(rels)
    pieces = refs[:n]
    wqkv, vec, pre_col, post_col, pre_row, post_row, flat = refs[n:]
    fill_flat(me_ref[0], pieces, rels, rows, flat)
    put_matrix(flat, row_of(1, 2), wqkv, D, 3 * D)
    vec[...] = jnp.zeros_like(vec)
    bq = row_of(1, 3)
    for at, row in ((SG1, row_of(1, 0)), (SB1, row_of(1, 1)), (SBQ, bq), (SBV, bq + D // LANES)):
        put_row(flat, row, vec, at, D)
    mix = jnp.broadcast_to(flat[row_of(1, 4) : row_of(1, 4) + 1, :], (HEADS, LANES))
    lane = lax.broadcasted_iota(jnp.int32, (HEADS, LANES), 1)
    row = lax.broadcasted_iota(jnp.int32, (HEADS, LANES), 0)
    pick_pre = jnp.where((lane < 64) & (lane // HEADS == row), mix, 0.0).astype(bf16)
    pick_post = jnp.where((lane >= 64) & (lane % HEADS == row), mix, 0.0).astype(bf16)
    table_lane = lax.broadcasted_iota(jnp.int32, (LANES, D), 0)
    table_col = lax.broadcasted_iota(jnp.int32, (LANES, D), 1) // WIDTH
    spread_pre = jnp.where(table_lane % HEADS == table_col, 1.0, 0.0).astype(bf16)
    spread_post = jnp.where((table_lane - 64) // HEADS == table_col, 1.0, 0.0).astype(bf16)
    factor = SCALE * LOG2E
    pre_row[...] = nn(pick_pre, spread_pre) * factor
    post_row[...] = nn(pick_post, spread_post)
    column = lambda a, b: lax.dot_general(a, b, (((0,), (1,)), ((), ())), preferred_element_type=f32)
    pre_col[...] = column(spread_pre, pick_pre) * factor
    post_col[...] = column(spread_post, pick_post)


def unpack_low(me, pieces, rels, rows, count):
    return pl.pallas_call(
        functools.partial(unpack_low_kernel, rels, rows),
        out_shape=[
            sds((D, 3 * D), bf16),
            sds((16, D), f32),
            sds((D, HEADS), f32),
            sds((D, HEADS), f32),
            sds((HEADS, D), f32),
            sds((HEADS, D), f32),
        ],
        in_specs=[SM] + [VM] * len(pieces),
        out_specs=[VM] * 6,
        scratch_shapes=[pltpu.VMEM((count * rows, LANES), f32)],
        compiler_params=params(),
        name="unpack_low",
    )(me, *pieces)


def unpack_feed_kernel(rels, rows, me_ref, *refs):
    n = len(rels)
    pieces = refs[:n]
    wo, w1, w2, vec, c1, flat = refs[n:]
    fill_flat(me_ref[0], pieces, rels, rows, flat)
    put_matrix(flat, row_of(1, 6), wo, D, D)
    put_matrix(flat, row_of(1, 11), w1, D, FF)
    put_matrix(flat, row_of(1, 13), w2, FF, D)
    vec[...] = jnp.zeros_like(vec)
    for at, number in ((SBO, 7), (SLS1, 8), (SG2, 9), (SB2, 10), (SC2, 14), (SLS2, 15)):
        put_row(flat, row_of(1, number), vec, at, D)
    put_row(flat, row_of(1, 12), c1, 0, FF)


def unpack_feed(me, pieces, rels, rows, count):
    return pl.pallas_call(
        functools.partial(unpack_feed_kernel, rels, rows),
        out_shape=[
            sds((D, D), bf16),
            sds((D, FF), bf16),
            sds((FF, D), bf16),
            sds((16, D), f32),
            sds((1, FF), f32),
        ],
        in_specs=[SM] + [VM] * len(pieces),
        out_specs=[VM] * 5,
        scratch_shapes=[pltpu.VMEM((count * rows, LANES), f32)],
        compiler_params=params(),
        name="unpack_feed",
    )(me, *pieces)


def unpack_class_kernel(rels, rows, me_ref, *refs):
    n = len(rels)
    pieces = refs[:n]
    wq, wkv, wo, w1, w2, vec, c1, total, flat = refs[n:]
    fill_flat(me_ref[0], pieces, rels, rows, flat)
    put_matrix(flat, row_of(2, 2), wq, D, D)
    put_matrix(flat, row_of(2, 4), wkv, D, 2 * D)
    put_matrix(flat, row_of(2, 6), wo, D, D)
    put_matrix(flat, row_of(2, 11), w1, D, FF)
    put_matrix(flat, row_of(2, 13), w2, FF, D)
    vec[...] = jnp.zeros_like(vec)
    for at, number in (
        (CG1, 0), (CB1, 1), (CBQ, 3), (CBV, 5), (CBO, 7), (CLS1, 8), (CG2, 9), (CB2, 10), (CC2, 14), (CLS2, 15),
    ):
        put_row(flat, row_of(2, number), vec, at, D)
    put_row(flat, row_of(2, 12), c1, 0, FF)
    count = jnp.zeros((1, LANES), f32)
    for ref, rel in zip(pieces, rels):
        for k in range(len(rel)):
            count = count + ref[k].astype(f32)[rows : rows + 1, :]
    total[...] = count


def const_spec(a):
    return pl.BlockSpec(a.shape, lambda i, nd=len(a.shape): (0,) * nd, pipeline_mode=pl.Buffered(1))


def cost(flops, read):
    return pl.CostEstimate(flops=int(flops), bytes_accessed=int(read), transcendentals=0)


class Steps:
    def __init__(self, ns, nl, padded, large_len):
        self.count = math.gcd(ns, nl)
        self.small, self.large = ns // self.count, nl // self.count
        self.padded, self.large_len = padded, large_len
        self.split = self.small * padded
        self.rows = self.split + self.large * large_len
        self.grid = (self.count,)

    def specs(self, cols):
        index = lambda i: (i, 0, 0)
        return [
            pl.BlockSpec((self.small, self.padded, cols), index),
            pl.BlockSpec((self.large, self.large_len, cols), index),
        ]

    def shapes(self, cols, kind):
        n = self.count
        return [sds((n * self.small, self.padded, cols), kind), sds((n * self.large, self.large_len, cols), kind)]

    def join(self, pair):
        cols = pair[0].shape[-1]
        return jnp.concatenate([ref[...].reshape(-1, cols) for ref in pair], 0)

    def put(self, pair, value):
        cols = value.shape[-1]
        pair[0][...] = value[: self.split].reshape(self.small, self.padded, cols)
        pair[1][...] = value[self.split :].reshape(self.large, self.large_len, cols)


def embed_kernel(steps, valid, ps, plg, patch_w, pos_small, pos_large, wqkv, vec, *outs):
    tok_o, qkv_o, tokens = outs[:2], outs[2:4], outs[4]
    row = lambda at: vec[at : at + 1, :]
    for i in range(steps.small):
        base = steps.padded * i
        tokens[base : base + steps.padded, :] = pos_small[...]
        tokens[base : base + valid, :] += nn(ps[i], patch_w[...])
    for i in range(steps.large):
        base = steps.split + steps.large_len * i
        tokens[base : base + steps.large_len, :] = nn(plg[i], patch_w[...]) + pos_large[...]
    tok = tokens[...]
    steps.put(tok_o, tok)
    unit, _ = stats(tok)
    a1 = (unit * row(SG1) + row(SB1)).astype(bf16)
    bias = jnp.concatenate([row(SBQ), jnp.zeros((1, D), f32), row(SBV)], 1)
    steps.put(qkv_o, (nn(a1, wqkv[...]) + bias).astype(bf16))


def embed(ps, plg, patch_w, pos_small, pos_large, wqkv, vec, padded, after):
    ns, valid, _ = ps.shape
    nl, large_len, _ = plg.shape
    steps = Steps(ns, nl, padded, large_len)
    weights = (patch_w, pos_small, pos_large, wqkv, vec)
    index = lambda i: (i, 0, 0)
    out = call(
        functools.partial(embed_kernel, steps, valid),
        (ps, plg, *weights),
        after,
        grid=steps.grid,
        out_shape=steps.shapes(D, f32) + steps.shapes(3 * D, bf16),
        in_specs=[
            pl.BlockSpec((steps.small, valid, PATCH_IN), index),
            pl.BlockSpec((steps.large, large_len, PATCH_IN), index),
        ]
        + [const_spec(a) for a in weights],
        out_specs=steps.specs(D) + steps.specs(3 * D),
        scratch_shapes=[pltpu.VMEM((steps.rows, D), f32)],
        cost_estimate=cost(12e9, 20e6),
        name="embed",
    )
    return out[:2], out[2:]


def attend_kernel(valid, qkv_ref, pre_col, post_col, att_ref, lse_ref, q_t, kk, v_t, acc):
    per, length = qkv_ref.shape[0], qkv_ref.shape[1]
    for i in range(per):
        q_t[i] = qkv_ref[i, :, 0:D].astype(f32).T
        kk[i, :, 0:D] = qkv_ref[i, :, D : 2 * D]
        kk[i, :, D:] = qkv_ref[i, :, D : 2 * D]
        v_t[i] = qkv_ref[i, :, 2 * D :].astype(f32).T.astype(bf16)
    for g in range(HEADS):
        pre, post = pre_col[:, g : g + 1], post_col[:, g : g + 1]
        for i in range(per):
            high, low = split(q_t[i] * pre)
            mixed = nn(kk[i], jnp.concatenate([high, low], 0))
            if valid < length:
                mixed = jnp.where(lax.broadcasted_iota(jnp.int32, mixed.shape, 0) < valid, mixed, NEG)
            top = jnp.max(mixed, 0, keepdims=True)
            raw = jnp.exp2(mixed - top)
            weight = colsum(raw)
            lse_ref[i, g : g + 1, :] = top + jnp.log2(weight)
            part = nn(v_t[i], raw.astype(bf16)) * post * (1.0 / weight)
            acc[i] = part if g == 0 else acc[i] + part
    for i in range(per):
        att_ref[i] = acc[i].T.astype(bf16)


def attend(qkv, pre_col, post_col, valid, per, flops, after):
    n, length, _ = qkv.shape
    spec = lambda *tail: pl.BlockSpec((per,) + tail, lambda i: (i, 0, 0))
    return call(
        functools.partial(attend_kernel, valid),
        (qkv, pre_col, post_col),
        after,
        grid=(n // per,),
        out_shape=[sds((n, length, D), bf16), sds((n, HEADS, length), f32)],
        in_specs=[spec(length, 3 * D), const_spec(pre_col), const_spec(post_col)],
        out_specs=[spec(length, D), spec(HEADS, length)],
        scratch_shapes=[
            pltpu.VMEM((per, D, length), f32),
            pltpu.VMEM((per, length, 2 * D), bf16),
            pltpu.VMEM((per, D, length), bf16),
            pltpu.VMEM((per, D, length), f32),
        ],
        cost_estimate=cost(flops, 10e6),
        name="attend",
    )


def feed_kernel(steps, tok_s, tok_l, att_s, att_l, wo, w1, w2, vec, c1, *outs):
    branch_o, mid_o, act_o, slope_o, lower_o, out_o = [outs[2 * i : 2 * i + 2] for i in range(6)]
    row = lambda at: vec[at : at + 1, :]
    branch = nn(steps.join((att_s, att_l)), wo[...]) + row(SBO)
    steps.put(branch_o, branch.astype(bf16))
    mid = steps.join((tok_s, tok_l)) + row(SLS1) * branch
    steps.put(mid_o, mid)
    unit, _ = stats(mid)
    n2 = (unit * row(SG2) + row(SB2)).astype(bf16)
    act, slope = gelu_pair(nn(n2, w1[...]) + c1[...])
    act = act.astype(bf16)
    steps.put(act_o, act)
    steps.put(slope_o, slope.astype(bf16))
    lower = nn(act, w2[...]) + row(SC2)
    steps.put(lower_o, lower.astype(bf16))
    steps.put(out_o, mid + row(SLS2) * lower)


FEED_OUT = [(D, bf16), (D, f32), (FF, bf16), (FF, bf16), (D, bf16), (D, f32)]


def feed(tok, att, weights, after):
    (ns, padded, _), (nl, large_len, _) = tok[0].shape, tok[1].shape
    steps = Steps(ns, nl, padded, large_len)
    out = call(
        functools.partial(feed_kernel, steps),
        (*tok, *att, *weights),
        after,
        grid=steps.grid,
        out_shape=[shape for entry in FEED_OUT for shape in steps.shapes(*entry)],
        in_specs=steps.specs(D) * 2 + [const_spec(a) for a in weights],
        out_specs=[spec for cols, _ in FEED_OUT for spec in steps.specs(cols)],
        cost_estimate=cost(20e9, 30e6),
        name="feed",
    )
    return [out[2 * i : 2 * i + 2] for i in range(6)]


BATCH = 8


def class_kernel(
    ns, nl, valid, out_s, out_l, wq, wkv, wo, w1, w2, vec, c1, svec, head_w, head_b, total, counts, labels_s, labels_l,
    d_s, d_l, g_wq, g_wkv, g_wo, g_w1, g_w2, g_vec, g_c1, g_svec, g_head_w, g_head_b, loss_o,
    a_s, a_l, p_s, p_l, z_ref, y_ref, b_ref, ps_ref, pc_ref, da_ref,
):
    row = lambda at: vec[at : at + 1, :]
    mask8 = head_mask(HEADS)
    mask64 = head_mask(HEADS * BATCH)
    cls = svec[1:2, :]
    unit_cls, inv_cls = stats(cls)
    a_cls = (unit_cls * row(CG1) + row(CB1)).astype(bf16)
    a_cls_f = a_cls.astype(f32)
    query = (nn(a_cls, wq[...]) + row(CBQ)).astype(bf16).astype(f32)
    q_diag = jnp.where(mask8, query, 0.0).astype(bf16)
    u_nat = nt(q_diag, wkv[:, 0:D]) * SCALE
    u_hi, u_lo = split(u_nat * LOG2E)
    u16 = jnp.concatenate([u_hi, u_lo], 0)
    s_cls = jnp.sum(u_nat * LOG2E * a_cls_f, -1, keepdims=True)
    z_ref[...] = jnp.zeros_like(z_ref)
    ps_ref[...] = jnp.zeros_like(ps_ref)

    def forward(i, src, a_ref, p_ref, slot):
        unit, _ = stats(src[i])
        a = (unit * row(CG1) + row(CB1)).astype(bf16)
        a_ref[i] = a
        s16 = nt(u16, a)
        s = s16[0:HEADS] + s16[HEADS:]
        keep = valid if a.shape[0] != GRID_LARGE**2 else a.shape[0]
        if keep < a.shape[0]:
            s = jnp.where(lax.broadcasted_iota(jnp.int32, s.shape, 1) < keep, s, NEG)
        top = jnp.maximum(jnp.max(s, -1, keepdims=True), s_cls)
        e = jnp.exp2(s - top)
        e_cls = jnp.exp2(s_cls - top)
        inverse = 1.0 / (jnp.sum(e, -1, keepdims=True) + e_cls)
        p, p_cls = e * inverse, e_cls * inverse
        p_ref[i] = p
        low, low_cls = p.astype(bf16), p_cls.astype(bf16).astype(f32)
        z_ref[pl.ds(slot * HEADS, HEADS), :] = nn(low, a) + low_cls * a_cls_f
        ps_ref[pl.ds(slot * HEADS, HEADS), :] = jnp.sum(low.astype(f32), -1, keepdims=True) + low_cls
        pc_ref[pl.ds(slot * HEADS, HEADS), :] = p_cls

    for i in range(ns):
        forward(i, out_s, a_s, p_s, i)
    for i in range(nl):
        forward(i, out_l, a_l, p_l, ns + i)

    z_hi, z_lo = split(z_ref[...])
    o_all = nn(jnp.concatenate([z_hi, z_lo], 0), wkv[:, D:])
    o_all = o_all[0 : HEADS * BATCH] + o_all[HEADS * BATCH :] + ps_ref[...] * row(CBV)
    att = jnp.sum(jnp.where(mask64, o_all, 0.0).reshape(BATCH, HEADS, D), 1).astype(bf16)
    branch = nn(att, wo[...]) + row(CBO)
    mid = cls + row(CLS1) * branch
    unit_mid, inv_mid = stats(mid)
    n2 = (unit_mid * row(CG2) + row(CB2)).astype(bf16)
    upper = nn(n2, w1[...]) + c1[...]
    act, slope = gelu_pair(upper)
    act = act.astype(bf16)
    lower = nn(act, w2[...]) + row(CC2)
    c_tok = mid + row(CLS2) * lower
    unit_c, inv_c = stats(c_tok)
    final = (unit_c * svec[2:3, :] + svec[3:4, :]).astype(bf16)
    logits = nn(final, head_w[...]) + head_b[...]
    lane = lax.broadcasted_iota(jnp.int32, logits.shape, 1)
    inside = lane < CLASSES
    logits = jnp.where(inside, logits, NEG)
    shifted = logits - jnp.max(logits, -1, keepdims=True)
    raw = jnp.exp(shifted)
    weight = jnp.sum(raw, -1, keepdims=True)
    logp = shifted - jnp.log(weight)
    image = lax.broadcasted_iota(jnp.int32, (BATCH, 1), 0)
    label = jnp.zeros((BATCH, 1), jnp.int32)
    for i in range(ns):
        label = jnp.where(image == i, labels_s[i], label)
    for i in range(nl):
        label = jnp.where(image == ns + i, labels_l[i], label)
    alive = ((image < ns) & (image < counts[0, 0])) | ((image >= ns) & (image - ns < counts[0, 1]))
    hit = lane == label
    picked = jnp.sum(jnp.where(hit, logp, 0.0), -1, keepdims=True)
    mean = jnp.sum(jnp.where(inside, logp, 0.0), -1, keepdims=True) * (1.0 / CLASSES)
    each = -((1.0 - smooth) * picked + smooth * mean)
    scaled = jnp.where(alive, 1.0, 0.0) / total[0:1, 0:1]
    loss_o[...] = jnp.broadcast_to(colsum(scaled * each), loss_o.shape)
    target = jnp.where(hit, 1.0 - smooth, 0.0) + smooth / CLASSES
    d_logits = jnp.where(inside, scaled * (raw / weight - target), 0.0).astype(bf16)

    d_final = nt(d_logits, head_w[...])
    g_head_w[...] = tn(final, d_logits)
    g_head_b[...] = colsum(d_logits.astype(f32))
    g_svec[...] = jnp.zeros_like(g_svec)
    g_svec[2:3, :] = colsum(d_final * unit_c)
    g_svec[3:4, :] = colsum(d_final)
    d_c = norm_back(d_final, unit_c, inv_c, svec[2:3, :])
    g_vec[...] = jnp.zeros_like(g_vec)
    g_vec[CLS2 : CLS2 + 1, :] = colsum(d_c * lower)
    d_lower = (d_c * row(CLS2)).astype(bf16)
    g_vec[CC2 : CC2 + 1, :] = colsum(d_lower.astype(f32))
    g_w2[...] = tn(act, d_lower)
    d_upper = (slope * nt(d_lower, w2[...])).astype(bf16)
    g_c1[...] = colsum(d_upper.astype(f32))
    g_w1[...] = tn(n2, d_upper)
    d_n2 = nt(d_upper, w1[...])
    g_vec[CG2 : CG2 + 1, :] = colsum(d_n2 * unit_mid)
    g_vec[CB2 : CB2 + 1, :] = colsum(d_n2)
    d_mid = d_c + norm_back(d_n2, unit_mid, inv_mid, row(CG2))
    g_vec[CLS1 : CLS1 + 1, :] = colsum(d_mid * branch)
    d_branch = (d_mid * row(CLS1)).astype(bf16)
    g_vec[CBO : CBO + 1, :] = colsum(d_branch.astype(f32))
    g_wo[...] = tn(att, d_branch)
    d_att = nt(d_branch, wo[...]).astype(bf16).astype(f32)
    d_diag = jnp.where(mask64, jnp.broadcast_to(d_att[:, None, :], (BATCH, HEADS, D)).reshape(BATCH * HEADS, D), 0.0)
    g_vec[CBV : CBV + 1, :] = colsum(d_diag * ps_ref[...])
    shift = jnp.sum(d_diag * row(CBV), -1, keepdims=True)
    d_diag_low = d_diag.astype(bf16)
    y_ref[...] = nt(d_diag_low, wkv[:, D:])
    g_wkv[:, D:] = tn(jnp.concatenate([z_hi, z_lo], 0), jnp.concatenate([d_diag_low, d_diag_low], 0))
    z_ref[:, 0:1] = shift
    b_ref[...] = jnp.zeros_like(b_ref)
    da_ref[...] = jnp.zeros_like(da_ref)
    un_hi, un_lo = split(u_nat)

    def backward(i, src, a_ref, p_ref, d_ref, slot):
        unit, inverse = stats(src[i])
        a = a_ref[i]
        here = pl.ds(slot * HEADS, HEADS)
        y = y_ref[here, :]
        y_hi, y_lo = split(y)
        d16 = nt(jnp.concatenate([y_hi, y_lo], 0), a)
        offset = z_ref[here, 0:1]
        d_p = d16[0:HEADS] + d16[HEADS:] + offset
        d_p_cls = jnp.sum(y * a_cls_f, -1, keepdims=True) + offset
        p, p_cls = p_ref[i], pc_ref[here, :]
        delta = jnp.sum(p * d_p, -1, keepdims=True) + p_cls * d_p_cls
        d_score = (p * (d_p - delta)).astype(bf16)
        d_score_cls = (p_cls * (d_p_cls - delta)).astype(bf16).astype(f32)
        low = p.astype(bf16)
        b_ref[...] += nn(d_score, a) + d_score_cls * a_cls_f
        da_ref[...] += d_score_cls * u_nat + p_cls.astype(bf16).astype(f32) * y
        left = jnp.concatenate([d_score.astype(f32), d_score.astype(f32), low.astype(f32), low.astype(f32)], 0)
        d_a = tn(left.astype(bf16), jnp.concatenate([un_hi, un_lo, y_hi, y_lo], 0))
        g_vec[CG1 : CG1 + 1, :] += colsum(d_a * unit)
        g_vec[CB1 : CB1 + 1, :] += colsum(d_a)
        d_ref[i] = norm_back(d_a, unit, inverse, row(CG1))

    for i in range(ns):
        backward(i, out_s, a_s, p_s, d_s, i)
    for i in range(nl):
        backward(i, out_l, a_l, p_l, d_l, ns + i)

    b_hi, b_lo = split(b_ref[...])
    bw = nn(jnp.concatenate([b_hi, b_lo], 0), wkv[:, 0:D])
    bw = bw[0:HEADS] + bw[HEADS:]
    d_query = (colsum(jnp.where(mask8, bw, 0.0)) * SCALE).astype(bf16)
    g_vec[CBQ : CBQ + 1, :] = d_query.astype(f32)
    q_scaled = q_diag.astype(f32) * SCALE
    qs_hi, qs_lo = split(q_scaled)
    g_wkv[:, 0:D] = tn(
        jnp.concatenate([b_hi, b_hi, b_lo, b_lo], 0), jnp.concatenate([qs_hi, qs_lo, qs_hi, qs_lo], 0)
    )
    first = lax.broadcasted_iota(jnp.int32, (16, D), 0) == 0
    spread_a = jnp.where(first, jnp.broadcast_to(a_cls_f, (16, D)), 0.0).astype(bf16)
    spread_q = jnp.where(first, jnp.broadcast_to(d_query.astype(f32), (16, D)), 0.0).astype(bf16)
    g_wq[...] = tn(spread_a, spread_q)
    d_a_cls = colsum(da_ref[...]) + nt(d_query, wq[...])
    g_vec[CG1 : CG1 + 1, :] += d_a_cls * unit_cls
    g_vec[CB1 : CB1 + 1, :] += d_a_cls
    g_svec[1:2, :] = colsum(d_mid) + norm_back(d_a_cls, unit_cls, inv_cls, row(CG1))


CLASS_WEIGHTS = [(D, D), (D, 2 * D), (D, D), (D, FF), (FF, D)]


def class_step_kernel(ns, nl, valid, unpack_rels, pack_rels, rows, n, me_ref, from_ref, counts, labels_s, labels_l, *refs):
    pieces, (out_s, out_l, svec, head_w, head_b), refs = refs[:n], refs[n : n + 5], refs[n + 5 :]
    (d_s, d_l, g_svec, g_head_w, g_head_b, loss, keep, send), refs = refs[:8], refs[8:]
    weights, total, grads, flat, work = refs[:7], refs[7], refs[8:15], refs[15], refs[16:]
    unpack_class_kernel(unpack_rels, rows, from_ref, *pieces, *weights, total, flat)
    class_kernel(
        ns, nl, valid, out_s, out_l, *weights, svec, head_w, head_b, total, counts, labels_s, labels_l,
        d_s, d_l, *grads, g_svec, g_head_w, g_head_b, loss, *work,
    )
    pack_class_kernel(pack_rels, rows, me_ref, *grads, keep, send, flat)


def class_step(me, unpack_me, pieces, unpack_rels, pack_rels, out, stem, counts, labels_s, labels_l, valid, rows, padded_rows):
    (ns, padded, _), (nl, large_len, _) = out[0].shape, out[1].shape
    _, svec, _, _, head_w, head_b = stem
    args = (me, unpack_me, counts, labels_s, labels_l, *pieces, *out, svec, head_w, head_b)
    half = len(pack_rels) // 2
    vectors = [pltpu.VMEM((16, D), f32), pltpu.VMEM((1, FF), f32)]
    return pl.pallas_call(
        functools.partial(
            class_step_kernel, ns, nl, valid, unpack_rels, pack_rels, rows, len(pieces)
        ),
        out_shape=[
            sds((ns, padded, D), f32),
            sds((nl, large_len, D), f32),
            sds((8, D), f32),
            sds((D, CLASS_PAD), f32),
            sds((1, CLASS_PAD), f32),
            sds((1, LANES), f32),
            sds((half, padded_rows, LANES), bf16),
            sds((half, padded_rows, LANES), bf16),
        ],
        in_specs=[SM] * 5 + [VM] * (len(args) - 5),
        out_specs=[VM] * 8,
        scratch_shapes=[pltpu.VMEM(shape, bf16) for shape in CLASS_WEIGHTS]
        + vectors
        + [pltpu.VMEM((1, LANES), f32)]
        + [pltpu.VMEM(shape, f32) for shape in CLASS_WEIGHTS]
        + vectors
        + [
            pltpu.VMEM((len(pack_rels) * rows + padded_rows - rows + 8, LANES), f32),
            pltpu.VMEM((ns, padded, D), bf16),
            pltpu.VMEM((nl, large_len, D), bf16),
            pltpu.VMEM((ns, HEADS, padded), f32),
            pltpu.VMEM((nl, HEADS, large_len), f32),
            pltpu.VMEM((BATCH * HEADS, D), f32),
            pltpu.VMEM((BATCH * HEADS, D), f32),
            pltpu.VMEM((HEADS, D), f32),
            pltpu.VMEM((BATCH * HEADS, 1), f32),
            pltpu.VMEM((BATCH * HEADS, 1), f32),
            pltpu.VMEM((HEADS, D), f32),
        ],
        compiler_params=params(),
        cost_estimate=cost(25e9, 40e6),
        name="class_step",
    )(*args)


def feed_back_kernel(steps, *refs):
    ins, (wo, w1, w2, vec), refs = [refs[2 * i : 2 * i + 2] for i in range(7)], refs[14:18], refs[18:]
    d_mid_o, d_att_o, sums = refs[:2], refs[2:4], refs[4:]
    g_wo, g_w1, g_w2, g_vec, g_c1 = sums
    row = lambda at: vec[at : at + 1, :]

    @pl.when(pl.program_id(0) == 0)
    def _():
        for ref in sums:
            ref[...] = jnp.zeros_like(ref)

    def add(at, value):
        g_vec[at : at + 1, :] += value

    d_out_r, mid_r, act_r, slope_r, lower_r, branch_r, att_r = ins
    d_out = steps.join(d_out_r)
    add(SLS2, colsum(d_out * steps.join(lower_r).astype(f32)))
    d_lower = (d_out * row(SLS2)).astype(bf16)
    add(SC2, colsum(d_lower.astype(f32)))
    unit, inverse = stats(steps.join(mid_r))
    n2 = (unit * row(SG2) + row(SB2)).astype(bf16)
    g_w2[...] += tn(steps.join(act_r), d_lower)
    d_upper = (nt(d_lower, w2[...]) * steps.join(slope_r).astype(f32)).astype(bf16)
    g_w1[...] += tn(n2, d_upper)
    g_c1[...] += colsum(d_upper.astype(f32))
    d_n2 = nt(d_upper, w1[...])
    add(SG2, colsum(d_n2 * unit))
    add(SB2, colsum(d_n2))
    d_mid = d_out + norm_back(d_n2, unit, inverse, row(SG2))
    steps.put(d_mid_o, d_mid)
    add(SLS1, colsum(d_mid * steps.join(branch_r).astype(f32)))
    d_branch = (d_mid * row(SLS1)).astype(bf16)
    add(SBO, colsum(d_branch.astype(f32)))
    g_wo[...] += tn(steps.join(att_r), d_branch)
    steps.put(d_att_o, nt(d_branch, wo[...]).astype(bf16))


def sum_specs(shapes):
    return [pl.BlockSpec(s.shape, lambda i: (0, 0), pipeline_mode=pl.Buffered(1)) for s in shapes]


def feed_back(pairs, weights, after):
    (ns, padded, _), (nl, large_len, _) = pairs[0][0].shape, pairs[0][1].shape
    steps = Steps(ns, nl, padded, large_len)
    sums = [sds((D, D), f32), sds((D, FF), f32), sds((FF, D), f32), sds((16, D), f32), sds((1, FF), f32)]
    out = call(
        functools.partial(feed_back_kernel, steps),
        (*[a for pair in pairs for a in pair], *weights),
        after,
        grid=steps.grid,
        out_shape=steps.shapes(D, f32) + steps.shapes(D, bf16) + sums,
        in_specs=[spec for pair in pairs for spec in steps.specs(pair[0].shape[2])] + [const_spec(a) for a in weights],
        out_specs=steps.specs(D) * 2 + sum_specs(sums),
        cost_estimate=cost(35e9, 30e6),
        name="feed_back",
    )
    return out[:2], out[2:4], out[4:]


def attend_back_kernel(valid, qkv_ref, d_att_ref, lse_ref, pre_col, post_col, pre_row, post_row, d_qkv_ref, g_pre, g_post,
                       q_t, kk, k_t, do_t, dq_t, d_k, d_v):
    per, length = qkv_ref.shape[0], qkv_ref.shape[1]
    for i in range(per):
        q_t[i] = qkv_ref[i, :, 0:D].astype(f32).T
        kk[i, :, 0:D] = qkv_ref[i, :, D : 2 * D]
        kk[i, :, D:] = qkv_ref[i, :, D : 2 * D]
        k_t[i] = qkv_ref[i, :, D : 2 * D].astype(f32).T.astype(bf16)
        do_t[i] = d_att_ref[i].astype(f32).T

    @pl.when(pl.program_id(0) == 0)
    def _():
        g_pre[...] = jnp.zeros_like(g_pre)
        g_post[...] = jnp.zeros_like(g_post)

    for g in range(HEADS):
        pre, post = pre_col[:, g : g + 1], post_col[:, g : g + 1]
        for i in range(per):
            q, k, v = qkv_ref[i, :, 0:D], qkv_ref[i, :, D : 2 * D], qkv_ref[i, :, 2 * D :]
            high, low = split(q_t[i] * pre)
            mixed = nn(kk[i], jnp.concatenate([high, low], 0))
            d_p = nn(v, (do_t[i] * post).astype(bf16))
            p = jnp.exp2(mixed - lse_ref[i, g : g + 1, :])
            if valid < length:
                p = jnp.where(lax.broadcasted_iota(jnp.int32, p.shape, 0) < valid, p, 0.0)
            delta = colsum(p * d_p)
            d_mixed = (p * (d_p - delta)).astype(bf16)
            r = nn(p.astype(bf16), d_att_ref[i])
            t = nn(d_mixed, q)
            u = nn(k_t[i], d_mixed)
            d_v_part, d_k_part, d_q_part = r * post_row[g : g + 1, :], t * pre_row[g : g + 1, :], u * pre
            d_v[i] = d_v_part if g == 0 else d_v[i] + d_v_part
            d_k[i] = d_k_part if g == 0 else d_k[i] + d_k_part
            dq_t[i] = d_q_part if g == 0 else dq_t[i] + d_q_part
            g_post[g : g + 1, :] += colsum(r * v.astype(f32))
            g_pre[g : g + 1, :] += colsum(t * k.astype(f32))
    inverse = 1.0 / LOG2E
    for i in range(per):
        d_qkv_ref[i, :, 0:D] = (dq_t[i].T * inverse).astype(bf16)
        d_qkv_ref[i, :, D : 2 * D] = (d_k[i] * inverse).astype(bf16)
        d_qkv_ref[i, :, 2 * D :] = d_v[i].astype(bf16)


def attend_back(qkv, d_att, lse, mixes, valid, first, count, per, flops, after):
    length = qkv.shape[1]
    spec = lambda *tail: pl.BlockSpec((per,) + tail, lambda i: (i + first // per, 0, 0))
    sums = [sds((HEADS, D), f32)] * 2
    return call(
        functools.partial(attend_back_kernel, valid),
        (qkv, d_att, lse, *mixes),
        after,
        grid=(count // per,),
        out_shape=[sds((count, length, 3 * D), bf16)] + sums,
        in_specs=[spec(length, 3 * D), spec(length, D), spec(HEADS, length)] + [const_spec(a) for a in mixes],
        out_specs=[pl.BlockSpec((per, length, 3 * D), lambda i: (i, 0, 0))] + sum_specs(sums),
        scratch_shapes=[
            pltpu.VMEM((per, D, length), f32),
            pltpu.VMEM((per, length, 2 * D), bf16),
            pltpu.VMEM((per, D, length), bf16),
            pltpu.VMEM((per, D, length), f32),
            pltpu.VMEM((per, D, length), f32),
            pltpu.VMEM((per, length, D), f32),
            pltpu.VMEM((per, length, D), f32),
        ],
        cost_estimate=cost(flops, 10e6),
        name="attend_back",
    )


def embed_back_kernel(steps, valid, late, me_ref, ps, plg, resize, *refs):
    tok_r, dq_s, d_mid_r, refs = refs[:2], refs[2], refs[3:5], refs[5:]
    n = steps.large * steps.count
    dq_l, (wqkv, vec, pre, post, g_wo, g_svec, g_head_w), refs = refs[:n], refs[n : n + 7], refs[n + 7 :]
    (keep, send), sums, (d_qkv, flat, tiles) = refs[:2], refs[2:8], refs[8:]
    g_wqkv, g_vec, g_patch_w, g_patch_b, g_pos, pos_large = sums
    row = lambda at: vec[at : at + 1, :]
    step = pl.program_id(0)

    @pl.when(step == 0)
    def _():
        for ref in sums:
            ref[...] = jnp.zeros_like(ref)

    d_qkv[: steps.split, :] = dq_s[...].reshape(steps.split, 3 * D)
    for k in range(steps.count):

        @pl.when(step == k)
        def _(k=k):
            for i in range(steps.large):
                base = steps.split + steps.large_len * i
                d_qkv[base : base + steps.large_len, :] = dq_l[k * steps.large + i][0]

    def add(at, value):
        g_vec[at : at + 1, :] += value

    add(SBQ, colsum(d_qkv[:, 0:D].astype(f32)))
    add(SBV, colsum(d_qkv[:, 2 * D :].astype(f32)))
    unit, inverse = stats(steps.join(tok_r))
    a1 = (unit * row(SG1) + row(SB1)).astype(bf16)
    g_wqkv[...] += tn(a1, d_qkv[...])
    d_a1 = nt(d_qkv[...], wqkv[...])
    add(SG1, colsum(d_a1 * unit))
    add(SB1, colsum(d_a1))
    d_tok = steps.join(d_mid_r) + norm_back(d_a1, unit, inverse, row(SG1))
    g_patch_b[0:1, :] += colsum(d_tok)
    for i in range(steps.small):
        mine = d_tok[steps.padded * i : steps.padded * i + valid, :]
        g_pos[...] += mine
        g_patch_w[...] += tn(ps[i], mine.astype(bf16))
    for i in range(steps.large):
        base = steps.split + steps.large_len * i
        mine = d_tok[base : base + steps.large_len, :]
        pos_large[...] += mine
        g_patch_w[...] += tn(plg[i], mine.astype(bf16))

    @pl.when(step == steps.count - 1)
    def _():
        g_pos[...] += lax.dot_general(
            resize[...], pos_large[...], (((1,), (0,)), ((), ())),
            preferred_element_type=f32, precision=lax.Precision.HIGHEST,
        )
        pack_late_kernel(
            *late, me_ref, g_wqkv, g_vec, pre, post, g_wo, g_patch_w, g_patch_b, g_pos, g_svec, g_head_w,
            keep, send, flat, tiles,
        )


def embed_back(me, ps, plg, tok, dq_s, d_mid, dq_l, wqkv, vec, others, late, padded_rows, after):
    ns, valid, _ = ps.shape
    nl, large_len, _ = plg.shape
    steps = Steps(ns, nl, tok[0].shape[1], large_len)
    resize = jnp.asarray(resize_table().T.copy())
    sums = [
        sds((D, 3 * D), f32),
        sds((16, D), f32),
        sds((PATCH_IN, D), f32),
        sds((8, D), f32),
        sds((valid, D), f32),
    ]
    index = lambda i: (i, 0, 0)
    half = len(late[0]) // 2
    outs = [sds((half, 2 * padded_rows, LANES), f32), sds((half, 2 * padded_rows, LANES), bf16)]
    return call(
        functools.partial(embed_back_kernel, steps, valid, late),
        (me, ps, plg, resize, *tok, dq_s, *d_mid, *dq_l, wqkv, vec, *others),
        after,
        grid=steps.grid,
        out_shape=outs,
        in_specs=[
            SM,
            pl.BlockSpec((steps.small, valid, PATCH_IN), index),
            pl.BlockSpec((steps.large, large_len, PATCH_IN), index),
            const_spec(resize),
            *steps.specs(D),
            steps.specs(3 * D)[0],
            *steps.specs(D),
        ]
        + [const_spec(a) for a in (*dq_l, wqkv, vec, *others)],
        out_specs=[const_spec(a) for a in outs],
        scratch_shapes=[pltpu.VMEM(a.shape, f32) for a in sums]
        + [
            pltpu.VMEM((large_len, D), f32),
            pltpu.VMEM((steps.rows, 3 * D), bf16),
            pltpu.VMEM((row_of(0, 6) + 1280, LANES), f32),
            pltpu.VMEM((8, D + 16, LANES), f32),
        ],
        cost_estimate=cost(20e9, 30e6),
        name="embed_back",
    )


def take_matrix(flat, row, src, rows, cols):
    step = cols // LANES
    for j in range(step):
        flat[pl.ds(row + j, rows, stride=step), :] = src[0:rows, LANES * j : LANES * (j + 1)]


def take_row(flat, row, src, at, cols):
    for j in range(cols // LANES):
        flat[row + j : row + j + 1, :] = src[at : at + 1, LANES * j : LANES * (j + 1)]


def slots_of(order):
    rels = [0]
    for bit in reversed(order):
        rels = rels + [r | (1 << bit) for r in rels]
    return rels


def emit_slots(me, flat, rows, rels, keep_ref, send_ref, offset=0):
    half = len(rels) // 2
    for k, r in enumerate(rels):
        value = flat[pl.ds(offset + rows * jnp.bitwise_xor(me, r), keep_ref.shape[1]), :]
        if k < half:
            keep_ref[k] = value.astype(keep_ref.dtype)
        else:
            send_ref[k - half] = value.astype(bf16)


def pack_class_kernel(rels, rows, me_ref, wq, wkv, wo, w1, w2, vec, c1, keep, send, flat):
    used = rows_used(2)
    flat[used:, :] = jnp.zeros((flat.shape[0] - used, LANES), f32)
    take_matrix(flat, row_of(2, 2), wq, D, D)
    take_matrix(flat, row_of(2, 4), wkv, D, 2 * D)
    take_matrix(flat, row_of(2, 6), wo, D, D)
    take_matrix(flat, row_of(2, 11), w1, D, FF)
    take_matrix(flat, row_of(2, 13), w2, FF, D)
    for at, number in (
        (CG1, 0), (CB1, 1), (CBQ, 3), (CBV, 5), (CBO, 7), (CLS1, 8), (CG2, 9), (CB2, 10), (CC2, 14), (CLS2, 15),
    ):
        take_row(flat, row_of(2, number), vec, at, D)
    take_row(flat, row_of(2, 12), c1, 0, FF)
    emit_slots(me_ref[0], flat, rows, rels, keep, send)


def take_head(flat, base, head_w, head_b, tiles, groups):
    for t in range(8):
        tiles[t, 0:D, :] = head_w[:, LANES * t : LANES * (t + 1)]
    lane = lax.broadcasted_iota(jnp.int32, (groups, LANES), 1)
    for rho in range(16):
        first, shift = (CLASSES * rho) // LANES, (CLASSES * rho) % LANES
        parts = [tiles[t, pl.ds(rho, groups, stride=16), :] for t in range(8)]
        if shift:
            parts = [pltpu.roll(p, shift, 1) for p in parts]
        for t in range(9 if shift + CLASSES > CLASS_PAD else 8):
            if shift:
                value = jnp.where(lane >= shift, parts[t] if t < 8 else 0.0, parts[t - 1] if t > 0 else 0.0)
            else:
                value = parts[t]
            here = pl.ds(base + first + t, groups, stride=125)
            flat[here, :] = flat[here, :] + value
    if head_b is not None:
        take_row(flat, base + row_of(0, 7) - row_of(0, 6), head_b, 0, CLASS_PAD)


HEAD_GROUPS = D // 16


def pack_feed_kernel(rels, rows, offset, quarter_rows, me_ref, wo, w1, w2, vec, c1, head_w, head_b, keep, send, flat, tiles):
    used, first = rows_used(1), row_of(1, 6)
    flat[0 : offset + first, :] = jnp.zeros((offset + first, LANES), f32)
    flat[offset + used :, :] = jnp.zeros((flat.shape[0] - used - offset, LANES), f32)
    take_head(flat, offset + row_of(0, 6) - quarter_rows, head_w, head_b, tiles, HEAD_GROUPS)
    boundary = quarter_rows - first
    flat[offset + first : offset + quarter_rows, :] = jnp.zeros((boundary, LANES), f32)
    take_matrix(flat, offset + first, wo, D, D)
    flat[offset + first : offset + quarter_rows, :] = jnp.zeros((boundary, LANES), f32)
    take_matrix(flat, offset + row_of(1, 11), w1, D, FF)
    take_matrix(flat, offset + row_of(1, 13), w2, FF, D)
    for at, number in ((SBO, 7), (SLS1, 8), (SG2, 9), (SB2, 10), (SC2, 14), (SLS2, 15)):
        take_row(flat, offset + row_of(1, number), vec, at, D)
    take_row(flat, offset + row_of(1, 12), c1, 0, FF)
    emit_slots(me_ref[0], flat, rows, rels, keep, send, offset)


def pack_late_kernel(
    rels, rows, quarter_rows, me_ref, wqkv, vec, pre, post, wo, patch_w, patch_b, pos, svec, head_w, keep, send, flat, tiles
):
    padded_rows = keep.shape[1] // 2
    for g in range(2):
        pack_late_group(g, quarter_rows, wqkv, vec, pre, post, wo, patch_w, patch_b, pos, svec, head_w, flat, tiles)
        here = pl.ds(g * padded_rows, padded_rows)
        emit_slots(me_ref[0], flat, rows, rels, keep.at[:, here], send.at[:, here])


def pack_late_group(g, quarter_rows, wqkv, vec, pre, post, wo, patch_w, patch_b, pos, svec, head_w, flat, tiles):
    if g == 0:
        first = row_of(0, 6)
        flat[first:, :] = jnp.zeros((flat.shape[0] - first, LANES), f32)
        take_matrix(flat, row_of(0, 0), patch_w, PATCH_IN, D)
        take_row(flat, row_of(0, 1), patch_b, 0, D)
        take_matrix(flat, row_of(0, 2), pos, GRID_SMALL**2, D)
        for at, number in ((1, 3), (2, 4), (3, 5)):
            take_row(flat, row_of(0, number), svec, at, D)
        take_head(flat, first, head_w, None, tiles, 8)
        return
    first = row_of(1, 6)
    take_matrix(flat, row_of(1, 2), wqkv, D, 3 * D)
    take_matrix(flat, first, wo, 24, D)
    bq = row_of(1, 3)
    for at, row in ((SG1, row_of(1, 0)), (SB1, row_of(1, 1)), (SBQ, bq), (SBV, bq + D // LANES)):
        take_row(flat, row, vec, at, D)
    table_col = lax.broadcasted_iota(jnp.int32, (D, LANES), 0) // WIDTH
    table_lane = lax.broadcasted_iota(jnp.int32, (D, LANES), 1)
    lane = lax.broadcasted_iota(jnp.int32, (HEADS, LANES), 1)
    row = lax.broadcasted_iota(jnp.int32, (HEADS, LANES), 0)
    exact = lambda a, b: lax.dot_general(
        a, b, (((1,), (0,)), ((), ())), preferred_element_type=f32, precision=lax.Precision.HIGHEST
    )
    sum_pre = exact(pre[...], jnp.where(table_lane % HEADS == table_col, 1.0, 0.0))
    sum_post = exact(post[...], jnp.where((table_lane - 64) // HEADS == table_col, 1.0, 0.0))
    line = colsum(jnp.where((lane < 64) & (lane // HEADS == row), sum_pre * SCALE, 0.0))
    line = line + colsum(jnp.where((lane >= 64) & (lane % HEADS == row), sum_post, 0.0))
    flat[row_of(1, 4) : row_of(1, 4) + 1, :] = line


def pack(kernel, name, me, arrays, rels, padded_rows, flat_rows, extra=()):
    half = len(rels) // 2
    return pl.pallas_call(
        kernel,
        out_shape=[sds((half, padded_rows, LANES), bf16)] * 2,
        in_specs=[SM] + [VM] * len(arrays),
        out_specs=[VM] * 2,
        scratch_shapes=[pltpu.VMEM((flat_rows, LANES), f32), *extra],
        compiler_params=params(),
        name=name,
    )(me, *arrays)


class Chain:
    def __init__(self, keep, send, order, z_bits, z_last=False):
        self.keep, self.send, self.order, self.z_bits, self.z_last = keep, send, list(order), z_bits, z_last
        self.total = None
        self.done = False

    def finish(self, total):
        self.total = self.send = total
        self.done = True

    def step(self, after=None):
        if self.order:
            (got,) = tied((exchange(self.send, self.order.pop(0), self.z_bits),), after)
            half = got.shape[0] // 2 if self.order else 1
            kept = self.keep[:half].astype(f32) + got[:half].astype(f32)
            if half == got.shape[0]:
                self.finish(kept[0])
                return
            passed = (self.keep[half:].astype(f32) + got[half:].astype(f32)).astype(bf16)
            self.keep, self.send = (kept, passed) if self.order else (kept[0], passed)
        elif not self.done:
            got = [exchange_z(self.send[k - 1], k) for k in range(1, self.send.shape[0] + 1)]
            total = self.keep
            for part in tied(tuple(got), after):
                total = total + part.astype(f32)
            self.finish(total)


def bounds_table():
    table = np.zeros((8, LANES), np.int32)
    table[0:3, :SEGMENTS] = STARTS // 64
    table[3:6, :SEGMENTS] = -(-ENDS // 64)
    return table


def pick(group, values):
    return jnp.where(group == 0, values[0], jnp.where(group == 1, values[1], values[2]))


def segment_sums(square, group, first_row, bounds):
    rows = square.shape[0]
    lane = lax.broadcasted_iota(jnp.int32, (rows, LANES), 1)
    left = jnp.sum(jnp.where(lane < 64, square, 0.0), -1, keepdims=True)
    right = jnp.sum(jnp.where(lane < 64, 0.0, square), -1, keepdims=True)
    place = 2 * (first_row + lax.broadcasted_iota(jnp.int32, (rows, LANES), 0))
    low, high = bounds[group : group + 1, :], bounds[3 + group : 4 + group, :]
    one = jnp.where((place >= low) & (place < high), left, 0.0)
    two = jnp.where((place + 1 >= low) & (place + 1 < high), right, 0.0)
    return colsum(one + two)


def adam_kernel(rows, me_ref, step_ref, bounds, master, first, second, g0, g1, g2, grad_o, first_o, second_o, update_o, sums_o):
    shard = rows * LANES
    for g, ref in enumerate((g0, g1, g2)):
        grad_o[g : g + 1, :] = ref[0:rows, :].reshape(1, shard)
    grad = grad_o[...]
    weight = master[...]
    new_first = beta_one * first[...] + (1.0 - beta_one) * grad
    new_second = beta_two * second[...] + (1.0 - beta_two) * grad * grad
    first_o[...] = new_first
    second_o[...] = new_second
    power = jnp.full((1, LANES), step_ref[0], jnp.int32).astype(f32)
    scale_one = (1.0 / (1.0 - jnp.power(f32(beta_one), power)))[:, 0:1]
    scale_two = (1.0 / (1.0 - jnp.power(f32(beta_two), power)))[:, 0:1]
    update = new_first * scale_one / (jnp.sqrt(new_second * scale_two) + adam_eps) + decay_rate * weight
    update_o[...] = update
    sums_o[...] = jnp.zeros_like(sums_o)
    first_row = me_ref[0] * rows
    for g in range(3):
        part = update_o[g : g + 1, :].reshape(rows, LANES)
        sums_o[3 + g : 4 + g, :] = segment_sums(part * part, g, first_row, bounds)


def adam(me, step, master, first, second, grads, rows):
    shape = master.shape
    return pl.pallas_call(
        functools.partial(adam_kernel, rows),
        out_shape=[sds(shape, f32)] * 4 + [sds((8, LANES), f32)],
        in_specs=[SM, SM] + [VM] * 7,
        out_specs=[VM] * 5,
        compiler_params=params(),
        name="adam",
    )(me, step, jnp.asarray(bounds_table()), master, first, second, *grads)


def apply_kernel(me_ref, sums, bounds, master, update, new_o, weight_o, norm_o, trust_o):
    shard = master.shape[1]
    roots = jnp.sqrt(sums[...])
    weight_norms, update_norms = roots[0:3, :], roots[3:6, :]
    lane = lax.broadcasted_iota(jnp.int32, (3, LANES), 1)
    group3 = lax.broadcasted_iota(jnp.int32, (3, LANES), 0)
    used = pick(group3, [int(REAL[g].sum()) for g in range(3)])
    trust = jnp.where(lane < used, weight_norms / (update_norms + norm_eps), 1.0)
    weight_o[...] = weight_norms[:, 0:SEGMENTS]
    norm_o[...] = update_norms[:, 0:SEGMENTS]
    trust_o[...] = trust[:, 0:SEGMENTS]
    rows = shard // LANES
    place = 2 * (me_ref[0] * rows + lax.broadcasted_iota(jnp.int32, (rows, LANES), 0))
    lane = lax.broadcasted_iota(jnp.int32, (rows, LANES), 1)
    for g in range(3):
        low, high, mine = bounds[g : g + 1, :], bounds[3 + g : 4 + g, :], trust[g : g + 1, :]
        left = jnp.sum(jnp.where((place >= low) & (place < high), mine, 0.0), -1, keepdims=True)
        right = jnp.sum(jnp.where((place + 1 >= low) & (place + 1 < high), mine, 0.0), -1, keepdims=True)
        ratio = jnp.where(lane < 64, left, right).reshape(1, shard)
        new_o[g : g + 1, :] = master[g : g + 1, :] - learn_rate * ratio * update[g : g + 1, :]


def apply_update(me, sums, master, update):
    return pl.pallas_call(
        apply_kernel,
        out_shape=[sds(master.shape, f32)] + [sds((3, SEGMENTS), f32)] * 3,
        in_specs=[SM] + [VM] * 4,
        out_specs=[VM] * 4,
        compiler_params=params(),
        name="apply_update",
    )(me, sums, jnp.asarray(bounds_table()), master, update)


def round_kernel(rows, counts, master, stem, selfb, classb, lines):
    tail = lines.shape[0] - rows
    for g, ref in enumerate((stem, selfb, classb)):
        lines[0:rows, :] = master[g : g + 1, :].reshape(rows, LANES)
        count = counts[0, 0] + counts[0, 1] if g == 2 else 0
        lines[rows:, :] = jnp.full((tail, LANES), count, jnp.int32).astype(f32)
        ref[0] = lines[...].astype(bf16)


def round_shards(counts, master, rows, padded_rows):
    return pl.pallas_call(
        functools.partial(round_kernel, rows),
        out_shape=[sds((1, padded_rows, LANES), bf16)] * 3,
        in_specs=[SM, VM],
        out_specs=[VM] * 3,
        scratch_shapes=[pltpu.VMEM((padded_rows, LANES), f32)],
        compiler_params=params(),
        name="round_shards",
    )(counts, master)


def weight_kernel(rows, me_ref, bounds, master, sums_o):
    sums_o[...] = jnp.zeros_like(sums_o)
    for g in range(3):
        part = master[g : g + 1, :].reshape(rows, LANES)
        sums_o[g : g + 1, :] = segment_sums(part * part, g, me_ref[0] * rows, bounds)


def weight_sums(me, master, rows):
    return pl.pallas_call(
        functools.partial(weight_kernel, rows),
        out_shape=sds((8, LANES), f32),
        in_specs=[SM, VM, VM],
        out_specs=VM,
        compiler_params=params(),
        name="weight_sums",
    )(me, jnp.asarray(bounds_table()), master)


def on_device(
    master,
    first_moment,
    second_moment,
    patches_small,
    patches_large,
    labels_small,
    labels_large,
    counts,
    step,
):
    rows = master.shape[1] // LANES
    padded_rows = -(-(rows + 1) // 16) * 16
    n_dp, n_z = lax.axis_size("dp"), lax.axis_size("fsdp")
    z_bits, bits = log2(n_z), log2(n_dp) + log2(n_z)
    devices = n_dp * n_z
    half, quarter = devices // 2, devices // 4
    assert row_of(0, 7) + CLASS_PAD // LANES <= half * rows
    assert row_of(1, 6) <= quarter * rows <= row_of(1, 6) + 64
    ns, valid, _ = patches_small.shape
    nl = patches_large.shape[0]
    padded = -(-valid // 16) * 16
    small_per = 2 if ns % 2 == 0 else 1
    me = lax.axis_index(AXES).astype(jnp.int32).reshape(1)
    me_half = jnp.bitwise_and(me, half - 1)
    me_quarter = jnp.bitwise_and(me, quarter - 1)
    dp = lax.axis_index("dp")
    n_quarter = n_dp // 4
    in_half, quarter_id = dp < n_dp // 2, dp // n_quarter

    core, second, top = z_bits, bits - 2, bits - 1
    inner = list(range(core + 1, second))
    arrays = lambda state: ([a for a, _ in state], [r for _, r in state])

    old_sums = weight_sums(me, master, rows)
    stem_shard, self_shard, class_shard = round_shards(counts, master, rows, padded_rows)
    up = n_dp // 2
    got = lax.ppermute(stem_shard, "dp", [(i, i + up) for i in range(up)])
    (got,) = tied((got,), old_sums)
    others = [lax.ppermute(self_shard, "dp", [(i, i ^ (a * n_quarter)) for i in range(n_dp)]) for a in (1, 2, 3)]
    stem_state = gather_z(jnp.where(in_half, stem_shard, got), [0])

    def of_quarter(b):
        value = self_shard
        for a in (1, 2, 3):
            value = jnp.where(quarter_id == (a ^ b), others[a - 1], value)
        return value

    first_state = gather_z(of_quarter(0), [0])
    rest = jnp.concatenate([of_quarter(b) for b in (1, 2, 3)], 0)
    for bit in inner:
        first_state = gather_bit(first_state, bit, z_bits)
    for bit in [*inner, second]:
        stem_state = gather_bit(stem_state, bit, z_bits)
    rest, class_shard, _ = lax.optimization_barrier((rest, class_shard, first_state[0][0]))
    first_state = gather_bit(first_state, core, z_bits)
    stem_state = gather_bit(stem_state, core, z_bits)
    class_all = lax.all_gather(class_shard[0], AXES, axis=0, tiled=False)

    patch_w, svec, pos_small, pos_large, head_w, head_b = stem = unpack_stem(
        me_half, *arrays(stem_state), rows, half, padded
    )
    wqkv, vec, pre_col, post_col, pre_row, post_row = unpack_low(me_quarter, *arrays(first_state), rows, quarter)
    tok, (qkv_s, qkv_l) = embed(
        patches_small, patches_large, patch_w, pos_small, pos_large, wqkv, vec, padded, []
    )
    att_s, lse_s = attend(qkv_s, pre_col, post_col, valid, small_per, 20e9, [])
    rest_state = gather_z(rest, [quarter, 2 * quarter, 3 * quarter], att_s)
    rest_all = rest_state[0][0]
    for bit in [*inner, core]:
        rest_state = gather_bit(rest_state, bit, z_bits)
    att_l, lse_l = attend(qkv_l, pre_col, post_col, qkv_l.shape[1], 1, 30e9, [rest_all, att_s])
    wo, w1, w2, vec_feed, c1 = unpack_feed(me_quarter, *arrays(first_state + rest_state), rows, devices)
    att = (att_s, att_l)
    branch, mid, act, slope, lower, out = feed(tok, att, (wo, w1, w2, vec_feed, c1), [])
    z_order = list(range(z_bits - 1, -1, -1))
    near_far = list(range(z_bits))
    class_order = [core, top, second] + inner + near_far
    feed_order = [core] + near_far + [top, second] + inner
    class_rels, feed_rels = slots_of(class_order), slots_of(feed_order)
    tail = padded_rows - rows + 8

    d_out_s, d_out_l, g_svec, g_head_w, g_head_b, loss, keep, send = class_step(
        me, jnp.zeros_like(me), [class_all], [list(range(devices))], class_rels, out, stem, counts, labels_small,
        labels_large, valid, rows, padded_rows,
    )
    class_chain = Chain(keep, send, class_order, z_bits)
    d_mid, (d_att_s, d_att_l), (g_wo, g_w1, g_w2, g_vec_feed, g_c1) = feed_back(
        ((d_out_s, d_out_l), mid, act, slope, lower, branch, att), (wo, w1, w2, vec_feed), [class_chain.send]
    )
    class_chain.step(d_att_s)
    quarter_rows = quarter * rows
    offset = -(-max(0, quarter_rows - row_of(0, 6)) // 8) * 8
    tiles = [pltpu.VMEM((8, D + 16, LANES), f32)]
    feed_chain = Chain(
        *pack(
            functools.partial(pack_feed_kernel, feed_rels, rows, offset, quarter_rows), "pack_feed", me,
            (g_wo, g_w1, g_w2, g_vec_feed, g_c1, g_head_w, g_head_b), feed_rels, padded_rows,
            offset + devices * rows + tail, tiles,
        ),
        feed_order, z_bits,
    )
    chains = (class_chain, feed_chain)
    mixes = (pre_col, post_col, pre_row, post_row)
    dq_s, pre_sum, post_sum = attend_back(
        qkv_s, d_att_s, lse_s, mixes, valid, 0, ns, small_per, 25e9, [chain.send for chain in chains]
    )
    part, dq_l = dq_s, []
    for i in range(nl):
        for chain in chains:
            chain.step(part)
        wait = [part] + [chain.send for chain in chains]
        part, pre_l, post_l = attend_back(qkv_l, d_att_l, lse_l, mixes, qkv_l.shape[1], i, 1, 1, 25e9, wait)
        dq_l.append(part)
        pre_sum, post_sum = pre_sum + pre_l, post_sum + post_l
    for chain in chains:
        chain.step(part)
    late_rels = slots_of([core] + inner + z_order)
    keep, send = embed_back(
        me_quarter, patches_small, patches_large, tok, dq_s, d_mid, dq_l, wqkv, vec,
        (pre_sum, post_sum, g_wo, g_svec, g_head_w), (late_rels, rows, quarter_rows), padded_rows,
        [chain.send for chain in chains],
    )
    for chain in chains:
        while not chain.done:
            chain.step(send)
    late_chain = Chain(keep, send, [core] + inner, z_bits, True)
    while not late_chain.done:
        late_chain.step()
    part = late_chain.total
    send = part.astype(bf16)
    for a in (1, 2, 3):
        got = lax.ppermute(send, "dp", [(i + a * n_quarter, i) for i in range(n_quarter)])
        part = part + got.astype(f32)
    head_part = lax.ppermute(feed_chain.total, "dp", [(i, i + n_quarter) for i in range(n_quarter)])
    first = quarter_id == 0
    grad_stem = jnp.where(first, part[:padded_rows], head_part)
    grad_self = jnp.where(first, part[padded_rows:], feed_chain.total)

    gradients, new_first, new_second, update, sums = adam(
        me, step, master, first_moment, second_moment, (grad_stem, grad_self, class_chain.total), rows
    )
    line = lax.broadcasted_iota(jnp.int32, (8, 1), 0)
    sums = sums + old_sums + jnp.where(line == 6, loss, 0.0)
    for bit in range(bits):
        sums = sums + exchange(sums, bit, z_bits)
    new_master, weight_norms, update_norms, trust_ratios = apply_update(me, sums, master, update)
    return sums[6, 0], gradients, new_first, new_second, new_master, weight_norms, update_norms, trust_ratios


def solution(mesh):
    return jax.shard_map(
        on_device,
        mesh=mesh,
        in_specs=(
            P(None, AXES),
            P(None, AXES),
            P(None, AXES),
            P(AXES, None, None),
            P(AXES, None, None),
            P(AXES),
            P(AXES),
            P(AXES, None),
            P(),
        ),
        out_specs=(
            P(),
            P(None, AXES),
            P(None, AXES),
            P(None, AXES),
            P(None, AXES),
            P(),
            P(),
            P(),
        ),
        check_vma=False,
    )
```

```python
import functools
import math

import jax
import jax.numpy as jnp
import numpy as np
from jax import lax
from jax.experimental import pallas as pl
from jax.experimental.pallas import tpu as pltpu
from jax.sharding import PartitionSpec as P

D = 384
HEADS = 8
WIDTH = D // HEADS
FF = 1536
CLASSES = 1000
CLASS_PAD = 1024
PATCH_IN = 768
GRID_SMALL = 14
GRID_LARGE = 24
LANES = 128
SEGMENTS = 16

LOG2E = 1.4426950408889634
SCALE = WIDTH**-0.5
NEG = -1e30
smooth = 0.1
beta_one = 0.9
beta_two = 0.999
adam_eps = 1e-06
decay_rate = 0.01
learn_rate = 0.3
norm_eps = 1e-06

f32 = jnp.float32
bf16 = jnp.bfloat16
AXES = ("dp", "fsdp")
VMEM_BYTES = 60 << 20


def shapes_of():
    dim = D
    tail = [(dim,), (dim,), (dim, FF), (FF,), (FF, dim), (dim,), (dim,)]
    stem = [
        (PATCH_IN, dim),
        (dim,),
        (GRID_SMALL * GRID_SMALL, dim),
        (dim,),
        (dim,),
        (dim,),
        (dim, CLASSES),
        (CLASSES,),
    ]
    selfb = [
        (dim,),
        (dim,),
        (dim, 3 * dim),
        (2 * dim,),
        (HEADS, HEADS),
        (HEADS, HEADS),
        (dim, dim),
        (dim,),
        (dim,),
    ] + tail
    classb = [
        (dim,),
        (dim,),
        (dim, dim),
        (dim,),
        (dim, 2 * dim),
        (dim,),
        (dim, dim),
        (dim,),
        (dim,),
    ] + tail
    return [stem, selfb, classb]


def segment_bounds():
    starts = np.zeros((3, SEGMENTS), np.int32)
    ends = np.zeros((3, SEGMENTS), np.int32)
    real = np.zeros((3, SEGMENTS), np.float32)
    for group, shapes in enumerate(shapes_of()):
        offset = 0
        for number, shape in enumerate(shapes):
            count = int(np.prod(shape))
            starts[group, number] = offset
            ends[group, number] = offset + count
            real[group, number] = 1.0
            offset += count
    return starts, ends, real


STARTS, ENDS, REAL = segment_bounds()


def row_of(group, number):
    return int(STARTS[group, number]) // LANES


def rows_used(group):
    return -(-int(ENDS[group].max()) // LANES)


def resize_table():
    rows = np.arange(GRID_LARGE).astype(np.float32) * np.float32((GRID_SMALL - 1) / (GRID_LARGE - 1))
    cols = np.arange(GRID_SMALL).astype(np.float32)
    line = np.maximum(np.float32(0.0), np.float32(1.0) - np.abs(rows[:, None] - cols[None, :]))
    return (line[:, None, :, None] * line[None, :, None, :]).reshape(GRID_LARGE**2, GRID_SMALL**2)


def nn(a, b):
    return lax.dot_general(a, b, (((1,), (0,)), ((), ())), preferred_element_type=f32)


def nt(a, b):
    return lax.dot_general(a, b, (((1,), (1,)), ((), ())), preferred_element_type=f32)


def tn(a, b):
    return lax.dot_general(a, b, (((0,), (0,)), ((), ())), preferred_element_type=f32)


def colsum(value):
    return jnp.sum(value, 0, keepdims=True)


def split(value):
    high = value.astype(bf16)
    return high, (value - high.astype(f32)).astype(bf16)


def stats(value):
    centred = value - jnp.mean(value, -1, keepdims=True)
    inverse = lax.rsqrt(jnp.mean(centred * centred, -1, keepdims=True) + 1e-06)
    return centred * inverse, inverse


def norm_back(d_out, unit, inverse, gain):
    inner = d_out * gain
    first = jnp.mean(inner, -1, keepdims=True)
    second = jnp.mean(inner * unit, -1, keepdims=True)
    return inverse * (inner - first - unit * second)


def gelu_pair(upper):
    cdf = 0.5 * (1.0 + lax.erf(upper * (0.5**0.5)))
    density = jnp.exp(-0.5 * upper * upper) * 0.3989422804014327
    return upper * cdf, cdf + upper * density


def head_mask(rows):
    lane = lax.broadcasted_iota(jnp.int32, (rows, D), 1)
    row = lax.broadcasted_iota(jnp.int32, (rows, D), 0)
    return (lane // WIDTH) == lax.rem(row, HEADS)


VM = pl.BlockSpec(memory_space=pltpu.VMEM)
SM = pl.BlockSpec(memory_space=pltpu.SMEM)


def params(**kw):
    return pltpu.CompilerParams(vmem_limit_bytes=VMEM_BYTES, **kw)


def sds(shape, dtype):
    return jax.ShapeDtypeStruct(shape, dtype)


def call(kernel, args, after, in_specs, **kw):
    n, m = len(args), len(after)

    def wrapped(*refs):
        kernel(*refs[:n], *refs[n + m :])

    specs = list(in_specs) + [pl.BlockSpec(memory_space=pl.ANY)] * m
    return pl.pallas_call(wrapped, in_specs=specs, compiler_params=params(), **kw)(*args, *after)


def log2(n):
    return n.bit_length() - 1


def exchange(value, bit, z_bits):
    if bit < z_bits:
        n = lax.axis_size("fsdp")
        return lax.ppermute(value, "fsdp", [(i, i ^ (1 << bit)) for i in range(n)])
    n = lax.axis_size("dp")
    return lax.ppermute(value, "dp", [(i, i ^ (1 << (bit - z_bits))) for i in range(n)])


def exchange_z(value, k):
    n = lax.axis_size("fsdp")
    return lax.ppermute(value, "fsdp", [(i, i ^ k) for i in range(n)])


def tied(values, after):
    if after is None:
        return values
    return lax.optimization_barrier((*values, after))[:-1]


def gather_z(value, rel, after=None):
    n = lax.axis_size("fsdp")
    got = tied([exchange_z(value, k) for k in range(1, n)], after)
    return [(jnp.concatenate([value, *got], 0), [r | k for k in range(n) for r in rel])]


def gather_bit(state, bit, z_bits, after=None):
    got = tied([exchange(a, bit, z_bits) for a, _ in state], after)
    return state + [(a, [r | (1 << bit) for r in rel]) for a, (_, rel) in zip(got, state)]


def put_matrix(flat, row, out_ref, rows, cols):
    step = cols // LANES
    for j in range(step):
        out_ref[:, LANES * j : LANES * (j + 1)] = flat[pl.ds(row + j, rows, stride=step), :].astype(bf16)


def put_row(flat, row, out_ref, at, cols):
    for j in range(cols // LANES):
        out_ref[at : at + 1, LANES * j : LANES * (j + 1)] = flat[row + j : row + j + 1, :]


def fill_flat(me, piece_refs, rels, rows, flat):
    for ref, rel in zip(piece_refs, rels):
        for k, r in enumerate(rel):
            flat[pl.ds(rows * jnp.bitwise_xor(me, r), rows), :] = ref[k].astype(f32)[0:rows]


def unpack_stem_kernel(rels, rows, me_ref, resize_ref, *refs):
    n = len(rels)
    pieces, (patch_w, vec, pos_small, pos_large, head_w, head_b), (flat, tiles) = refs[:n], refs[n : n + 6], refs[n + 6 :]
    fill_flat(me_ref[0], pieces, rels, rows, flat)
    put_matrix(flat, row_of(0, 0), patch_w, PATCH_IN, D)
    vec[...] = jnp.zeros_like(vec)
    for at, number in enumerate((1, 3, 4, 5)):
        put_row(flat, row_of(0, number), vec, at, D)
    bias = vec[0:1, :]
    small = GRID_SMALL**2
    pos_small[...] = jnp.zeros_like(pos_small)
    for j in range(D // LANES):
        pos_small[0:small, LANES * j : LANES * (j + 1)] = flat[pl.ds(row_of(0, 2) + j, small, stride=D // LANES), :]
    pos_large[...] = (
        lax.dot_general(
            resize_ref[...], pos_small[...], (((1,), (0,)), ((), ())),
            preferred_element_type=f32, precision=lax.Precision.HIGHEST,
        )
        + bias
    )
    pos_small[...] += bias
    lane = lax.broadcasted_iota(jnp.int32, (24, LANES), 1)
    base = row_of(0, 6)
    for rho in range(16):
        first, shift = (CLASSES * rho) // LANES, (CLASSES * rho) % LANES
        parts = [flat[pl.ds(base + first + t, 24, stride=125), :] for t in range(9)]
        if shift:
            parts = [pltpu.roll(p, LANES - shift, 1) for p in parts]
        for t in range(8):
            value = jnp.where(lane < LANES - shift, parts[t], parts[t + 1]) if shift else parts[t]
            if t == 7:
                value = jnp.where(lane < CLASSES - 7 * LANES, value, 0.0)
            tiles[t, pl.ds(rho, 24, stride=16), :] = value
    for t in range(8):
        head_w[:, LANES * t : LANES * (t + 1)] = tiles[t, 0:D, :].astype(bf16)
    put_row(flat, row_of(0, 7), head_b, 0, CLASS_PAD)


def unpack_stem(me, pieces, rels, rows, count, padded):
    resize = np.zeros((GRID_LARGE**2, padded), np.float32)
    resize[:, : GRID_SMALL**2] = resize_table()
    return pl.pallas_call(
        functools.partial(unpack_stem_kernel, rels, rows),
        out_shape=[
            sds((PATCH_IN, D), bf16),
            sds((8, D), f32),
            sds((padded, D), f32),
            sds((GRID_LARGE**2, D), f32),
            sds((D, CLASS_PAD), bf16),
            sds((1, CLASS_PAD), f32),
        ],
        in_specs=[SM] + [VM] * (1 + len(pieces)),
        out_specs=[VM] * 6,
        scratch_shapes=[pltpu.VMEM((count * rows, LANES), f32), pltpu.VMEM((8, D + 16, LANES), f32)],
        compiler_params=params(),
        name="unpack_stem",
    )(me, jnp.asarray(resize), *pieces)


SG1, SB1, SBQ, SBV, SBO, SLS1, SG2, SB2, SC2, SLS2 = range(10)
CG1, CB1, CBQ, CBV, CBO, CLS1, CG2, CB2, CC2, CLS2 = range(10)


def unpack_low_kernel(rels, rows, me_ref, *refs):
    n = len(rels)
    pieces = refs[:n]
    wqkv, vec, pre_col, post_col, pre_row, post_row, flat = refs[n:]
    fill_flat(me_ref[0], pieces, rels, rows, flat)
    put_matrix(flat, row_of(1, 2), wqkv, D, 3 * D)
    vec[...] = jnp.zeros_like(vec)
    bq = row_of(1, 3)
    for at, row in ((SG1, row_of(1, 0)), (SB1, row_of(1, 1)), (SBQ, bq), (SBV, bq + D // LANES)):
        put_row(flat, row, vec, at, D)
    mix = jnp.broadcast_to(flat[row_of(1, 4) : row_of(1, 4) + 1, :], (HEADS, LANES))
    lane = lax.broadcasted_iota(jnp.int32, (HEADS, LANES), 1)
    row = lax.broadcasted_iota(jnp.int32, (HEADS, LANES), 0)
    pick_pre = jnp.where((lane < 64) & (lane // HEADS == row), mix, 0.0).astype(bf16)
    pick_post = jnp.where((lane >= 64) & (lane % HEADS == row), mix, 0.0).astype(bf16)
    table_lane = lax.broadcasted_iota(jnp.int32, (LANES, D), 0)
    table_col = lax.broadcasted_iota(jnp.int32, (LANES, D), 1) // WIDTH
    spread_pre = jnp.where(table_lane % HEADS == table_col, 1.0, 0.0).astype(bf16)
    spread_post = jnp.where((table_lane - 64) // HEADS == table_col, 1.0, 0.0).astype(bf16)
    factor = SCALE * LOG2E
    pre_row[...] = nn(pick_pre, spread_pre) * factor
    post_row[...] = nn(pick_post, spread_post)
    column = lambda a, b: lax.dot_general(a, b, (((0,), (1,)), ((), ())), preferred_element_type=f32)
    pre_col[...] = column(spread_pre, pick_pre) * factor
    post_col[...] = column(spread_post, pick_post)


def unpack_low(me, pieces, rels, rows, count):
    return pl.pallas_call(
        functools.partial(unpack_low_kernel, rels, rows),
        out_shape=[
            sds((D, 3 * D), bf16),
            sds((16, D), f32),
            sds((D, HEADS), f32),
            sds((D, HEADS), f32),
            sds((HEADS, D), f32),
            sds((HEADS, D), f32),
        ],
        in_specs=[SM] + [VM] * len(pieces),
        out_specs=[VM] * 6,
        scratch_shapes=[pltpu.VMEM((count * rows, LANES), f32)],
        compiler_params=params(),
        name="unpack_low",
    )(me, *pieces)


def unpack_feed_kernel(rels, rows, me_ref, *refs):
    n = len(rels)
    pieces = refs[:n]
    wo, w1, w2, vec, c1, flat = refs[n:]
    fill_flat(me_ref[0], pieces, rels, rows, flat)
    put_matrix(flat, row_of(1, 6), wo, D, D)
    put_matrix(flat, row_of(1, 11), w1, D, FF)
    put_matrix(flat, row_of(1, 13), w2, FF, D)
    vec[...] = jnp.zeros_like(vec)
    for at, number in ((SBO, 7), (SLS1, 8), (SG2, 9), (SB2, 10), (SC2, 14), (SLS2, 15)):
        put_row(flat, row_of(1, number), vec, at, D)
    put_row(flat, row_of(1, 12), c1, 0, FF)


def unpack_feed(me, pieces, rels, rows, count):
    return pl.pallas_call(
        functools.partial(unpack_feed_kernel, rels, rows),
        out_shape=[
            sds((D, D), bf16),
            sds((D, FF), bf16),
            sds((FF, D), bf16),
            sds((16, D), f32),
            sds((1, FF), f32),
        ],
        in_specs=[SM] + [VM] * len(pieces),
        out_specs=[VM] * 5,
        scratch_shapes=[pltpu.VMEM((count * rows, LANES), f32)],
        compiler_params=params(),
        name="unpack_feed",
    )(me, *pieces)


def unpack_class_kernel(rels, rows, me_ref, *refs):
    n = len(rels)
    pieces = refs[:n]
    wq, wkv, wo, w1, w2, vec, c1, total, flat = refs[n:]
    fill_flat(me_ref[0], pieces, rels, rows, flat)
    put_matrix(flat, row_of(2, 2), wq, D, D)
    put_matrix(flat, row_of(2, 4), wkv, D, 2 * D)
    put_matrix(flat, row_of(2, 6), wo, D, D)
    put_matrix(flat, row_of(2, 11), w1, D, FF)
    put_matrix(flat, row_of(2, 13), w2, FF, D)
    vec[...] = jnp.zeros_like(vec)
    for at, number in (
        (CG1, 0), (CB1, 1), (CBQ, 3), (CBV, 5), (CBO, 7), (CLS1, 8), (CG2, 9), (CB2, 10), (CC2, 14), (CLS2, 15),
    ):
        put_row(flat, row_of(2, number), vec, at, D)
    put_row(flat, row_of(2, 12), c1, 0, FF)
    count = jnp.zeros((1, LANES), f32)
    for ref, rel in zip(pieces, rels):
        for k in range(len(rel)):
            count = count + ref[k].astype(f32)[rows : rows + 1, :]
    total[...] = count


def const_spec(a):
    return pl.BlockSpec(a.shape, lambda i, nd=len(a.shape): (0,) * nd, pipeline_mode=pl.Buffered(1))


def cost(flops, read):
    return pl.CostEstimate(flops=int(flops), bytes_accessed=int(read), transcendentals=0)


class Steps:
    def __init__(self, ns, nl, padded, large_len):
        self.count = math.gcd(ns, nl)
        self.small, self.large = ns // self.count, nl // self.count
        self.padded, self.large_len = padded, large_len
        self.split = self.small * padded
        self.rows = self.split + self.large * large_len
        self.grid = (self.count,)

    def specs(self, cols):
        index = lambda i: (i, 0, 0)
        return [
            pl.BlockSpec((self.small, self.padded, cols), index),
            pl.BlockSpec((self.large, self.large_len, cols), index),
        ]

    def shapes(self, cols, kind):
        n = self.count
        return [sds((n * self.small, self.padded, cols), kind), sds((n * self.large, self.large_len, cols), kind)]

    def join(self, pair):
        cols = pair[0].shape[-1]
        return jnp.concatenate([ref[...].reshape(-1, cols) for ref in pair], 0)

    def put(self, pair, value):
        cols = value.shape[-1]
        pair[0][...] = value[: self.split].reshape(self.small, self.padded, cols)
        pair[1][...] = value[self.split :].reshape(self.large, self.large_len, cols)


def embed_kernel(steps, valid, ps, plg, patch_w, pos_small, pos_large, wqkv, vec, *outs):
    tok_o, qkv_o, tokens = outs[:2], outs[2:4], outs[4]
    row = lambda at: vec[at : at + 1, :]
    for i in range(steps.small):
        base = steps.padded * i
        tokens[base : base + steps.padded, :] = pos_small[...]
        tokens[base : base + valid, :] += nn(ps[i], patch_w[...])
    for i in range(steps.large):
        base = steps.split + steps.large_len * i
        tokens[base : base + steps.large_len, :] = nn(plg[i], patch_w[...]) + pos_large[...]
    tok = tokens[...]
    steps.put(tok_o, tok)
    unit, _ = stats(tok)
    a1 = (unit * row(SG1) + row(SB1)).astype(bf16)
    bias = jnp.concatenate([row(SBQ), jnp.zeros((1, D), f32), row(SBV)], 1)
    steps.put(qkv_o, (nn(a1, wqkv[...]) + bias).astype(bf16))


def embed(ps, plg, patch_w, pos_small, pos_large, wqkv, vec, padded, after):
    ns, valid, _ = ps.shape
    nl, large_len, _ = plg.shape
    steps = Steps(ns, nl, padded, large_len)
    weights = (patch_w, pos_small, pos_large, wqkv, vec)
    index = lambda i: (i, 0, 0)
    out = call(
        functools.partial(embed_kernel, steps, valid),
        (ps, plg, *weights),
        after,
        grid=steps.grid,
        out_shape=steps.shapes(D, f32) + steps.shapes(3 * D, bf16),
        in_specs=[
            pl.BlockSpec((steps.small, valid, PATCH_IN), index),
            pl.BlockSpec((steps.large, large_len, PATCH_IN), index),
        ]
        + [const_spec(a) for a in weights],
        out_specs=steps.specs(D) + steps.specs(3 * D),
        scratch_shapes=[pltpu.VMEM((steps.rows, D), f32)],
        cost_estimate=cost(12e9, 20e6),
        name="embed",
    )
    return out[:2], out[2:]


def attend_kernel(valid, qkv_ref, pre_col, post_col, att_ref, lse_ref, q_t, kk, v_t, acc):
    per, length = qkv_ref.shape[0], qkv_ref.shape[1]
    for i in range(per):
        q_t[i] = qkv_ref[i, :, 0:D].astype(f32).T
        kk[i, :, 0:D] = qkv_ref[i, :, D : 2 * D]
        kk[i, :, D:] = qkv_ref[i, :, D : 2 * D]
        v_t[i] = qkv_ref[i, :, 2 * D :].astype(f32).T.astype(bf16)
    for g in range(HEADS):
        pre, post = pre_col[:, g : g + 1], post_col[:, g : g + 1]
        for i in range(per):
            high, low = split(q_t[i] * pre)
            mixed = nn(kk[i], jnp.concatenate([high, low], 0))
            if valid < length:
                mixed = jnp.where(lax.broadcasted_iota(jnp.int32, mixed.shape, 0) < valid, mixed, NEG)
            top = jnp.max(mixed, 0, keepdims=True)
            raw = jnp.exp2(mixed - top)
            weight = colsum(raw)
            lse_ref[i, g : g + 1, :] = top + jnp.log2(weight)
            part = nn(v_t[i], raw.astype(bf16)) * post * (1.0 / weight)
            acc[i] = part if g == 0 else acc[i] + part
    for i in range(per):
        att_ref[i] = acc[i].T.astype(bf16)


def attend(qkv, pre_col, post_col, valid, per, flops, after):
    n, length, _ = qkv.shape
    spec = lambda *tail: pl.BlockSpec((per,) + tail, lambda i: (i, 0, 0))
    return call(
        functools.partial(attend_kernel, valid),
        (qkv, pre_col, post_col),
        after,
        grid=(n // per,),
        out_shape=[sds((n, length, D), bf16), sds((n, HEADS, length), f32)],
        in_specs=[spec(length, 3 * D), const_spec(pre_col), const_spec(post_col)],
        out_specs=[spec(length, D), spec(HEADS, length)],
        scratch_shapes=[
            pltpu.VMEM((per, D, length), f32),
            pltpu.VMEM((per, length, 2 * D), bf16),
            pltpu.VMEM((per, D, length), bf16),
            pltpu.VMEM((per, D, length), f32),
        ],
        cost_estimate=cost(flops, 10e6),
        name="attend",
    )


def feed_kernel(steps, tok_s, tok_l, att_s, att_l, wo, w1, w2, vec, c1, *outs):
    branch_o, mid_o, act_o, slope_o, lower_o, out_o = [outs[2 * i : 2 * i + 2] for i in range(6)]
    row = lambda at: vec[at : at + 1, :]
    branch = nn(steps.join((att_s, att_l)), wo[...]) + row(SBO)
    steps.put(branch_o, branch.astype(bf16))
    mid = steps.join((tok_s, tok_l)) + row(SLS1) * branch
    steps.put(mid_o, mid)
    unit, _ = stats(mid)
    n2 = (unit * row(SG2) + row(SB2)).astype(bf16)
    act, slope = gelu_pair(nn(n2, w1[...]) + c1[...])
    act = act.astype(bf16)
    steps.put(act_o, act)
    steps.put(slope_o, slope.astype(bf16))
    lower = nn(act, w2[...]) + row(SC2)
    steps.put(lower_o, lower.astype(bf16))
    steps.put(out_o, mid + row(SLS2) * lower)


FEED_OUT = [(D, bf16), (D, f32), (FF, bf16), (FF, bf16), (D, bf16), (D, f32)]


def feed(tok, att, weights, after):
    (ns, padded, _), (nl, large_len, _) = tok[0].shape, tok[1].shape
    steps = Steps(ns, nl, padded, large_len)
    out = call(
        functools.partial(feed_kernel, steps),
        (*tok, *att, *weights),
        after,
        grid=steps.grid,
        out_shape=[shape for entry in FEED_OUT for shape in steps.shapes(*entry)],
        in_specs=steps.specs(D) * 2 + [const_spec(a) for a in weights],
        out_specs=[spec for cols, _ in FEED_OUT for spec in steps.specs(cols)],
        cost_estimate=cost(20e9, 30e6),
        name="feed",
    )
    return [out[2 * i : 2 * i + 2] for i in range(6)]


BATCH = 8


def class_kernel(
    ns, nl, valid, out_s, out_l, wq, wkv, wo, w1, w2, vec, c1, svec, head_w, head_b, total, counts, labels_s, labels_l,
    d_s, d_l, g_wq, g_wkv, g_wo, g_w1, g_w2, g_vec, g_c1, g_svec, g_head_w, g_head_b, loss_o,
    a_s, a_l, p_s, p_l, z_ref, y_ref, b_ref, ps_ref, pc_ref, da_ref,
):
    row = lambda at: vec[at : at + 1, :]
    mask8 = head_mask(HEADS)
    mask64 = head_mask(HEADS * BATCH)
    cls = svec[1:2, :]
    unit_cls, inv_cls = stats(cls)
    a_cls = (unit_cls * row(CG1) + row(CB1)).astype(bf16)
    a_cls_f = a_cls.astype(f32)
    query = (nn(a_cls, wq[...]) + row(CBQ)).astype(bf16).astype(f32)
    q_diag = jnp.where(mask8, query, 0.0).astype(bf16)
    u_nat = nt(q_diag, wkv[:, 0:D]) * SCALE
    u_hi, u_lo = split(u_nat * LOG2E)
    u16 = jnp.concatenate([u_hi, u_lo], 0)
    s_cls = jnp.sum(u_nat * LOG2E * a_cls_f, -1, keepdims=True)
    z_ref[...] = jnp.zeros_like(z_ref)
    ps_ref[...] = jnp.zeros_like(ps_ref)

    def forward(i, src, a_ref, p_ref, slot):
        unit, _ = stats(src[i])
        a = (unit * row(CG1) + row(CB1)).astype(bf16)
        a_ref[i] = a
        s16 = nt(u16, a)
        s = s16[0:HEADS] + s16[HEADS:]
        keep = valid if a.shape[0] != GRID_LARGE**2 else a.shape[0]
        if keep < a.shape[0]:
            s = jnp.where(lax.broadcasted_iota(jnp.int32, s.shape, 1) < keep, s, NEG)
        top = jnp.maximum(jnp.max(s, -1, keepdims=True), s_cls)
        e = jnp.exp2(s - top)
        e_cls = jnp.exp2(s_cls - top)
        inverse = 1.0 / (jnp.sum(e, -1, keepdims=True) + e_cls)
        p, p_cls = e * inverse, e_cls * inverse
        p_ref[i] = p
        low, low_cls = p.astype(bf16), p_cls.astype(bf16).astype(f32)
        z_ref[pl.ds(slot * HEADS, HEADS), :] = nn(low, a) + low_cls * a_cls_f
        ps_ref[pl.ds(slot * HEADS, HEADS), :] = jnp.sum(low.astype(f32), -1, keepdims=True) + low_cls
        pc_ref[pl.ds(slot * HEADS, HEADS), :] = p_cls

    for i in range(ns):
        forward(i, out_s, a_s, p_s, i)
    for i in range(nl):
        forward(i, out_l, a_l, p_l, ns + i)

    z_hi, z_lo = split(z_ref[...])
    o_all = nn(jnp.concatenate([z_hi, z_lo], 0), wkv[:, D:])
    o_all = o_all[0 : HEADS * BATCH] + o_all[HEADS * BATCH :] + ps_ref[...] * row(CBV)
    att = jnp.sum(jnp.where(mask64, o_all, 0.0).reshape(BATCH, HEADS, D), 1).astype(bf16)
    branch = nn(att, wo[...]) + row(CBO)
    mid = cls + row(CLS1) * branch
    unit_mid, inv_mid = stats(mid)
    n2 = (unit_mid * row(CG2) + row(CB2)).astype(bf16)
    upper = nn(n2, w1[...]) + c1[...]
    act, slope = gelu_pair(upper)
    act = act.astype(bf16)
    lower = nn(act, w2[...]) + row(CC2)
    c_tok = mid + row(CLS2) * lower
    unit_c, inv_c = stats(c_tok)
    final = (unit_c * svec[2:3, :] + svec[3:4, :]).astype(bf16)
    logits = nn(final, head_w[...]) + head_b[...]
    lane = lax.broadcasted_iota(jnp.int32, logits.shape, 1)
    inside = lane < CLASSES
    logits = jnp.where(inside, logits, NEG)
    shifted = logits - jnp.max(logits, -1, keepdims=True)
    raw = jnp.exp(shifted)
    weight = jnp.sum(raw, -1, keepdims=True)
    logp = shifted - jnp.log(weight)
    image = lax.broadcasted_iota(jnp.int32, (BATCH, 1), 0)
    label = jnp.zeros((BATCH, 1), jnp.int32)
    for i in range(ns):
        label = jnp.where(image == i, labels_s[i], label)
    for i in range(nl):
        label = jnp.where(image == ns + i, labels_l[i], label)
    alive = ((image < ns) & (image < counts[0, 0])) | ((image >= ns) & (image - ns < counts[0, 1]))
    hit = lane == label
    picked = jnp.sum(jnp.where(hit, logp, 0.0), -1, keepdims=True)
    mean = jnp.sum(jnp.where(inside, logp, 0.0), -1, keepdims=True) * (1.0 / CLASSES)
    each = -((1.0 - smooth) * picked + smooth * mean)
    scaled = jnp.where(alive, 1.0, 0.0) / total[0:1, 0:1]
    loss_o[...] = jnp.broadcast_to(colsum(scaled * each), loss_o.shape)
    target = jnp.where(hit, 1.0 - smooth, 0.0) + smooth / CLASSES
    d_logits = jnp.where(inside, scaled * (raw / weight - target), 0.0).astype(bf16)

    d_final = nt(d_logits, head_w[...])
    g_head_w[...] = tn(final, d_logits)
    g_head_b[...] = colsum(d_logits.astype(f32))
    g_svec[...] = jnp.zeros_like(g_svec)
    g_svec[2:3, :] = colsum(d_final * unit_c)
    g_svec[3:4, :] = colsum(d_final)
    d_c = norm_back(d_final, unit_c, inv_c, svec[2:3, :])
    g_vec[...] = jnp.zeros_like(g_vec)
    g_vec[CLS2 : CLS2 + 1, :] = colsum(d_c * lower)
    d_lower = (d_c * row(CLS2)).astype(bf16)
    g_vec[CC2 : CC2 + 1, :] = colsum(d_lower.astype(f32))
    g_w2[...] = tn(act, d_lower)
    d_upper = (slope * nt(d_lower, w2[...])).astype(bf16)
    g_c1[...] = colsum(d_upper.astype(f32))
    g_w1[...] = tn(n2, d_upper)
    d_n2 = nt(d_upper, w1[...])
    g_vec[CG2 : CG2 + 1, :] = colsum(d_n2 * unit_mid)
    g_vec[CB2 : CB2 + 1, :] = colsum(d_n2)
    d_mid = d_c + norm_back(d_n2, unit_mid, inv_mid, row(CG2))
    g_vec[CLS1 : CLS1 + 1, :] = colsum(d_mid * branch)
    d_branch = (d_mid * row(CLS1)).astype(bf16)
    g_vec[CBO : CBO + 1, :] = colsum(d_branch.astype(f32))
    g_wo[...] = tn(att, d_branch)
    d_att = nt(d_branch, wo[...]).astype(bf16).astype(f32)
    d_diag = jnp.where(mask64, jnp.broadcast_to(d_att[:, None, :], (BATCH, HEADS, D)).reshape(BATCH * HEADS, D), 0.0)
    g_vec[CBV : CBV + 1, :] = colsum(d_diag * ps_ref[...])
    shift = jnp.sum(d_diag * row(CBV), -1, keepdims=True)
    d_diag_low = d_diag.astype(bf16)
    y_ref[...] = nt(d_diag_low, wkv[:, D:])
    g_wkv[:, D:] = tn(jnp.concatenate([z_hi, z_lo], 0), jnp.concatenate([d_diag_low, d_diag_low], 0))
    z_ref[:, 0:1] = shift
    b_ref[...] = jnp.zeros_like(b_ref)
    da_ref[...] = jnp.zeros_like(da_ref)
    un_hi, un_lo = split(u_nat)

    def backward(i, src, a_ref, p_ref, d_ref, slot):
        unit, inverse = stats(src[i])
        a = a_ref[i]
        here = pl.ds(slot * HEADS, HEADS)
        y = y_ref[here, :]
        y_hi, y_lo = split(y)
        d16 = nt(jnp.concatenate([y_hi, y_lo], 0), a)
        offset = z_ref[here, 0:1]
        d_p = d16[0:HEADS] + d16[HEADS:] + offset
        d_p_cls = jnp.sum(y * a_cls_f, -1, keepdims=True) + offset
        p, p_cls = p_ref[i], pc_ref[here, :]
        delta = jnp.sum(p * d_p, -1, keepdims=True) + p_cls * d_p_cls
        d_score = (p * (d_p - delta)).astype(bf16)
        d_score_cls = (p_cls * (d_p_cls - delta)).astype(bf16).astype(f32)
        low = p.astype(bf16)
        b_ref[...] += nn(d_score, a) + d_score_cls * a_cls_f
        da_ref[...] += d_score_cls * u_nat + p_cls.astype(bf16).astype(f32) * y
        left = jnp.concatenate([d_score.astype(f32), d_score.astype(f32), low.astype(f32), low.astype(f32)], 0)
        d_a = tn(left.astype(bf16), jnp.concatenate([un_hi, un_lo, y_hi, y_lo], 0))
        g_vec[CG1 : CG1 + 1, :] += colsum(d_a * unit)
        g_vec[CB1 : CB1 + 1, :] += colsum(d_a)
        d_ref[i] = norm_back(d_a, unit, inverse, row(CG1))

    for i in range(ns):
        backward(i, out_s, a_s, p_s, d_s, i)
    for i in range(nl):
        backward(i, out_l, a_l, p_l, d_l, ns + i)

    b_hi, b_lo = split(b_ref[...])
    bw = nn(jnp.concatenate([b_hi, b_lo], 0), wkv[:, 0:D])
    bw = bw[0:HEADS] + bw[HEADS:]
    d_query = (colsum(jnp.where(mask8, bw, 0.0)) * SCALE).astype(bf16)
    g_vec[CBQ : CBQ + 1, :] = d_query.astype(f32)
    q_scaled = q_diag.astype(f32) * SCALE
    qs_hi, qs_lo = split(q_scaled)
    g_wkv[:, 0:D] = tn(
        jnp.concatenate([b_hi, b_hi, b_lo, b_lo], 0), jnp.concatenate([qs_hi, qs_lo, qs_hi, qs_lo], 0)
    )
    first = lax.broadcasted_iota(jnp.int32, (16, D), 0) == 0
    spread_a = jnp.where(first, jnp.broadcast_to(a_cls_f, (16, D)), 0.0).astype(bf16)
    spread_q = jnp.where(first, jnp.broadcast_to(d_query.astype(f32), (16, D)), 0.0).astype(bf16)
    g_wq[...] = tn(spread_a, spread_q)
    d_a_cls = colsum(da_ref[...]) + nt(d_query, wq[...])
    g_vec[CG1 : CG1 + 1, :] += d_a_cls * unit_cls
    g_vec[CB1 : CB1 + 1, :] += d_a_cls
    g_svec[1:2, :] = colsum(d_mid) + norm_back(d_a_cls, unit_cls, inv_cls, row(CG1))


CLASS_WEIGHTS = [(D, D), (D, 2 * D), (D, D), (D, FF), (FF, D)]


def class_step_kernel(ns, nl, valid, unpack_rels, pack_rels, rows, n, me_ref, from_ref, counts, labels_s, labels_l, *refs):
    pieces, (out_s, out_l, svec, head_w, head_b), refs = refs[:n], refs[n : n + 5], refs[n + 5 :]
    (d_s, d_l, g_svec, g_head_w, g_head_b, loss, keep, send), refs = refs[:8], refs[8:]
    weights, total, grads, flat, work = refs[:7], refs[7], refs[8:15], refs[15], refs[16:]
    unpack_class_kernel(unpack_rels, rows, from_ref, *pieces, *weights, total, flat)
    class_kernel(
        ns, nl, valid, out_s, out_l, *weights, svec, head_w, head_b, total, counts, labels_s, labels_l,
        d_s, d_l, *grads, g_svec, g_head_w, g_head_b, loss, *work,
    )
    pack_class_kernel(pack_rels, rows, me_ref, *grads, keep, send, flat)


def class_step(me, unpack_me, pieces, unpack_rels, pack_rels, out, stem, counts, labels_s, labels_l, valid, rows, padded_rows):
    (ns, padded, _), (nl, large_len, _) = out[0].shape, out[1].shape
    _, svec, _, _, head_w, head_b = stem
    args = (me, unpack_me, counts, labels_s, labels_l, *pieces, *out, svec, head_w, head_b)
    half = len(pack_rels) // 2
    vectors = [pltpu.VMEM((16, D), f32), pltpu.VMEM((1, FF), f32)]
    return pl.pallas_call(
        functools.partial(
            class_step_kernel, ns, nl, valid, unpack_rels, pack_rels, rows, len(pieces)
        ),
        out_shape=[
            sds((ns, padded, D), f32),
            sds((nl, large_len, D), f32),
            sds((8, D), f32),
            sds((D, CLASS_PAD), f32),
            sds((1, CLASS_PAD), f32),
            sds((1, LANES), f32),
            sds((half, padded_rows, LANES), bf16),
            sds((half, padded_rows, LANES), bf16),
        ],
        in_specs=[SM] * 5 + [VM] * (len(args) - 5),
        out_specs=[VM] * 8,
        scratch_shapes=[pltpu.VMEM(shape, bf16) for shape in CLASS_WEIGHTS]
        + vectors
        + [pltpu.VMEM((1, LANES), f32)]
        + [pltpu.VMEM(shape, f32) for shape in CLASS_WEIGHTS]
        + vectors
        + [
            pltpu.VMEM((len(pack_rels) * rows + padded_rows - rows + 8, LANES), f32),
            pltpu.VMEM((ns, padded, D), bf16),
            pltpu.VMEM((nl, large_len, D), bf16),
            pltpu.VMEM((ns, HEADS, padded), f32),
            pltpu.VMEM((nl, HEADS, large_len), f32),
            pltpu.VMEM((BATCH * HEADS, D), f32),
            pltpu.VMEM((BATCH * HEADS, D), f32),
            pltpu.VMEM((HEADS, D), f32),
            pltpu.VMEM((BATCH * HEADS, 1), f32),
            pltpu.VMEM((BATCH * HEADS, 1), f32),
            pltpu.VMEM((HEADS, D), f32),
        ],
        compiler_params=params(),
        cost_estimate=cost(25e9, 40e6),
        name="class_step",
    )(*args)


def feed_back_kernel(steps, *refs):
    ins, (wo, w1, w2, vec), refs = [refs[2 * i : 2 * i + 2] for i in range(7)], refs[14:18], refs[18:]
    d_mid_o, d_att_o, sums = refs[:2], refs[2:4], refs[4:]
    g_wo, g_w1, g_w2, g_vec, g_c1 = sums
    row = lambda at: vec[at : at + 1, :]

    @pl.when(pl.program_id(0) == 0)
    def _():
        for ref in sums:
            ref[...] = jnp.zeros_like(ref)

    def add(at, value):
        g_vec[at : at + 1, :] += value

    d_out_r, mid_r, act_r, slope_r, lower_r, branch_r, att_r = ins
    d_out = steps.join(d_out_r)
    add(SLS2, colsum(d_out * steps.join(lower_r).astype(f32)))
    d_lower = (d_out * row(SLS2)).astype(bf16)
    add(SC2, colsum(d_lower.astype(f32)))
    unit, inverse = stats(steps.join(mid_r))
    n2 = (unit * row(SG2) + row(SB2)).astype(bf16)
    g_w2[...] += tn(steps.join(act_r), d_lower)
    d_upper = (nt(d_lower, w2[...]) * steps.join(slope_r).astype(f32)).astype(bf16)
    g_w1[...] += tn(n2, d_upper)
    g_c1[...] += colsum(d_upper.astype(f32))
    d_n2 = nt(d_upper, w1[...])
    add(SG2, colsum(d_n2 * unit))
    add(SB2, colsum(d_n2))
    d_mid = d_out + norm_back(d_n2, unit, inverse, row(SG2))
    steps.put(d_mid_o, d_mid)
    add(SLS1, colsum(d_mid * steps.join(branch_r).astype(f32)))
    d_branch = (d_mid * row(SLS1)).astype(bf16)
    add(SBO, colsum(d_branch.astype(f32)))
    g_wo[...] += tn(steps.join(att_r), d_branch)
    steps.put(d_att_o, nt(d_branch, wo[...]).astype(bf16))


def sum_specs(shapes):
    return [pl.BlockSpec(s.shape, lambda i: (0, 0), pipeline_mode=pl.Buffered(1)) for s in shapes]


def feed_back(pairs, weights, after):
    (ns, padded, _), (nl, large_len, _) = pairs[0][0].shape, pairs[0][1].shape
    steps = Steps(ns, nl, padded, large_len)
    sums = [sds((D, D), f32), sds((D, FF), f32), sds((FF, D), f32), sds((16, D), f32), sds((1, FF), f32)]
    out = call(
        functools.partial(feed_back_kernel, steps),
        (*[a for pair in pairs for a in pair], *weights),
        after,
        grid=steps.grid,
        out_shape=steps.shapes(D, f32) + steps.shapes(D, bf16) + sums,
        in_specs=[spec for pair in pairs for spec in steps.specs(pair[0].shape[2])] + [const_spec(a) for a in weights],
        out_specs=steps.specs(D) * 2 + sum_specs(sums),
        cost_estimate=cost(35e9, 30e6),
        name="feed_back",
    )
    return out[:2], out[2:4], out[4:]


def attend_back_kernel(valid, qkv_ref, d_att_ref, lse_ref, pre_col, post_col, pre_row, post_row, d_qkv_ref, g_pre, g_post,
                       q_t, kk, k_t, do_t, dq_t, d_k, d_v):
    per, length = qkv_ref.shape[0], qkv_ref.shape[1]
    for i in range(per):
        q_t[i] = qkv_ref[i, :, 0:D].astype(f32).T
        kk[i, :, 0:D] = qkv_ref[i, :, D : 2 * D]
        kk[i, :, D:] = qkv_ref[i, :, D : 2 * D]
        k_t[i] = qkv_ref[i, :, D : 2 * D].astype(f32).T.astype(bf16)
        do_t[i] = d_att_ref[i].astype(f32).T

    @pl.when(pl.program_id(0) == 0)
    def _():
        g_pre[...] = jnp.zeros_like(g_pre)
        g_post[...] = jnp.zeros_like(g_post)

    for g in range(HEADS):
        pre, post = pre_col[:, g : g + 1], post_col[:, g : g + 1]
        for i in range(per):
            q, k, v = qkv_ref[i, :, 0:D], qkv_ref[i, :, D : 2 * D], qkv_ref[i, :, 2 * D :]
            high, low = split(q_t[i] * pre)
            mixed = nn(kk[i], jnp.concatenate([high, low], 0))
            d_p = nn(v, (do_t[i] * post).astype(bf16))
            p = jnp.exp2(mixed - lse_ref[i, g : g + 1, :])
            if valid < length:
                p = jnp.where(lax.broadcasted_iota(jnp.int32, p.shape, 0) < valid, p, 0.0)
            delta = colsum(p * d_p)
            d_mixed = (p * (d_p - delta)).astype(bf16)
            r = nn(p.astype(bf16), d_att_ref[i])
            t = nn(d_mixed, q)
            u = nn(k_t[i], d_mixed)
            d_v_part, d_k_part, d_q_part = r * post_row[g : g + 1, :], t * pre_row[g : g + 1, :], u * pre
            d_v[i] = d_v_part if g == 0 else d_v[i] + d_v_part
            d_k[i] = d_k_part if g == 0 else d_k[i] + d_k_part
            dq_t[i] = d_q_part if g == 0 else dq_t[i] + d_q_part
            g_post[g : g + 1, :] += colsum(r * v.astype(f32))
            g_pre[g : g + 1, :] += colsum(t * k.astype(f32))
    inverse = 1.0 / LOG2E
    for i in range(per):
        d_qkv_ref[i, :, 0:D] = (dq_t[i].T * inverse).astype(bf16)
        d_qkv_ref[i, :, D : 2 * D] = (d_k[i] * inverse).astype(bf16)
        d_qkv_ref[i, :, 2 * D :] = d_v[i].astype(bf16)


def attend_back(qkv, d_att, lse, mixes, valid, first, count, per, flops, after):
    length = qkv.shape[1]
    spec = lambda *tail: pl.BlockSpec((per,) + tail, lambda i: (i + first // per, 0, 0))
    sums = [sds((HEADS, D), f32)] * 2
    return call(
        functools.partial(attend_back_kernel, valid),
        (qkv, d_att, lse, *mixes),
        after,
        grid=(count // per,),
        out_shape=[sds((count, length, 3 * D), bf16)] + sums,
        in_specs=[spec(length, 3 * D), spec(length, D), spec(HEADS, length)] + [const_spec(a) for a in mixes],
        out_specs=[pl.BlockSpec((per, length, 3 * D), lambda i: (i, 0, 0))] + sum_specs(sums),
        scratch_shapes=[
            pltpu.VMEM((per, D, length), f32),
            pltpu.VMEM((per, length, 2 * D), bf16),
            pltpu.VMEM((per, D, length), bf16),
            pltpu.VMEM((per, D, length), f32),
            pltpu.VMEM((per, D, length), f32),
            pltpu.VMEM((per, length, D), f32),
            pltpu.VMEM((per, length, D), f32),
        ],
        cost_estimate=cost(flops, 10e6),
        name="attend_back",
    )


def embed_back_kernel(steps, valid, late, me_ref, ps, plg, resize, *refs):
    tok_r, dq_s, d_mid_r, refs = refs[:2], refs[2], refs[3:5], refs[5:]
    n = steps.large * steps.count
    dq_l, (wqkv, vec, pre, post, g_wo, g_svec, g_head_w), refs = refs[:n], refs[n : n + 7], refs[n + 7 :]
    (keep, send), sums, (d_qkv, flat, tiles) = refs[:2], refs[2:8], refs[8:]
    g_wqkv, g_vec, g_patch_w, g_patch_b, g_pos, pos_large = sums
    row = lambda at: vec[at : at + 1, :]
    step = pl.program_id(0)

    @pl.when(step == 0)
    def _():
        for ref in sums:
            ref[...] = jnp.zeros_like(ref)

    d_qkv[: steps.split, :] = dq_s[...].reshape(steps.split, 3 * D)
    for k in range(steps.count):

        @pl.when(step == k)
        def _(k=k):
            for i in range(steps.large):
                base = steps.split + steps.large_len * i
                d_qkv[base : base + steps.large_len, :] = dq_l[k * steps.large + i][0]

    def add(at, value):
        g_vec[at : at + 1, :] += value

    add(SBQ, colsum(d_qkv[:, 0:D].astype(f32)))
    add(SBV, colsum(d_qkv[:, 2 * D :].astype(f32)))
    unit, inverse = stats(steps.join(tok_r))
    a1 = (unit * row(SG1) + row(SB1)).astype(bf16)
    g_wqkv[...] += tn(a1, d_qkv[...])
    d_a1 = nt(d_qkv[...], wqkv[...])
    add(SG1, colsum(d_a1 * unit))
    add(SB1, colsum(d_a1))
    d_tok = steps.join(d_mid_r) + norm_back(d_a1, unit, inverse, row(SG1))
    g_patch_b[0:1, :] += colsum(d_tok)
    for i in range(steps.small):
        mine = d_tok[steps.padded * i : steps.padded * i + valid, :]
        g_pos[...] += mine
        g_patch_w[...] += tn(ps[i], mine.astype(bf16))
    for i in range(steps.large):
        base = steps.split + steps.large_len * i
        mine = d_tok[base : base + steps.large_len, :]
        pos_large[...] += mine
        g_patch_w[...] += tn(plg[i], mine.astype(bf16))

    @pl.when(step == steps.count - 1)
    def _():
        g_pos[...] += lax.dot_general(
            resize[...], pos_large[...], (((1,), (0,)), ((), ())),
            preferred_element_type=f32, precision=lax.Precision.HIGHEST,
        )
        pack_late_kernel(
            *late, me_ref, g_wqkv, g_vec, pre, post, g_wo, g_patch_w, g_patch_b, g_pos, g_svec, g_head_w,
            keep, send, flat, tiles,
        )


def embed_back(me, ps, plg, tok, dq_s, d_mid, dq_l, wqkv, vec, others, late, padded_rows, after):
    ns, valid, _ = ps.shape
    nl, large_len, _ = plg.shape
    steps = Steps(ns, nl, tok[0].shape[1], large_len)
    resize = jnp.asarray(resize_table().T.copy())
    sums = [
        sds((D, 3 * D), f32),
        sds((16, D), f32),
        sds((PATCH_IN, D), f32),
        sds((8, D), f32),
        sds((valid, D), f32),
    ]
    index = lambda i: (i, 0, 0)
    half = len(late[0]) // 2
    outs = [sds((half, 2 * padded_rows, LANES), f32), sds((half, 2 * padded_rows, LANES), bf16)]
    return call(
        functools.partial(embed_back_kernel, steps, valid, late),
        (me, ps, plg, resize, *tok, dq_s, *d_mid, *dq_l, wqkv, vec, *others),
        after,
        grid=steps.grid,
        out_shape=outs,
        in_specs=[
            SM,
            pl.BlockSpec((steps.small, valid, PATCH_IN), index),
            pl.BlockSpec((steps.large, large_len, PATCH_IN), index),
            const_spec(resize),
            *steps.specs(D),
            steps.specs(3 * D)[0],
            *steps.specs(D),
        ]
        + [const_spec(a) for a in (*dq_l, wqkv, vec, *others)],
        out_specs=[const_spec(a) for a in outs],
        scratch_shapes=[pltpu.VMEM(a.shape, f32) for a in sums]
        + [
            pltpu.VMEM((large_len, D), f32),
            pltpu.VMEM((steps.rows, 3 * D), bf16),
            pltpu.VMEM((row_of(0, 6) + 1280, LANES), f32),
            pltpu.VMEM((8, D + 16, LANES), f32),
        ],
        cost_estimate=cost(20e9, 30e6),
        name="embed_back",
    )


def take_matrix(flat, row, src, rows, cols):
    step = cols // LANES
    for j in range(step):
        flat[pl.ds(row + j, rows, stride=step), :] = src[0:rows, LANES * j : LANES * (j + 1)]


def take_row(flat, row, src, at, cols):
    for j in range(cols // LANES):
        flat[row + j : row + j + 1, :] = src[at : at + 1, LANES * j : LANES * (j + 1)]


def slots_of(order):
    rels = [0]
    for bit in reversed(order):
        rels = rels + [r | (1 << bit) for r in rels]
    return rels


def emit_slots(me, flat, rows, rels, keep_ref, send_ref, offset=0):
    half = len(rels) // 2
    for k, r in enumerate(rels):
        value = flat[pl.ds(offset + rows * jnp.bitwise_xor(me, r), keep_ref.shape[1]), :]
        if k < half:
            keep_ref[k] = value.astype(keep_ref.dtype)
        else:
            send_ref[k - half] = value.astype(bf16)


def pack_class_kernel(rels, rows, me_ref, wq, wkv, wo, w1, w2, vec, c1, keep, send, flat):
    used = rows_used(2)
    flat[used:, :] = jnp.zeros((flat.shape[0] - used, LANES), f32)
    take_matrix(flat, row_of(2, 2), wq, D, D)
    take_matrix(flat, row_of(2, 4), wkv, D, 2 * D)
    take_matrix(flat, row_of(2, 6), wo, D, D)
    take_matrix(flat, row_of(2, 11), w1, D, FF)
    take_matrix(flat, row_of(2, 13), w2, FF, D)
    for at, number in (
        (CG1, 0), (CB1, 1), (CBQ, 3), (CBV, 5), (CBO, 7), (CLS1, 8), (CG2, 9), (CB2, 10), (CC2, 14), (CLS2, 15),
    ):
        take_row(flat, row_of(2, number), vec, at, D)
    take_row(flat, row_of(2, 12), c1, 0, FF)
    emit_slots(me_ref[0], flat, rows, rels, keep, send)


def take_head(flat, base, head_w, head_b, tiles, groups):
    for t in range(8):
        tiles[t, 0:D, :] = head_w[:, LANES * t : LANES * (t + 1)]
    lane = lax.broadcasted_iota(jnp.int32, (groups, LANES), 1)
    for rho in range(16):
        first, shift = (CLASSES * rho) // LANES, (CLASSES * rho) % LANES
        parts = [tiles[t, pl.ds(rho, groups, stride=16), :] for t in range(8)]
        if shift:
            parts = [pltpu.roll(p, shift, 1) for p in parts]
        for t in range(9 if shift + CLASSES > CLASS_PAD else 8):
            if shift:
                value = jnp.where(lane >= shift, parts[t] if t < 8 else 0.0, parts[t - 1] if t > 0 else 0.0)
            else:
                value = parts[t]
            here = pl.ds(base + first + t, groups, stride=125)
            flat[here, :] = flat[here, :] + value
    if head_b is not None:
        take_row(flat, base + row_of(0, 7) - row_of(0, 6), head_b, 0, CLASS_PAD)


HEAD_GROUPS = D // 16


def pack_feed_kernel(rels, rows, offset, quarter_rows, me_ref, wo, w1, w2, vec, c1, head_w, head_b, keep, send, flat, tiles):
    used, first = rows_used(1), row_of(1, 6)
    flat[0 : offset + first, :] = jnp.zeros((offset + first, LANES), f32)
    flat[offset + used :, :] = jnp.zeros((flat.shape[0] - used - offset, LANES), f32)
    take_head(flat, offset + row_of(0, 6) - quarter_rows, head_w, head_b, tiles, HEAD_GROUPS)
    boundary = quarter_rows - first
    flat[offset + first : offset + quarter_rows, :] = jnp.zeros((boundary, LANES), f32)
    take_matrix(flat, offset + first, wo, D, D)
    flat[offset + first : offset + quarter_rows, :] = jnp.zeros((boundary, LANES), f32)
    take_matrix(flat, offset + row_of(1, 11), w1, D, FF)
    take_matrix(flat, offset + row_of(1, 13), w2, FF, D)
    for at, number in ((SBO, 7), (SLS1, 8), (SG2, 9), (SB2, 10), (SC2, 14), (SLS2, 15)):
        take_row(flat, offset + row_of(1, number), vec, at, D)
    take_row(flat, offset + row_of(1, 12), c1, 0, FF)
    emit_slots(me_ref[0], flat, rows, rels, keep, send, offset)


def pack_late_kernel(
    rels, rows, quarter_rows, me_ref, wqkv, vec, pre, post, wo, patch_w, patch_b, pos, svec, head_w, keep, send, flat, tiles
):
    padded_rows = keep.shape[1] // 2
    for g in range(2):
        pack_late_group(g, quarter_rows, wqkv, vec, pre, post, wo, patch_w, patch_b, pos, svec, head_w, flat, tiles)
        here = pl.ds(g * padded_rows, padded_rows)
        emit_slots(me_ref[0], flat, rows, rels, keep.at[:, here], send.at[:, here])


def pack_late_group(g, quarter_rows, wqkv, vec, pre, post, wo, patch_w, patch_b, pos, svec, head_w, flat, tiles):
    if g == 0:
        first = row_of(0, 6)
        flat[first:, :] = jnp.zeros((flat.shape[0] - first, LANES), f32)
        take_matrix(flat, row_of(0, 0), patch_w, PATCH_IN, D)
        take_row(flat, row_of(0, 1), patch_b, 0, D)
        take_matrix(flat, row_of(0, 2), pos, GRID_SMALL**2, D)
        for at, number in ((1, 3), (2, 4), (3, 5)):
            take_row(flat, row_of(0, number), svec, at, D)
        take_head(flat, first, head_w, None, tiles, 8)
        return
    first = row_of(1, 6)
    take_matrix(flat, row_of(1, 2), wqkv, D, 3 * D)
    take_matrix(flat, first, wo, 24, D)
    bq = row_of(1, 3)
    for at, row in ((SG1, row_of(1, 0)), (SB1, row_of(1, 1)), (SBQ, bq), (SBV, bq + D // LANES)):
        take_row(flat, row, vec, at, D)
    table_col = lax.broadcasted_iota(jnp.int32, (D, LANES), 0) // WIDTH
    table_lane = lax.broadcasted_iota(jnp.int32, (D, LANES), 1)
    lane = lax.broadcasted_iota(jnp.int32, (HEADS, LANES), 1)
    row = lax.broadcasted_iota(jnp.int32, (HEADS, LANES), 0)
    exact = lambda a, b: lax.dot_general(
        a, b, (((1,), (0,)), ((), ())), preferred_element_type=f32, precision=lax.Precision.HIGHEST
    )
    sum_pre = exact(pre[...], jnp.where(table_lane % HEADS == table_col, 1.0, 0.0))
    sum_post = exact(post[...], jnp.where((table_lane - 64) // HEADS == table_col, 1.0, 0.0))
    line = colsum(jnp.where((lane < 64) & (lane // HEADS == row), sum_pre * SCALE, 0.0))
    line = line + colsum(jnp.where((lane >= 64) & (lane % HEADS == row), sum_post, 0.0))
    flat[row_of(1, 4) : row_of(1, 4) + 1, :] = line


def pack(kernel, name, me, arrays, rels, padded_rows, flat_rows, extra=()):
    half = len(rels) // 2
    return pl.pallas_call(
        kernel,
        out_shape=[sds((half, padded_rows, LANES), bf16)] * 2,
        in_specs=[SM] + [VM] * len(arrays),
        out_specs=[VM] * 2,
        scratch_shapes=[pltpu.VMEM((flat_rows, LANES), f32), *extra],
        compiler_params=params(),
        name=name,
    )(me, *arrays)


class Chain:
    def __init__(self, keep, send, order, z_bits, z_last=False):
        self.keep, self.send, self.order, self.z_bits, self.z_last = keep, send, list(order), z_bits, z_last
        self.total = None
        self.done = False

    def finish(self, total):
        self.total = self.send = total
        self.done = True

    def step(self, after=None):
        if self.order:
            (got,) = tied((exchange(self.send, self.order.pop(0), self.z_bits),), after)
            half = got.shape[0] // 2 if self.order else 1
            kept = self.keep[:half].astype(f32) + got[:half].astype(f32)
            if half == got.shape[0]:
                self.finish(kept[0])
                return
            passed = (self.keep[half:].astype(f32) + got[half:].astype(f32)).astype(bf16)
            self.keep, self.send = (kept, passed) if self.order else (kept[0], passed)
        elif not self.done:
            got = [exchange_z(self.send[k - 1], k) for k in range(1, self.send.shape[0] + 1)]
            total = self.keep
            for part in tied(tuple(got), after):
                total = total + part.astype(f32)
            self.finish(total)


def bounds_table():
    table = np.zeros((8, LANES), np.int32)
    table[0:3, :SEGMENTS] = STARTS // 64
    table[3:6, :SEGMENTS] = -(-ENDS // 64)
    return table


def pick(group, values):
    return jnp.where(group == 0, values[0], jnp.where(group == 1, values[1], values[2]))


def segment_sums(square, group, first_row, bounds):
    rows = square.shape[0]
    lane = lax.broadcasted_iota(jnp.int32, (rows, LANES), 1)
    left = jnp.sum(jnp.where(lane < 64, square, 0.0), -1, keepdims=True)
    right = jnp.sum(jnp.where(lane < 64, 0.0, square), -1, keepdims=True)
    place = 2 * (first_row + lax.broadcasted_iota(jnp.int32, (rows, LANES), 0))
    low, high = bounds[group : group + 1, :], bounds[3 + group : 4 + group, :]
    one = jnp.where((place >= low) & (place < high), left, 0.0)
    two = jnp.where((place + 1 >= low) & (place + 1 < high), right, 0.0)
    return colsum(one + two)


def adam_kernel(rows, me_ref, step_ref, bounds, master, first, second, g0, g1, g2, grad_o, first_o, second_o, update_o, sums_o):
    shard = rows * LANES
    for g, ref in enumerate((g0, g1, g2)):
        grad_o[g : g + 1, :] = ref[0:rows, :].reshape(1, shard)
    grad = grad_o[...]
    weight = master[...]
    new_first = beta_one * first[...] + (1.0 - beta_one) * grad
    new_second = beta_two * second[...] + (1.0 - beta_two) * grad * grad
    first_o[...] = new_first
    second_o[...] = new_second
    power = jnp.full((1, LANES), step_ref[0], jnp.int32).astype(f32)
    scale_one = (1.0 / (1.0 - jnp.power(f32(beta_one), power)))[:, 0:1]
    scale_two = (1.0 / (1.0 - jnp.power(f32(beta_two), power)))[:, 0:1]
    update = new_first * scale_one / (jnp.sqrt(new_second * scale_two) + adam_eps) + decay_rate * weight
    update_o[...] = update
    sums_o[...] = jnp.zeros_like(sums_o)
    first_row = me_ref[0] * rows
    for g in range(3):
        part = update_o[g : g + 1, :].reshape(rows, LANES)
        sums_o[3 + g : 4 + g, :] = segment_sums(part * part, g, first_row, bounds)


def adam(me, step, master, first, second, grads, rows):
    shape = master.shape
    return pl.pallas_call(
        functools.partial(adam_kernel, rows),
        out_shape=[sds(shape, f32)] * 4 + [sds((8, LANES), f32)],
        in_specs=[SM, SM] + [VM] * 7,
        out_specs=[VM] * 5,
        compiler_params=params(),
        name="adam",
    )(me, step, jnp.asarray(bounds_table()), master, first, second, *grads)


def apply_kernel(me_ref, sums, bounds, master, update, new_o, weight_o, norm_o, trust_o):
    shard = master.shape[1]
    roots = jnp.sqrt(sums[...])
    weight_norms, update_norms = roots[0:3, :], roots[3:6, :]
    lane = lax.broadcasted_iota(jnp.int32, (3, LANES), 1)
    group3 = lax.broadcasted_iota(jnp.int32, (3, LANES), 0)
    used = pick(group3, [int(REAL[g].sum()) for g in range(3)])
    trust = jnp.where(lane < used, weight_norms / (update_norms + norm_eps), 1.0)
    weight_o[...] = weight_norms[:, 0:SEGMENTS]
    norm_o[...] = update_norms[:, 0:SEGMENTS]
    trust_o[...] = trust[:, 0:SEGMENTS]
    rows = shard // LANES
    place = 2 * (me_ref[0] * rows + lax.broadcasted_iota(jnp.int32, (rows, LANES), 0))
    lane = lax.broadcasted_iota(jnp.int32, (rows, LANES), 1)
    for g in range(3):
        low, high, mine = bounds[g : g + 1, :], bounds[3 + g : 4 + g, :], trust[g : g + 1, :]
        left = jnp.sum(jnp.where((place >= low) & (place < high), mine, 0.0), -1, keepdims=True)
        right = jnp.sum(jnp.where((place + 1 >= low) & (place + 1 < high), mine, 0.0), -1, keepdims=True)
        ratio = jnp.where(lane < 64, left, right).reshape(1, shard)
        new_o[g : g + 1, :] = master[g : g + 1, :] - learn_rate * ratio * update[g : g + 1, :]


def apply_update(me, sums, master, update):
    return pl.pallas_call(
        apply_kernel,
        out_shape=[sds(master.shape, f32)] + [sds((3, SEGMENTS), f32)] * 3,
        in_specs=[SM] + [VM] * 4,
        out_specs=[VM] * 4,
        compiler_params=params(),
        name="apply_update",
    )(me, sums, jnp.asarray(bounds_table()), master, update)


def round_kernel(rows, counts, master, stem, selfb, classb, lines):
    tail = lines.shape[0] - rows
    for g, ref in enumerate((stem, selfb, classb)):
        lines[0:rows, :] = master[g : g + 1, :].reshape(rows, LANES)
        count = counts[0, 0] + counts[0, 1] if g == 2 else 0
        lines[rows:, :] = jnp.full((tail, LANES), count, jnp.int32).astype(f32)
        ref[0] = lines[...].astype(bf16)


def round_shards(counts, master, rows, padded_rows):
    return pl.pallas_call(
        functools.partial(round_kernel, rows),
        out_shape=[sds((1, padded_rows, LANES), bf16)] * 3,
        in_specs=[SM, VM],
        out_specs=[VM] * 3,
        scratch_shapes=[pltpu.VMEM((padded_rows, LANES), f32)],
        compiler_params=params(),
        name="round_shards",
    )(counts, master)


def weight_kernel(rows, me_ref, bounds, master, sums_o):
    sums_o[...] = jnp.zeros_like(sums_o)
    for g in range(3):
        part = master[g : g + 1, :].reshape(rows, LANES)
        sums_o[g : g + 1, :] = segment_sums(part * part, g, me_ref[0] * rows, bounds)


def weight_sums(me, master, rows):
    return pl.pallas_call(
        functools.partial(weight_kernel, rows),
        out_shape=sds((8, LANES), f32),
        in_specs=[SM, VM, VM],
        out_specs=VM,
        compiler_params=params(),
        name="weight_sums",
    )(me, jnp.asarray(bounds_table()), master)


def on_device(
    master,
    first_moment,
    second_moment,
    patches_small,
    patches_large,
    labels_small,
    labels_large,
    counts,
    step,
):
    rows = master.shape[1] // LANES
    padded_rows = -(-(rows + 1) // 16) * 16
    n_dp, n_z = lax.axis_size("dp"), lax.axis_size("fsdp")
    z_bits, bits = log2(n_z), log2(n_dp) + log2(n_z)
    devices = n_dp * n_z
    half, quarter = devices // 2, devices // 4
    assert row_of(0, 7) + CLASS_PAD // LANES <= half * rows
    assert row_of(1, 6) <= quarter * rows <= row_of(1, 6) + 64
    ns, valid, _ = patches_small.shape
    nl = patches_large.shape[0]
    padded = -(-valid // 16) * 16
    small_per = 2 if ns % 2 == 0 else 1
    me = lax.axis_index(AXES).astype(jnp.int32).reshape(1)
    me_half = jnp.bitwise_and(me, half - 1)
    me_quarter = jnp.bitwise_and(me, quarter - 1)
    dp = lax.axis_index("dp")
    n_quarter = n_dp // 4
    in_half, quarter_id = dp < n_dp // 2, dp // n_quarter

    core, second, top = z_bits, bits - 2, bits - 1
    inner = list(range(core + 1, second))
    arrays = lambda state: ([a for a, _ in state], [r for _, r in state])

    old_sums = weight_sums(me, master, rows)
    stem_shard, self_shard, class_shard = round_shards(counts, master, rows, padded_rows)
    up = n_dp // 2
    got = lax.ppermute(stem_shard, "dp", [(i, i + up) for i in range(up)])
    (got,) = tied((got,), old_sums)
    others = [lax.ppermute(self_shard, "dp", [(i, i ^ (a * n_quarter)) for i in range(n_dp)]) for a in (1, 2, 3)]
    stem_state = gather_z(jnp.where(in_half, stem_shard, got), [0])

    def of_quarter(b):
        value = self_shard
        for a in (1, 2, 3):
            value = jnp.where(quarter_id == (a ^ b), others[a - 1], value)
        return value

    first_state = gather_z(of_quarter(0), [0])
    rest = jnp.concatenate([of_quarter(b) for b in (1, 2, 3)], 0)
    for bit in inner:
        first_state = gather_bit(first_state, bit, z_bits)
    for bit in [*inner, second]:
        stem_state = gather_bit(stem_state, bit, z_bits)
    rest, class_shard, _ = lax.optimization_barrier((rest, class_shard, first_state[0][0]))
    first_state = gather_bit(first_state, core, z_bits)
    stem_state = gather_bit(stem_state, core, z_bits)
    class_all = lax.all_gather(class_shard[0], AXES, axis=0, tiled=False)

    patch_w, svec, pos_small, pos_large, head_w, head_b = stem = unpack_stem(
        me_half, *arrays(stem_state), rows, half, padded
    )
    wqkv, vec, pre_col, post_col, pre_row, post_row = unpack_low(me_quarter, *arrays(first_state), rows, quarter)
    tok, (qkv_s, qkv_l) = embed(
        patches_small, patches_large, patch_w, pos_small, pos_large, wqkv, vec, padded, []
    )
    att_s, lse_s = attend(qkv_s, pre_col, post_col, valid, small_per, 20e9, [])
    rest_state = gather_z(rest, [quarter, 2 * quarter, 3 * quarter], att_s)
    rest_all = rest_state[0][0]
    for bit in [*inner, core]:
        rest_state = gather_bit(rest_state, bit, z_bits)
    att_l, lse_l = attend(qkv_l, pre_col, post_col, qkv_l.shape[1], 1, 30e9, [rest_all, att_s])
    wo, w1, w2, vec_feed, c1 = unpack_feed(me_quarter, *arrays(first_state + rest_state), rows, devices)
    att = (att_s, att_l)
    branch, mid, act, slope, lower, out = feed(tok, att, (wo, w1, w2, vec_feed, c1), [])
    z_order = list(range(z_bits - 1, -1, -1))
    near_far = list(range(z_bits))
    class_order = [core, top, second] + inner + near_far
    feed_order = [core] + near_far + inner + [top, second]
    class_rels, feed_rels = slots_of(class_order), slots_of(feed_order)
    tail = padded_rows - rows + 8

    d_out_s, d_out_l, g_svec, g_head_w, g_head_b, loss, keep, send = class_step(
        me, jnp.zeros_like(me), [class_all], [list(range(devices))], class_rels, out, stem, counts, labels_small,
        labels_large, valid, rows, padded_rows,
    )
    class_chain = Chain(keep, send, class_order, z_bits)
    d_mid, (d_att_s, d_att_l), (g_wo, g_w1, g_w2, g_vec_feed, g_c1) = feed_back(
        ((d_out_s, d_out_l), mid, act, slope, lower, branch, att), (wo, w1, w2, vec_feed), [class_chain.send]
    )
    class_chain.step(d_att_s)
    quarter_rows = quarter * rows
    offset = -(-max(0, quarter_rows - row_of(0, 6)) // 8) * 8
    tiles = [pltpu.VMEM((8, D + 16, LANES), f32)]
    feed_chain = Chain(
        *pack(
            functools.partial(pack_feed_kernel, feed_rels, rows, offset, quarter_rows), "pack_feed", me,
            (g_wo, g_w1, g_w2, g_vec_feed, g_c1, g_head_w, g_head_b), feed_rels, padded_rows,
            offset + devices * rows + tail, tiles,
        ),
        feed_order, z_bits,
    )
    chains = (class_chain, feed_chain)
    mixes = (pre_col, post_col, pre_row, post_row)
    dq_s, pre_sum, post_sum = attend_back(
        qkv_s, d_att_s, lse_s, mixes, valid, 0, ns, small_per, 25e9, [chain.send for chain in chains]
    )
    part, dq_l = dq_s, []
    for i in range(nl):
        for chain in chains:
            chain.step(part)
        wait = [part] + [chain.send for chain in chains]
        part, pre_l, post_l = attend_back(qkv_l, d_att_l, lse_l, mixes, qkv_l.shape[1], i, 1, 1, 25e9, wait)
        dq_l.append(part)
        pre_sum, post_sum = pre_sum + pre_l, post_sum + post_l
    for chain in chains:
        chain.step(part)
    late_rels = slots_of([core] + inner + z_order)
    keep, send = embed_back(
        me_quarter, patches_small, patches_large, tok, dq_s, d_mid, dq_l, wqkv, vec,
        (pre_sum, post_sum, g_wo, g_svec, g_head_w), (late_rels, rows, quarter_rows), padded_rows,
        [chain.send for chain in chains],
    )
    while not class_chain.done:
        class_chain.step(send)
    while len(feed_chain.order) > 1:
        feed_chain.step(send)
    head_part = feed_chain.send[0].astype(f32) + lax.ppermute(
        feed_chain.keep[0].astype(bf16), "dp", [(i, i + n_quarter) for i in range(n_quarter)]
    ).astype(f32)
    feed_chain.step()
    late_chain = Chain(keep, send, [core] + inner, z_bits, True)
    while not late_chain.done:
        late_chain.step()
    part = late_chain.total
    (send,) = tied(tied((part.astype(bf16),), head_part), feed_chain.total)
    for a in (1, 2, 3):
        got = lax.ppermute(send, "dp", [(i + a * n_quarter, i) for i in range(n_quarter)])
        part = part + got.astype(f32)
    first = quarter_id == 0
    grad_stem = jnp.where(first, part[:padded_rows], jnp.where(quarter_id == 1, head_part, 0.0))
    grad_self = jnp.where(first, part[padded_rows:], feed_chain.total)

    gradients, new_first, new_second, update, sums = adam(
        me, step, master, first_moment, second_moment, (grad_stem, grad_self, class_chain.total), rows
    )
    line = lax.broadcasted_iota(jnp.int32, (8, 1), 0)
    sums = sums + old_sums + jnp.where(line == 6, loss, 0.0)
    for bit in range(bits):
        sums = sums + exchange(sums, bit, z_bits)
    new_master, weight_norms, update_norms, trust_ratios = apply_update(me, sums, master, update)
    return sums[6, 0], gradients, new_first, new_second, new_master, weight_norms, update_norms, trust_ratios


def solution(mesh):
    return jax.shard_map(
        on_device,
        mesh=mesh,
        in_specs=(
            P(None, AXES),
            P(None, AXES),
            P(None, AXES),
            P(AXES, None, None),
            P(AXES, None, None),
            P(AXES),
            P(AXES),
            P(AXES, None),
            P(),
        ),
        out_specs=(
            P(),
            P(None, AXES),
            P(None, AXES),
            P(None, AXES),
            P(None, AXES),
            P(),
            P(),
            P(),
        ),
        check_vma=False,
    )
```
